32 devices in a mesh: gx: 16 (over z, y, core), gy: 2 (over x).
Axes of the slice: x: 2, y: 2, z: 4, core: 2. Of those that a mesh axis runs over, the one named last changes fastest.
Arguments:
- velocity: float32 [3, 262144], P(None, ('gx', 'gy')), may hold values from -6 to 6
- inv_mass: float32 [262144], P(('gx', 'gy')), may hold values from 0.5 to 2
- drag: float32 [262144], P(('gx', 'gy')), may hold values from 0.2 to 5
- grain_cell: int32 [262144], P(('gx', 'gy')), may hold values from 0 to 2047
- boundary_list: int32 [16384], P(('gx', 'gy')), may hold values from 0 to 8191
- contact_pair: int32 [2, 524288], P(None, ('gx', 'gy')), may hold values from 0 to 10239, as said below
- frames: float32 [9, 524288], P(None, ('gx', 'gy')), may hold values from -0.45 to 1.4
- blocks: float32 [9, 524288], P(None, ('gx', 'gy')), may hold values from -0.15 to 1
- impulse_start: float32 [3, 524288], P(None, ('gx', 'gy')), may hold values from -4 to 4
- gap: float32 [3, 524288], P(None, ('gx', 'gy')), may hold values from -4 to 4
- contact_mask: int32 [524288], P(('gx', 'gy')), may hold values 0 or 1
- pressure: float32 [8, 256, 32], P(None, 'gx', 'gy'), may hold values from -6 to 6
Outputs:
- final_velocity: float32 [3, 262144], P(None, ('gx', 'gy'))
- final_impulse: float32 [3, 524288], P(None, ('gx', 'gy'))
The draws below stay inside these ranges and needn't reach their ends.
Inputs may be any that keep to these rules, and one draw needn't show every extreme that they name: `contact_pair`: slots below 8192 are the block's own grains, slots from 8192 on are the four ghost groups of 512. Contacts are sorted in space: for the contacts of tile t of a block (contacts 128 t to 128 t + 127), a slot below 8192 lies in (64 t + r) mod 8192 and a slot from 8192 on in 8192 + ((16 t + r) mod 4 * 512), with r from 0 to 255 and from 0 to 63 respectively.
All inputs are finite; a program needn't handle non-finite values. No bound on the sum of `contact_mask` on one device may be relied on, other than what follows from the above.
Results may differ from the reference program's by a relative error of at most 0.0003.
Values sent between devices are 32-bit elements; how exact they have to be, the bound alone decides.
A program may use at most 64 MiB of HBM per device.

```python
import math
from functools import partial
import jax
import jax.numpy as jnp

G = 8192
B = 512
TILES = 128
K = 16384
PZ = 8
PX = 16
PY = 16
CELLS = 2048
SWEEPS = 2
GRAINS = 262144
BOUND = 16384
CONTACTS = 524288
N_GX = 16
N_GY = 2


def draw_contact_pair(key, part):
    key = jax.random.fold_in(key, 37)
    key_own, key_ghost, key_pick = jax.random.split(key, 3)
    block_count = CONTACTS // K
    shape = (2, block_count, TILES, 128)
    tile_index = jnp.arange(TILES, dtype=jnp.int32)[None, None, :, None]
    own_slot = (64 * tile_index + jax.random.randint(key_own, shape, 0, 256, dtype=jnp.int32)) % G
    ghost_slot = G + (16 * tile_index + jax.random.randint(key_ghost, shape, 0, 64, dtype=jnp.int32)) % (4 * B)
    pick_own = jax.random.randint(key_pick, shape, 0, 5, dtype=jnp.int32) < 4
    slots = jnp.where(pick_own, own_slot, ghost_slot)
    slots = slots.at[0, :, 0, 0].set(0)
    slots = slots.at[1, :, TILES - 1, 0].set(G + 4 * B - 1)
    return slots.reshape(2, CONTACTS).astype(jnp.int32)


def draw_frames(key, part):
    key_one, key_two = jax.random.split(jax.random.fold_in(key, 11))
    shape = (9, CONTACTS)
    diag_mask = (jnp.arange(9) % 4 == 0)[:, None]
    diagonal_part = jax.random.uniform(key_one, shape, jnp.float32, 0.7, 1.3)
    offdiag_part = jax.random.uniform(key_two, shape, jnp.float32, -0.35, 0.35)
    return jnp.where(diag_mask, diagonal_part, offdiag_part).astype(jnp.float32)


def draw_blocks(key, part):
    key_one, key_two = jax.random.split(jax.random.fold_in(key, 23))
    shape = (9, CONTACTS)
    diag_mask = (jnp.arange(9) % 4 == 0)[:, None]
    diagonal_part = jnp.exp(jax.random.uniform(key_one, shape, jnp.float32, jnp.log(0.3), jnp.log(0.9)))
    offdiag_part = jax.random.uniform(key_two, shape, jnp.float32, -0.12, 0.12)
    return jnp.where(diag_mask, diagonal_part, offdiag_part).astype(jnp.float32)


def touch_ends(drawn, own_key, smallest, high):
    shape = drawn.shape
    index_at = [jax.random.randint(jax.random.fold_in(own_key, axis), (), 0, shape[axis]) for axis in range(len(shape))]
    drawn = drawn.at[tuple(index_at)].set(smallest)
    longest = shape.index(max(shape))
    index_at[longest] = (index_at[longest] + 1) % shape[longest]
    return drawn.at[tuple(index_at)].set(high)


def levels(key, extent, shards, least, top_value):
    level, own = 1.0, jax.random.fold_in(key, 6)
    for position, blocks in shards:
        draws = jnp.exp(jax.random.uniform(jax.random.fold_in(own, position), (blocks,), jnp.float32, least / len(shards), top_value / len(shards)))
        level = level * jnp.repeat(draws, extent[position] // blocks).reshape([-1 if axis == position else 1 for axis in range(len(extent))])
    return level


def normal_values(stream_key, shape, width, most, shards=(), kind=jnp.bfloat16):
    drawn = width * jax.random.normal(stream_key, shape, jnp.float32)
    if shards:
        drawn = drawn * levels(stream_key, shape, shards, -0.22, 0.18)
    return jnp.clip(drawn, -most, most).astype(kind)


def setup_inputs(seed: int = 0) -> dict:
    key_list = jax.random.split(jax.random.key(seed), 13)
    return {
        "velocity": normal_values(key_list[0], (3, GRAINS), 1.0, 6.0, ((1, 32),), jnp.float32),
        "inv_mass": jnp.clip(jnp.exp(math.log(2.0) - 1.3862944 * jax.random.uniform(key_list[1], (GRAINS,), jnp.float32) ** levels(key_list[1], (GRAINS,), ((0, 32),), -0.2, 0.2)), 0.5, 2.0),
        "drag": jnp.clip(jnp.exp(math.log(5.0) - 3.218876 * jax.random.uniform(key_list[2], (GRAINS,), jnp.float32) ** levels(key_list[2], (GRAINS,), ((0, 32),), -0.2, 0.2)), 0.2, 5.0),
        "grain_cell": touch_ends(jax.random.randint(key_list[3], (GRAINS,), 0, CELLS), jax.random.fold_in(key_list[3], 1), 0, CELLS - 1).astype(jnp.int32),
        "boundary_list": touch_ends(jax.random.randint(key_list[4], (BOUND,), 0, G), jax.random.fold_in(key_list[4], 1), 0, G - 1).astype(jnp.int32),
        "contact_pair": draw_contact_pair(jax.random.fold_in(key_list[12], 71), 0),
        "frames": draw_frames(jax.random.fold_in(key_list[12], 71), 0),
        "blocks": draw_blocks(jax.random.fold_in(key_list[12], 71), 0),
        "impulse_start": normal_values(key_list[8], (3, CONTACTS), 0.5, 4.0, ((1, 32),), jnp.float32),
        "gap": normal_values(key_list[9], (3, CONTACTS), 0.5, 4.0, ((1, 32),), jnp.float32),
        "contact_mask": touch_ends((jax.random.randint(key_list[10], (CONTACTS,), 0, 4) < 3).astype(jnp.int32), jax.random.fold_in(key_list[10], 1), 0, 1),
        "pressure": normal_values(key_list[11], (PZ, PX * N_GX, PY * N_GY), 1.0, 6.0, ((1, 16), (2, 2)), jnp.float32),
    }


TIME_STEP = 0.5
FRICTION = 0.5
FLOOR_VALUE = 0.1

def contact_update(relative, frames, blocks, impulse, offset, active):
    local_rel = [sum((frames[3 * row_pos + col_pos] * relative[col_pos] for col_pos in range(3))) for row_pos in range(3)]
    target = [local_rel[row_pos] + offset[row_pos] for row_pos in range(3)]
    trial = [impulse[row_pos] - sum((blocks[3 * row_pos + col_pos] * target[col_pos] for col_pos in range(3))) for row_pos in range(3)]
    normal = jnp.maximum(trial[0], 0.0)
    tangent = jnp.sqrt(trial[1] * trial[1] + trial[2] * trial[2])
    factor = jnp.minimum(1.0, FRICTION * normal / jnp.maximum(tangent, FLOOR_VALUE))
    updated = jnp.stack([normal, factor * trial[1], factor * trial[2]]) * active
    push = jnp.stack([sum((frames[3 * row_pos + col_pos] * updated[row_pos] for row_pos in range(3))) for col_pos in range(3)])
    return (updated, push)

def spread_one(push, first_end, second_end, slot_count):
    index_all = jnp.concatenate([second_end, first_end])
    return jnp.stack([jax.ops.segment_sum(jnp.concatenate([push[row_pos], -push[row_pos]]), index_all, num_segments=slot_count) for row_pos in range(3)])

def collect_one(values, targets, slot_count):
    return jnp.stack([jax.ops.segment_sum(values[row_pos], targets, num_segments=slot_count) for row_pos in range(3)])

def reference(velocity, inv_mass, drag, grain_cell, boundary_list, contact_pair, frames, blocks, impulse_start, gap, contact_mask, pressure):
    blocks_all = N_GX * N_GY
    slope_shear = (jnp.roll(pressure, -1, 1) - jnp.roll(pressure, 1, 1)) * 0.5
    slope_lateral = (jnp.roll(pressure, -1, 2) - jnp.roll(pressure, 1, 2)) * 0.5
    padded = jnp.pad(pressure, ((1, 1), (0, 0), (0, 0)))
    slope_vertical = (padded[2:] - padded[:-2]) * 0.5
    slope = jnp.stack([slope_shear, slope_lateral, slope_vertical])
    slope = slope.reshape(3, PZ, N_GX, PX, N_GY, PY).transpose(0, 2, 4, 1, 3, 5).reshape(3, blocks_all, PZ * PX * PY)
    moving = velocity.reshape(3, blocks_all, G)
    inverse = inv_mass.reshape(blocks_all, G)
    drag_all = drag.reshape(blocks_all, G)
    cells = grain_cell.reshape(blocks_all, G)
    slope_at = jnp.take_along_axis(slope, cells[None], axis=2)
    free_velocity = (moving - TIME_STEP * (drag_all + inverse)[None] * slope_at) / (1.0 + TIME_STEP * drag_all)[None]
    bound_rows = boundary_list.reshape(blocks_all, B)
    first_end = contact_pair[0].reshape(blocks_all, K)
    second_end = contact_pair[1].reshape(blocks_all, K)
    frame_all = frames.reshape(9, blocks_all, K)
    block_all = blocks.reshape(9, blocks_all, K)
    impulse = impulse_start.reshape(3, blocks_all, K)
    offset = gap.reshape(3, blocks_all, K)
    active = contact_mask.reshape(blocks_all, K).astype(jnp.float32)
    spread_all = jax.vmap(partial(spread_one, slot_count=G + 4 * B), in_axes=(1, 0, 0), out_axes=1)
    collect_all = jax.vmap(partial(collect_one, slot_count=G), in_axes=(1, 0), out_axes=1)
    current = free_velocity
    for sweep_step in range(SWEEPS):
        shared = jnp.take_along_axis(current, bound_rows[None], axis=2).reshape(3, N_GX, N_GY, B)
        ghosts = jnp.concatenate([jnp.roll(shared, 1, 1), jnp.roll(shared, -1, 1), jnp.roll(shared, 1, 2), jnp.roll(shared, -1, 2)], axis=3)
        extended = jnp.concatenate([current, ghosts.reshape(3, blocks_all, 4 * B)], axis=2)
        moving_a = jnp.take_along_axis(extended, first_end[None], axis=2)
        moving_b = jnp.take_along_axis(extended, second_end[None], axis=2)
        impulse, push = contact_update(moving_b - moving_a, frame_all, block_all, impulse, offset, active)
        slot_sum = spread_all(push, first_end, second_end)
        ghost_sum = slot_sum[:, :, G:].reshape(3, N_GX, N_GY, 4, B)
        received = jnp.roll(ghost_sum[:, :, :, 1], 1, 1) + jnp.roll(ghost_sum[:, :, :, 0], -1, 1)
        received = received + jnp.roll(ghost_sum[:, :, :, 3], 1, 2) + jnp.roll(ghost_sum[:, :, :, 2], -1, 2)
        total = slot_sum[:, :, :G] + collect_all(received.reshape(3, blocks_all, B), bound_rows)
        current = free_velocity + inverse[None] * total
    return (current.reshape(3, blocks_all * G), impulse.reshape(3, blocks_all * K))
```

```python
import jax
import jax.numpy as jnp
from jax import lax
from jax.experimental import pallas as pl
from jax.experimental.pallas import tpu as pltpu
from jax.sharding import PartitionSpec as P

SWEEPS = 2
TIME_STEP = 0.5
FRICTION = 0.5
FLOOR_VALUE = 0.1
LANES = 128
HALF = LANES // 2
ROWS = 48
PITCH = 49
STAGE = 49
OWN_PITCH = 25
GHOST_PITCH = 17
F32 = jnp.float32
BF16 = jnp.bfloat16


def take_lanes(values, lanes):
    return jnp.take_along_axis(values, lanes, axis=1, mode="promise_in_bounds")


def spread_row(ref, row):
    return jnp.broadcast_to(ref[pl.ds(row, 1), :], (8, LANES))


def step_kernel(
    sizes,
    vel_hbm, mass_hbm, drag_hbm, cell_hbm, bound_hbm, pair_hbm, frame_hbm, block_hbm,
    start_hbm, gap_hbm, mask_hbm, pres_hbm,
    out_vel, out_imp,
    vel_ref, mass_ref, drag_ref, cell_ref, bound_ref, pair_ref, frame_ref, block_ref,
    start_ref, gap_ref, mask_ref, pres_raw, pres_wide, pres_ref,
    pres_in, ghost_in, sum_in, ghost_out, sum_out,
    slope_s, vel_s, free_s, stage, ends, codes, lanes_s, spots, table, ext, ghost_s,
    left, sums, ghost_sums, bound_hot, bound_row,
    send_sem, recv_sem, load_sem,
):
    nx, ny = sizes
    tiles = mask_ref.shape[0]
    own_rows = mass_ref.shape[0]
    side_rows = bound_ref.shape[0]
    ghost_rows = 4 * side_rows
    cell_rows = pres_ref.shape[0]
    ext_rows = 2 * own_rows + 8
    gpad = 2 * ghost_rows
    own_slots = own_rows * LANES
    ghost_slots = ghost_rows * LANES
    own_part = own_rows + 2
    ghost_part = ghost_rows + 1
    row_iota = lax.broadcasted_iota(jnp.int32, (8, LANES), 0)

    mx, my = lax.axis_index("gx"), lax.axis_index("gy")
    sides = (
        (lax.rem(mx + nx - 1, nx), my),
        (lax.rem(mx + 1, nx), my),
        (mx, lax.rem(my + ny - 1, ny)),
        (mx, lax.rem(my + 1, ny)),
    )

    loads = [
        pltpu.make_async_copy(source, target, load_sem.at[k])
        for k, (source, target) in enumerate(
            (
                (pair_hbm, pair_ref), (frame_hbm, frame_ref), (block_hbm, block_ref),
                (start_hbm, start_ref), (gap_hbm, gap_ref), (vel_hbm, vel_ref),
                (bound_hbm, bound_ref), (cell_hbm, cell_ref), (drag_hbm, drag_ref),
                (mass_hbm, mass_ref), (mask_hbm, mask_ref),
            )
        )
    ]
    pres_load = pltpu.make_async_copy(pres_hbm, pres_raw, load_sem.at[11])
    pres_load.start()
    for load in loads:
        load.start()

    barrier = pltpu.get_barrier_semaphore()
    for side in sides:
        pl.semaphore_signal(barrier, inc=1, device_id=side, device_id_type=pl.DeviceIdType.MESH)

    lane = lax.broadcasted_iota(jnp.int32, (cell_rows, LANES), 1)
    pres_load.wait()
    width = pres_raw.shape[2]
    pres_wide[:, 0:width] = pres_raw[...].reshape(-1, width)
    per_row = LANES // width
    p = pres_wide[pl.ds(0, cell_rows, stride=per_row), :]
    for k in range(1, per_row):
        piece = pltpu.roll(pres_wide[pl.ds(k, cell_rows, stride=per_row), :], k * width, 1)
        p = jnp.where(lane < k * width, p, piece)
    pres_ref[...] = p
    pl.semaphore_wait(barrier, 4)

    def exchange(step, source, target):
        copies = []
        for g in range(4):
            copies.append(
                pltpu.make_async_remote_copy(
                    src_ref=source(g),
                    dst_ref=target(g ^ 1),
                    send_sem=send_sem.at[step, g],
                    recv_sem=recv_sem.at[step, g ^ 1],
                    device_id=sides[g],
                    device_id_type=pl.DeviceIdType.MESH,
                )
            )
        for copy in copies:
            copy.start()
        return copies

    sent = []

    def finish(copies):
        for copy in copies:
            copy.wait_recv()
        sent.extend(copies)

    flying = exchange(0, lambda g: pres_ref, lambda g: pres_in.at[g])

    for load in loads:
        load.wait()

    def stage_tile(t, carry):
        cols = pl.ds(pl.multiple_of(t * LANES, LANES), LANES)
        base = t * STAGE
        stage[pl.ds(base, 9), :] = frame_ref[:, cols]
        stage[pl.ds(base + 16, 9), :] = block_ref[:, cols]
        stage[pl.ds(base + 32, 3), :] = start_ref[:, cols]
        stage[pl.ds(base + 40, 3), :] = gap_ref[:, cols]
        ends[pl.ds(t * 3, 2), :] = pair_ref[:, cols]
        return carry

    lax.fori_loop(0, tiles, stage_tile, 0, unroll=4)

    def stage_grain(t, carry):
        cols = pl.ds(pl.multiple_of(t * LANES, LANES), LANES)
        vel_s[pl.ds(t * 3, 3), :] = vel_ref[:, cols]
        return carry

    lax.fori_loop(0, own_rows, stage_grain, 0, unroll=4)

    def place(u, carry):
        tile = u * 8 + row_iota
        for e in range(2):
            slot = ends[pl.ds(u * 24 + 1 - e, 8, stride=3), :]
            own = slot < own_slots
            near = (slot - HALF * tile) & (own_slots - 1)
            far = (slot - own_slots - HALF * (tile >> 2)) & (ghost_slots - 1)
            rel = jnp.where(own, near, far)
            at = pl.ds(pl.multiple_of(e * tiles + u * 8, 8), 8)
            codes[at, :] = jnp.where(own, 0, 4) + (rel >> 6)
            lanes_s[at, :] = rel & (LANES - 1)
            spots[at, :] = (rel & (HALF - 1)).astype(F32)
        return carry

    lax.fori_loop(0, tiles // 8, place, 0, unroll=2)

    bound_all = bound_ref[...]
    bound_lane = bound_all & (LANES - 1)
    bound_at = bound_all >> 7
    hot_iota = lax.broadcasted_iota(jnp.int32, (LANES, LANES), 0)
    row_hot = lax.broadcasted_iota(jnp.int32, (own_rows, LANES), 0)
    for q in range(side_rows):
        cols = slice(q * LANES, (q + 1) * LANES)
        bound_hot[:, cols] = jnp.where(hot_iota == bound_lane[q : q + 1], 1.0, 0.0).astype(BF16)
        bound_row[:, cols] = jnp.where(row_hot == bound_at[q : q + 1], 1.0, 0.0).astype(BF16)
    two_lane = jnp.concatenate([bound_lane, bound_lane], axis=0)
    two_at = jnp.concatenate([bound_at, bound_at], axis=0)
    half = own_rows // 2
    upper = row_iota < side_rows

    def pick_bound(turn):
        def body(k, acc):
            acc = list(acc)
            for i in range(4):
                r = k * 4 + i
                hit = two_at == jnp.where(upper, r, r + half)
                for c in range(3):
                    low = spread_row(ext, c * ext_rows + 2 * r)
                    high = spread_row(ext, c * ext_rows + 2 * (r + half))
                    got = take_lanes(jnp.where(upper, low, high), two_lane)
                    acc[c] = jnp.where(hit, got, acc[c])
            return tuple(acc)

        zero = jnp.zeros((8, LANES), F32)
        acc = lax.fori_loop(0, half // 4, body, (zero, zero, zero), unroll=4)
        low_at = two_at < half
        for c in range(3):
            got = acc[c]
            ghost_out[turn, c * side_rows : (c + 1) * side_rows, :] = jnp.where(
                low_at[:side_rows], got[:side_rows], got[side_rows:]
            )

    def spread_halves(ref, first, value):
        rows = value.shape[0]
        turned = pltpu.roll(value, HALF, 1)
        after = jnp.concatenate([turned[1:], turned[:1]], axis=0)
        first_half = lax.broadcasted_iota(jnp.int32, value.shape, 1) < HALF
        ref[pl.ds(first, rows, stride=2), :] = value
        ref[pl.ds(first + 1, rows, stride=2), :] = jnp.where(first_half, turned, after)

    def spread_current(c, value):
        spread_halves(ext, c * ext_rows, value)
        ext[pl.ds(c * ext_rows + 2 * own_rows, 8), :] = ext[pl.ds(c * ext_rows, 8), :]

    finish(flying)

    even = (lax.broadcasted_iota(jnp.int32, (cell_rows, LANES), 0) & 1) == 0
    up1 = lambda a: jnp.concatenate([a[1:], a[:1]], axis=0)
    down1 = lambda a: jnp.concatenate([a[-1:], a[:-1]], axis=0)
    turn = lambda a, n: pltpu.roll(a, n % LANES, 1)
    p_next = turn(p, -16)
    plus = jnp.where(lane < 112, p_next, jnp.where(even, up1(p_next), down1(turn(pres_in[1], -16))))
    p_prev = turn(p, 16)
    minus = jnp.where(lane >= 16, p_prev, jnp.where(even, up1(turn(pres_in[0], 16)), down1(p_prev)))
    slope_s[0:cell_rows] = (plus - minus) * 0.5
    plus = jnp.where((lane & 15) < 15, turn(p, -1), turn(pres_in[3], 15))
    minus = jnp.where((lane & 15) > 0, turn(p, 1), turn(pres_in[2], -15))
    slope_s[cell_rows : 2 * cell_rows] = (plus - minus) * 0.5
    none = jnp.zeros((2, LANES), F32)
    slope_s[2 * cell_rows : 3 * cell_rows] = (
        jnp.concatenate([p[2:], none], axis=0) - jnp.concatenate([none, p[:-2]], axis=0)
    ) * 0.5

    def free(k, carry):
        at = pl.ds(pl.multiple_of(k * 8, 8), 8)
        cells = cell_ref[at, :]
        cell_at, cell_lane = cells >> 7, cells & (LANES - 1)
        drag, mass = drag_ref[at, :], mass_ref[at, :]
        for c in range(3):
            slope = jnp.zeros((8, LANES), F32)
            for r in range(cell_rows):
                got = take_lanes(spread_row(slope_s, c * cell_rows + r), cell_lane)
                slope = jnp.where(cell_at == r, got, slope)
            v = vel_s[pl.ds(k * 24 + c, 8, stride=3), :]
            free_s[pl.ds(pl.multiple_of(c * own_rows + k * 8, 8), 8), :] = (
                v - TIME_STEP * (drag + mass) * slope
            ) / (1.0 + TIME_STEP * drag)
        return carry

    lax.fori_loop(0, own_rows // 8, free, 0, unroll=2)
    for c in range(3):
        spread_current(c, free_s[c * own_rows : (c + 1) * own_rows, :])
    pick_bound(0)
    flying = exchange(1, lambda g: ghost_out.at[0], lambda g: ghost_in.at[0, g])

    iotas = [
        (lax.broadcasted_iota(jnp.int32, (16, LANES), 0) + 16 * q).astype(F32).astype(BF16)
        for q in range(HALF // 16)
    ]
    signs = [jnp.full((16, LANES), sign, BF16) for sign in (1.0, -1.0)]
    zero16 = jnp.zeros((16, LANES), BF16)

    def build(t, carry):
        for e in range(2):
            row = jnp.broadcast_to(spots[pl.ds(e * tiles + t, 1), :], (16, LANES)).astype(BF16)
            for q in range(HALF // 16):
                at = slice(e * HALF + 16 * q, e * HALF + 16 * (q + 1))
                table[t, at, :] = jnp.where(iotas[q] == row, signs[e], zero16)
        return carry

    lax.fori_loop(0, tiles, build, 0, unroll=4)
    for i in range(32):
        left[i * PITCH + 36 : i * PITCH + ROWS, :] = jnp.zeros((12, LANES), F32)

    nt = (((1,), (1,)), ((), ()))
    for sweep in range(SWEEPS):
        finish(flying)
        for c in range(3):
            spread_halves(
                ghost_s,
                c * gpad,
                jnp.concatenate(
                    [
                        ghost_in[sweep, g, c * side_rows : (c + 1) * side_rows, :]
                        for g in range(4)
                    ],
                    axis=0,
                ),
            )

        def contacts(u, odd):
            at = pl.ds(pl.multiple_of(u * 8, 8), 8)
            code, lanes = [], []
            for e in range(2):
                end_at = pl.ds(pl.multiple_of(e * tiles + u * 8, 8), 8)
                code.append(codes[end_at, :])
                lanes.append(lanes_s[end_at, :])
            relative = []
            for c in range(3):
                near = ext[pl.ds(c * ext_rows + u * 8, 8), :]
                next_ = ext[pl.ds(c * ext_rows + u * 8 + 2, 8), :]
                far = jnp.where(
                    row_iota < 4,
                    spread_row(ghost_s, c * gpad + 2 * u),
                    spread_row(ghost_s, c * gpad + 2 * u + 1),
                )
                ends_val = []
                for e in range(2):
                    val = jnp.where(
                        code[e] < 4, take_lanes(next_, lanes[e]), take_lanes(far, lanes[e])
                    )
                    ends_val.append(jnp.where(code[e] < 2, take_lanes(near, lanes[e]), val))
                relative.append(ends_val[0] - ends_val[1])
            part = lambda k: stage[pl.ds(u * (8 * STAGE) + k, 8, stride=STAGE), :]
            fr = [part(k) for k in range(9)]
            target = [
                fr[3 * m] * relative[0]
                + fr[3 * m + 1] * relative[1]
                + fr[3 * m + 2] * relative[2]
                + part(40 + m)
                for m in range(3)
            ]
            trial = []
            for k in range(3):
                before = part(32 + k)
                trial.append(
                    before
                    - (
                        part(16 + 3 * k) * target[0]
                        + part(17 + 3 * k) * target[1]
                        + part(18 + 3 * k) * target[2]
                    )
                )
            active = mask_ref[at, :].astype(F32)
            normal = jnp.maximum(trial[0], 0.0)
            tangent = jnp.sqrt(trial[1] * trial[1] + trial[2] * trial[2])
            factor = jnp.minimum(1.0, FRICTION * normal / jnp.maximum(tangent, FLOOR_VALUE))
            imp = [normal * active, factor * trial[1] * active, factor * trial[2] * active]
            for k in range(3):
                stage[pl.ds(u * (8 * STAGE) + 32 + k, 8, stride=STAGE), :] = imp[k]
            for c in range(3):
                push = fr[c] * imp[0] + fr[3 + c] * imp[1] + fr[6 + c] * imp[2]
                high = push.astype(BF16).astype(F32)
                for s, term in enumerate((high, push - high)):
                    for e in range(2):
                        for h in range(6):
                            left[
                                pl.ds((e * 8 + odd) * PITCH + (h * 3 + c) * 2 + s, 8, stride=PITCH), :
                            ] = jnp.where(code[e] == h, term, 0.0)
            ghost_sum = None
            for i in range(8):
                got = lax.dot_general(
                    jnp.concatenate(
                        [
                            left[(odd + i) * PITCH : (odd + i) * PITCH + ROWS, :].astype(BF16),
                            left[(odd + i + 8) * PITCH : (odd + i + 8) * PITCH + ROWS, :].astype(BF16),
                        ],
                        axis=1,
                    ),
                    jnp.concatenate(
                        [
                            table[u * 8 + i, e * HALF : (e + 1) * HALF, :]
                            for e in range(2)
                        ],
                        axis=1,
                    ),
                    nt,
                    preferred_element_type=F32,
                )
                at = ((i & 1) * own_part + u * 4 + (i >> 1) + 2) * OWN_PITCH
                sums[pl.ds(at, 24), 0:HALF] = got[0:24]
                ghost_sum = got[24:40] if i % 4 == 0 else ghost_sum + got[24:40]
                if i % 4 == 3:
                    at = ((i >> 2) * ghost_part + u + 1) * GHOST_PITCH
                    ghost_sums[pl.ds(at, 16), 0:HALF] = ghost_sum

        def two(k, carry):
            contacts(2 * k, 0)
            contacts(2 * k + 1, 16)
            return carry

        lax.fori_loop(0, tiles // 16, two, 0, unroll=2)
        for par in range(2):
            base = par * ghost_part * GHOST_PITCH
            ghost_sums[base : base + GHOST_PITCH, :] = ghost_sums[
                base + ghost_rows * GHOST_PITCH : base + (ghost_rows + 1) * GHOST_PITCH, :
            ]
            base = par * own_part * OWN_PITCH
            sums[base : base + 2 * OWN_PITCH, :] = sums[
                base + own_rows * OWN_PITCH : base + (own_rows + 2) * OWN_PITCH, :
            ]
        first_half = lax.broadcasted_iota(jnp.int32, (8, LANES), 1) < HALF

        def gather_halves(ref, part_rows, pitch, pad, r, terms):
            halves = []
            for par in range(2):
                total = None
                for h, row in terms:
                    for s in range(2):
                        block = par - h
                        first = ((block & 1) * part_rows + r + (block >> 1) + pad) * pitch + row + s
                        got = ref[pl.ds(first, 8, stride=pitch), :]
                        total = got if total is None else total + got
                halves.append(total)
            return jnp.where(first_half, halves[0], pltpu.roll(halves[1], HALF, 1))

        for c in range(3):
            for r in range(0, ghost_rows, 8):
                terms = [(h, h * 6 + c * 2) for h in range(2)]
                total = gather_halves(ghost_sums, ghost_part, GHOST_PITCH, 1, r, terms)
                for i in range(0, 8, side_rows):
                    sum_out[
                        sweep, (r + i) // side_rows, c * side_rows : (c + 1) * side_rows, :
                    ] = total[i : i + side_rows]
        flying = exchange(2 + 2 * sweep, lambda g: sum_out.at[sweep, g], lambda g: sum_in.at[sweep, g])
        own_total = []
        for c in range(3):
            parts = []
            for r in range(0, own_rows, 8):
                terms = [(h, h * 6 + c * 2) for h in range(4)]
                parts.append(gather_halves(sums, own_part, OWN_PITCH, 2, r, terms))
            own_total.append(jnp.concatenate(parts, axis=0))
        if sweep == SWEEPS - 1:

            def unstage(t, carry):
                cols = pl.ds(pl.multiple_of(t * LANES, LANES), LANES)
                start_ref[:, cols] = stage[pl.ds(t * STAGE + 32, 3), :]
                return carry

            lax.fori_loop(0, tiles, unstage, 0, unroll=8)
            imp_store = pltpu.make_async_copy(start_ref, out_imp, load_sem.at[0])
            imp_store.start()
        finish(flying)
        received = (
            sum_in[sweep, 0] + sum_in[sweep, 1] + sum_in[sweep, 2] + sum_in[sweep, 3]
        )
        high = received.astype(BF16).astype(F32)
        low = received - high
        mass = mass_ref[...]
        for c in range(3):
            total = own_total[c]
            for term in (high, low):
                row = jnp.concatenate(
                    [
                        bound_row[:, q * LANES : (q + 1) * LANES]
                        * jnp.broadcast_to(
                            term[c * side_rows + q : c * side_rows + q + 1], (own_rows, LANES)
                        ).astype(BF16)
                        for q in range(side_rows)
                    ],
                    axis=1,
                )
                total = total + lax.dot_general(
                    row, bound_hot[...], nt, preferred_element_type=F32
                )
            current = free_s[c * own_rows : (c + 1) * own_rows, :] + mass * total
            if sweep < SWEEPS - 1:
                spread_current(c, current)
            else:
                vel_s[pl.ds(c, own_rows, stride=3), :] = current
        if sweep < SWEEPS - 1:
            pick_bound(sweep + 1)
            flying = exchange(
                3 + 2 * sweep, lambda g: ghost_out.at[sweep + 1], lambda g: ghost_in.at[sweep + 1, g]
            )

    def unstage_grain(t, carry):
        cols = pl.ds(pl.multiple_of(t * LANES, LANES), LANES)
        vel_ref[:, cols] = vel_s[pl.ds(t * 3, 3), :]
        return carry

    lax.fori_loop(0, own_rows, unstage_grain, 0, unroll=8)
    vel_store = pltpu.make_async_copy(vel_ref, out_vel, load_sem.at[1])
    vel_store.start()
    for copy in sent:
        copy.wait_send()
    imp_store.wait()
    vel_store.wait()


def solution(mesh):
    sizes = (mesh.shape["gx"], mesh.shape["gy"])

    def local(
        velocity, inv_mass, drag, grain_cell, boundary_list, contact_pair, frames, blocks,
        impulse_start, gap, contact_mask, pressure,
    ):
        own_rows = velocity.shape[1] // LANES
        tiles = contact_pair.shape[1] // LANES
        side_rows = boundary_list.shape[0] // LANES
        cell_rows = pressure.size // LANES
        gpad = 8 * side_rows
        rounds = 1 + 2 * SWEEPS
        out_vel, out_imp = pl.pallas_call(
            lambda *refs: step_kernel(sizes, *refs),
            out_shape=(
                jax.ShapeDtypeStruct(velocity.shape, F32),
                jax.ShapeDtypeStruct(impulse_start.shape, F32),
            ),
            in_specs=[pl.BlockSpec(memory_space=pltpu.HBM)] * 12,
            out_specs=(pl.BlockSpec(memory_space=pltpu.HBM),) * 2,
            scratch_shapes=[
                pltpu.VMEM((3, velocity.shape[1]), F32),
                pltpu.VMEM((own_rows, LANES), F32),
                pltpu.VMEM((own_rows, LANES), F32),
                pltpu.VMEM((own_rows, LANES), jnp.int32),
                pltpu.VMEM((side_rows, LANES), jnp.int32),
                pltpu.VMEM((2, contact_pair.shape[1]), jnp.int32),
                pltpu.VMEM((9, contact_pair.shape[1]), F32),
                pltpu.VMEM((9, contact_pair.shape[1]), F32),
                pltpu.VMEM((3, contact_pair.shape[1]), F32),
                pltpu.VMEM((3, contact_pair.shape[1]), F32),
                pltpu.VMEM((tiles, LANES), jnp.int32),
                pltpu.VMEM(pressure.shape, F32),
                pltpu.VMEM((pressure.size // pressure.shape[2], LANES), F32),
                pltpu.VMEM((cell_rows, LANES), F32),
                pltpu.VMEM((4, cell_rows, LANES), F32),
                pltpu.VMEM((SWEEPS, 4, 3 * side_rows, LANES), F32),
                pltpu.VMEM((SWEEPS, 4, 3 * side_rows, LANES), F32),
                pltpu.VMEM((SWEEPS, 3 * side_rows, LANES), F32),
                pltpu.VMEM((SWEEPS, 4, 3 * side_rows, LANES), F32),
                pltpu.VMEM((3 * cell_rows, LANES), F32),
                pltpu.VMEM((own_rows * 3, LANES), F32),
                pltpu.VMEM((3 * own_rows, LANES), F32),
                pltpu.VMEM((tiles * STAGE, LANES), F32),
                pltpu.VMEM((tiles * 3, LANES), jnp.int32),
                pltpu.VMEM((2 * tiles, LANES), jnp.int32),
                pltpu.VMEM((2 * tiles, LANES), jnp.int32),
                pltpu.VMEM((2 * tiles, LANES), F32),
                pltpu.VMEM((tiles, LANES, LANES), BF16),
                pltpu.VMEM((3 * (2 * own_rows + 8), LANES), F32),
                pltpu.VMEM((3 * gpad, LANES), F32),
                pltpu.VMEM((32 * PITCH, LANES), F32),
                pltpu.VMEM((2 * (own_rows + 2) * OWN_PITCH, LANES), F32),
                pltpu.VMEM((2 * (4 * side_rows + 1) * GHOST_PITCH, LANES), F32),
                pltpu.VMEM((LANES, side_rows * LANES), BF16),
                pltpu.VMEM((own_rows, side_rows * LANES), BF16),
                pltpu.SemaphoreType.DMA((rounds, 4)),
                pltpu.SemaphoreType.DMA((rounds, 4)),
                pltpu.SemaphoreType.DMA((12,)),
            ],
            compiler_params=pltpu.CompilerParams(
                collective_id=0, has_side_effects=True, vmem_limit_bytes=62 * 1024 * 1024
            ),
        )(
            velocity,
            inv_mass.reshape(own_rows, LANES),
            drag.reshape(own_rows, LANES),
            grain_cell.reshape(own_rows, LANES),
            boundary_list.reshape(side_rows, LANES),
            contact_pair,
            frames,
            blocks,
            impulse_start,
            gap,
            contact_mask.reshape(tiles, LANES),
            pressure,
        )
        return out_vel, out_imp

    grains, lists = P(("gx", "gy")), P(None, ("gx", "gy"))
    return jax.shard_map(
        local,
        mesh=mesh,
        in_specs=(
            lists, grains, grains, grains, grains, lists, lists, lists, lists, lists, grains,
            P(None, "gx", "gy"),
        ),
        out_specs=(lists, lists),
        check_vma=False,
    )
```

```python
import jax
import jax.numpy as jnp
from jax import lax
from jax.experimental import pallas as pl
from jax.experimental.pallas import tpu as pltpu
from jax.sharding import PartitionSpec as P

SWEEPS = 2
TIME_STEP = 0.5
FRICTION = 0.5
FLOOR_VALUE = 0.1
LANES = 128
HALF = LANES // 2
ROWS = 48
PITCH = 49
STAGE = 49
OWN_PITCH = 25
GHOST_PITCH = 17
F32 = jnp.float32
BF16 = jnp.bfloat16
NEAR = ((-1, 0), (1, 0), (0, -1), (0, 1))
FAR = ((-2, 0), (2, 0), (0, -2), (0, 2), (-1, -1), (-1, 1), (1, -1), (1, 1))
AROUND = NEAR + FAR


def take_lanes(values, lanes):
    return jnp.take_along_axis(values, lanes, axis=1, mode="promise_in_bounds")


def spread_row(ref, row):
    return jnp.broadcast_to(ref[pl.ds(row, 1), :], (8, LANES))


def step_kernel(
    sizes,
    vel_hbm, mass_hbm, drag_hbm, cell_hbm, bound_hbm, pair_hbm, frame_hbm, block_hbm,
    start_hbm, gap_hbm, mask_hbm, pres_hbm,
    out_vel, out_imp,
    vel_ref, mass_ref, drag_ref, cell_ref, bound_ref, pair_ref, frame_ref, block_ref,
    start_ref, gap_ref, mask_ref, pres_raw, pres_wide, pres_ref,
    pres_in, grain_in, grain_out, ghost_in, sum_in, ghost_out, sum_out,
    slope_s, slope_n, vel_s, free_s, stage, ends, codes, lanes_s, spots, table, ext, ghost_s,
    left, sums, ghost_sums, bound_hot, bound_row,
    send_sem, recv_sem, pres_send, pres_recv, load_sem,
):
    nx, ny = sizes
    tiles = mask_ref.shape[0]
    own_rows = mass_ref.shape[0]
    side_rows = bound_ref.shape[0]
    ghost_rows = 4 * side_rows
    cell_rows = pres_ref.shape[0]
    ext_rows = 2 * own_rows + 8
    gpad = 2 * ghost_rows
    own_slots = own_rows * LANES
    ghost_slots = ghost_rows * LANES
    own_part = own_rows + 2
    ghost_part = ghost_rows + 1
    row_iota = lax.broadcasted_iota(jnp.int32, (8, LANES), 0)

    mx, my = lax.axis_index("gx"), lax.axis_index("gy")
    reach = lambda dx, dy: (lax.rem(mx + dx + 2 * nx, nx), lax.rem(my + dy + 2 * ny, ny))
    sides = [reach(dx, dy) for dx, dy in NEAR]
    others = [k for k, (dx, dy) in enumerate(AROUND) if dx % nx or dy % ny]

    loads = [
        pltpu.make_async_copy(source, target, load_sem.at[k])
        for k, (source, target) in enumerate(
            (
                (vel_hbm, vel_ref), (bound_hbm, bound_ref), (drag_hbm, drag_ref),
                (mass_hbm, mass_ref), (cell_hbm, cell_ref), (pair_hbm, pair_ref),
                (mask_hbm, mask_ref), (start_hbm, start_ref), (gap_hbm, gap_ref),
                (frame_hbm, frame_ref), (block_hbm, block_ref),
            )
        )
    ]
    pres_load = pltpu.make_async_copy(pres_hbm, pres_raw, load_sem.at[11])
    pres_load.start()
    for load in loads:
        load.start()

    barrier = pltpu.get_barrier_semaphore()
    for k in others:
        pl.semaphore_signal(
            barrier, inc=1, device_id=reach(*AROUND[k]), device_id_type=pl.DeviceIdType.MESH
        )

    lane = lax.broadcasted_iota(jnp.int32, (cell_rows, LANES), 1)
    pres_load.wait()
    width = pres_raw.shape[2]
    pres_wide[:, 0:width] = pres_raw[...].reshape(-1, width)
    per_row = LANES // width
    p = pres_wide[pl.ds(0, cell_rows, stride=per_row), :]
    for k in range(1, per_row):
        piece = pltpu.roll(pres_wide[pl.ds(k, cell_rows, stride=per_row), :], k * width, 1)
        p = jnp.where(lane < k * width, p, piece)
    pres_ref[...] = p
    def exchange(step, source, target):
        copies = []
        for g in range(4):
            copies.append(
                pltpu.make_async_remote_copy(
                    src_ref=source(g),
                    dst_ref=target(g ^ 1),
                    send_sem=send_sem.at[step, g],
                    recv_sem=recv_sem.at[step, g ^ 1],
                    device_id=sides[g],
                    device_id_type=pl.DeviceIdType.MESH,
                )
            )
        for copy in copies:
            copy.start()
        return copies

    sent = []

    def finish(copies):
        for copy in copies:
            copy.wait_recv()
        sent.extend(copies)

    for load in loads[:5]:
        load.wait()
    bound_all = bound_ref[...]
    bound_lane = bound_all & (LANES - 1)
    bound_at = bound_all >> 7
    two_lane = jnp.concatenate([bound_lane, bound_lane], axis=0)
    two_at = jnp.concatenate([bound_at, bound_at], axis=0)
    half = own_rows // 2
    upper = row_iota < side_rows
    low_at = two_at < half

    def pick(row_of, kinds):
        def body(k, acc):
            acc = list(acc)
            for i in range(4):
                r = k * 4 + i
                hit = two_at == jnp.where(upper, r, r + half)
                for c in range(len(kinds)):
                    got = take_lanes(jnp.where(upper, row_of(c, r), row_of(c, r + half)), two_lane)
                    acc[c] = jnp.where(hit, got, acc[c])
            return tuple(acc)

        start = tuple(jnp.zeros((8, LANES), kind) for kind in kinds)
        acc = lax.fori_loop(0, half // 4, body, start, unroll=2)
        return [
            jnp.where(low_at[:side_rows], got[:side_rows], got[side_rows:]) for got in acc
        ]

    def grain_row(c, r):
        if c < 3:
            cols = pl.ds(pl.multiple_of(r * LANES, LANES), LANES)
            return jnp.broadcast_to(vel_ref[pl.ds(c, 1), cols], (8, LANES))
        return spread_row((drag_ref, mass_ref, cell_ref)[c - 3], r)

    *moving, drag_b, mass_b, cell_b = pick(grain_row, (F32,) * 5 + (jnp.int32,))
    below = 1.0 + TIME_STEP * drag_b
    for c in range(3):
        grain_out[c * side_rows : (c + 1) * side_rows, :] = moving[c] / below
    grain_out[3 * side_rows : 4 * side_rows, :] = TIME_STEP * (drag_b + mass_b) / below
    grain_out[4 * side_rows : 5 * side_rows, :] = cell_b.astype(F32)
    pl.semaphore_wait(barrier, len(others))
    spreading = {}
    for k in others:
        dx, dy = AROUND[k]
        back = AROUND.index((-dx, -dy))
        spreading[back] = pltpu.make_async_remote_copy(
            src_ref=pres_ref,
            dst_ref=pres_in.at[back],
            send_sem=pres_send.at[k],
            recv_sem=pres_recv.at[back],
            device_id=reach(dx, dy),
            device_id_type=pl.DeviceIdType.MESH,
        )
    for copy in spreading.values():
        copy.start()
    flying = exchange(0, lambda g: grain_out, lambda g: grain_in.at[g])
    for load in loads[5:]:
        load.wait()

    def stage_tile(t, carry):
        cols = pl.ds(pl.multiple_of(t * LANES, LANES), LANES)
        base = t * STAGE
        stage[pl.ds(base, 9), :] = frame_ref[:, cols]
        stage[pl.ds(base + 16, 9), :] = block_ref[:, cols]
        stage[pl.ds(base + 32, 3), :] = start_ref[:, cols]
        stage[pl.ds(base + 40, 3), :] = gap_ref[:, cols]
        ends[pl.ds(t * 3, 2), :] = pair_ref[:, cols]
        return carry

    lax.fori_loop(0, tiles, stage_tile, 0, unroll=4)

    def stage_grain(t, carry):
        cols = pl.ds(pl.multiple_of(t * LANES, LANES), LANES)
        vel_s[pl.ds(t * 3, 3), :] = vel_ref[:, cols]
        return carry

    lax.fori_loop(0, own_rows, stage_grain, 0, unroll=4)

    def place(u, carry):
        tile = u * 8 + row_iota
        for e in range(2):
            slot = ends[pl.ds(u * 24 + 1 - e, 8, stride=3), :]
            own = slot < own_slots
            near = (slot - HALF * tile) & (own_slots - 1)
            far = (slot - own_slots - HALF * (tile >> 2)) & (ghost_slots - 1)
            rel = jnp.where(own, near, far)
            at = pl.ds(pl.multiple_of(e * tiles + u * 8, 8), 8)
            codes[at, :] = jnp.where(own, 0, 4) + (rel >> 6)
            lanes_s[at, :] = rel & (LANES - 1)
            spots[at, :] = (rel & (HALF - 1)).astype(F32)
        return carry

    lax.fori_loop(0, tiles // 8, place, 0, unroll=2)

    hot_iota = lax.broadcasted_iota(jnp.int32, (LANES, LANES), 0)
    row_hot = lax.broadcasted_iota(jnp.int32, (own_rows, LANES), 0)
    for q in range(side_rows):
        cols = slice(q * LANES, (q + 1) * LANES)
        bound_hot[:, cols] = jnp.where(hot_iota == bound_lane[q : q + 1], 1.0, 0.0).astype(BF16)
        bound_row[:, cols] = jnp.where(row_hot == bound_at[q : q + 1], 1.0, 0.0).astype(BF16)

    def pick_bound(turn):
        got = pick(lambda c, r: spread_row(ext, c * ext_rows + 2 * r), (F32,) * 3)
        for c in range(3):
            ghost_out[turn, c * side_rows : (c + 1) * side_rows, :] = got[c]

    def spread_halves(ref, first, value):
        rows = value.shape[0]
        turned = pltpu.roll(value, HALF, 1)
        after = jnp.concatenate([turned[1:], turned[:1]], axis=0)
        first_half = lax.broadcasted_iota(jnp.int32, value.shape, 1) < HALF
        ref[pl.ds(first, rows, stride=2), :] = value
        ref[pl.ds(first + 1, rows, stride=2), :] = jnp.where(first_half, turned, after)

    def spread_current(c, value):
        spread_halves(ext, c * ext_rows, value)
        ext[pl.ds(c * ext_rows + 2 * own_rows, 8), :] = ext[pl.ds(c * ext_rows, 8), :]

    iotas = [
        (lax.broadcasted_iota(jnp.int32, (16, LANES), 0) + 16 * q).astype(F32).astype(BF16)
        for q in range(HALF // 16)
    ]
    signs = [jnp.full((16, LANES), sign, BF16) for sign in (1.0, -1.0)]
    zero16 = jnp.zeros((16, LANES), BF16)

    def build(t, carry):
        for e in range(2):
            row = jnp.broadcast_to(spots[pl.ds(e * tiles + t, 1), :], (16, LANES)).astype(BF16)
            for q in range(HALF // 16):
                at = slice(e * HALF + 16 * q, e * HALF + 16 * (q + 1))
                table[t, at, :] = jnp.where(iotas[q] == row, signs[e], zero16)
        return carry

    lax.fori_loop(0, tiles, build, 0, unroll=4)
    for i in range(32):
        left[i * PITCH + 36 : i * PITCH + ROWS, :] = jnp.zeros((12, LANES), F32)

    for k in range(4):
        spreading[k].wait_recv()
    even = (lax.broadcasted_iota(jnp.int32, (cell_rows, LANES), 0) & 1) == 0
    up1 = lambda a: jnp.concatenate([a[1:], a[:1]], axis=0)
    down1 = lambda a: jnp.concatenate([a[-1:], a[:-1]], axis=0)
    turn = lambda a, n: pltpu.roll(a, n % LANES, 1)
    none = jnp.zeros((2, LANES), F32)

    def pres_at(dx, dy):
        if dx % nx == 0 and dy % ny == 0:
            return p
        return pres_in[AROUND.index((dx, dy))]

    def slopes(ref, first, dx, dy):
        mid = pres_at(dx, dy)
        prev_x, next_x = pres_at(dx - 1, dy), pres_at(dx + 1, dy)
        prev_y, next_y = pres_at(dx, dy - 1), pres_at(dx, dy + 1)
        after = turn(mid, -16)
        plus = jnp.where(lane < 112, after, jnp.where(even, up1(after), down1(turn(next_x, -16))))
        before = turn(mid, 16)
        minus = jnp.where(lane >= 16, before, jnp.where(even, up1(turn(prev_x, 16)), down1(before)))
        ref[first : first + cell_rows] = (plus - minus) * 0.5
        plus = jnp.where((lane & 15) < 15, turn(mid, -1), turn(next_y, 15))
        minus = jnp.where((lane & 15) > 0, turn(mid, 1), turn(prev_y, -15))
        ref[first + cell_rows : first + 2 * cell_rows] = (plus - minus) * 0.5
        ref[first + 2 * cell_rows : first + 3 * cell_rows] = (
            jnp.concatenate([mid[2:], none], axis=0) - jnp.concatenate([none, mid[:-2]], axis=0)
        ) * 0.5

    slopes(slope_s, 0, 0, 0)

    def free(k, carry):
        at = pl.ds(pl.multiple_of(k * 8, 8), 8)
        cells = cell_ref[at, :]
        cell_at, cell_lane = cells >> 7, cells & (LANES - 1)
        drag, mass = drag_ref[at, :], mass_ref[at, :]
        for c in range(3):
            slope = jnp.zeros((8, LANES), F32)
            for r in range(cell_rows):
                got = take_lanes(spread_row(slope_s, c * cell_rows + r), cell_lane)
                slope = jnp.where(cell_at == r, got, slope)
            v = vel_s[pl.ds(k * 24 + c, 8, stride=3), :]
            free_s[pl.ds(pl.multiple_of(c * own_rows + k * 8, 8), 8), :] = (
                v - TIME_STEP * (drag + mass) * slope
            ) / (1.0 + TIME_STEP * drag)
        return carry

    lax.fori_loop(0, own_rows // 8, free, 0, unroll=2)
    for c in range(3):
        spread_current(c, free_s[c * own_rows : (c + 1) * own_rows, :])
    for k in others[4:]:
        spreading[k].wait_recv()
    sent.extend(spreading.values())
    finish(flying)
    for g in range(4):
        slopes(slope_n, 3 * cell_rows * g, *NEAR[g])
    ghost_free = [[], [], []]
    for g in (0, 2):
        both = [
            jnp.concatenate(
                [grain_in[g + i, k * side_rows : (k + 1) * side_rows, :] for i in range(2)], axis=0
            )
            for k in range(5)
        ]
        cells = both[4].astype(jnp.int32)
        cell_at, cell_lane = cells >> 7, cells & (LANES - 1)
        for c in range(3):
            slope = jnp.zeros((8, LANES), F32)
            for r in range(cell_rows):
                first = (3 * g + c) * cell_rows + r
                row = jnp.where(
                    row_iota < side_rows,
                    spread_row(slope_n, first),
                    spread_row(slope_n, first + 3 * cell_rows),
                )
                slope = jnp.where(cell_at == r, take_lanes(row, cell_lane), slope)
            ghost_free[c].append(both[c] - both[3] * slope)
    for c in range(3):
        spread_halves(ghost_s, c * gpad, jnp.concatenate(ghost_free[c], axis=0))

    nt = (((1,), (1,)), ((), ()))
    for sweep in range(SWEEPS):
        def contacts(u, odd):
            at = pl.ds(pl.multiple_of(u * 8, 8), 8)
            code, lanes = [], []
            for e in range(2):
                end_at = pl.ds(pl.multiple_of(e * tiles + u * 8, 8), 8)
                code.append(codes[end_at, :])
                lanes.append(lanes_s[end_at, :])
            relative = []
            for c in range(3):
                near = ext[pl.ds(c * ext_rows + u * 8, 8), :]
                next_ = ext[pl.ds(c * ext_rows + u * 8 + 2, 8), :]
                far = jnp.where(
                    row_iota < 4,
                    spread_row(ghost_s, c * gpad + 2 * u),
                    spread_row(ghost_s, c * gpad + 2 * u + 1),
                )
                ends_val = []
                for e in range(2):
                    val = jnp.where(
                        code[e] < 4, take_lanes(next_, lanes[e]), take_lanes(far, lanes[e])
                    )
                    ends_val.append(jnp.where(code[e] < 2, take_lanes(near, lanes[e]), val))
                relative.append(ends_val[0] - ends_val[1])
            part = lambda k: stage[pl.ds(u * (8 * STAGE) + k, 8, stride=STAGE), :]
            fr = [part(k) for k in range(9)]
            target = [
                fr[3 * m] * relative[0]
                + fr[3 * m + 1] * relative[1]
                + fr[3 * m + 2] * relative[2]
                + part(40 + m)
                for m in range(3)
            ]
            trial = []
            for k in range(3):
                before = part(32 + k)
                trial.append(
                    before
                    - (
                        part(16 + 3 * k) * target[0]
                        + part(17 + 3 * k) * target[1]
                        + part(18 + 3 * k) * target[2]
                    )
                )
            active = mask_ref[at, :].astype(F32)
            normal = jnp.maximum(trial[0], 0.0)
            tangent = jnp.sqrt(trial[1] * trial[1] + trial[2] * trial[2])
            factor = jnp.minimum(1.0, FRICTION * normal / jnp.maximum(tangent, FLOOR_VALUE))
            imp = [normal * active, factor * trial[1] * active, factor * trial[2] * active]
            for k in range(3):
                stage[pl.ds(u * (8 * STAGE) + 32 + k, 8, stride=STAGE), :] = imp[k]
            for c in range(3):
                push = fr[c] * imp[0] + fr[3 + c] * imp[1] + fr[6 + c] * imp[2]
                high = push.astype(BF16).astype(F32)
                for s, term in enumerate((high, push - high)):
                    for e in range(2):
                        for h in range(6):
                            left[
                                pl.ds((e * 8 + odd) * PITCH + (h * 3 + c) * 2 + s, 8, stride=PITCH), :
                            ] = jnp.where(code[e] == h, term, 0.0)
            ghost_sum = None
            for i in range(8):
                got = lax.dot_general(
                    jnp.concatenate(
                        [
                            left[(odd + i) * PITCH : (odd + i) * PITCH + ROWS, :].astype(BF16),
                            left[(odd + i + 8) * PITCH : (odd + i + 8) * PITCH + ROWS, :].astype(BF16),
                        ],
                        axis=1,
                    ),
                    jnp.concatenate(
                        [
                            table[u * 8 + i, e * HALF : (e + 1) * HALF, :]
                            for e in range(2)
                        ],
                        axis=1,
                    ),
                    nt,
                    preferred_element_type=F32,
                )
                at = ((i & 1) * own_part + u * 4 + (i >> 1) + 2) * OWN_PITCH
                sums[pl.ds(at, 24), 0:HALF] = got[0:24]
                ghost_sum = got[24:40] if i % 4 == 0 else ghost_sum + got[24:40]
                if i % 4 == 3:
                    at = ((i >> 2) * ghost_part + u + 1) * GHOST_PITCH
                    ghost_sums[pl.ds(at, 16), 0:HALF] = ghost_sum

        def two(k, carry):
            contacts(2 * k, 0)
            contacts(2 * k + 1, 16)
            return carry

        lax.fori_loop(0, tiles // 16, two, 0, unroll=2)
        for par in range(2):
            base = par * ghost_part * GHOST_PITCH
            ghost_sums[base : base + GHOST_PITCH, :] = ghost_sums[
                base + ghost_rows * GHOST_PITCH : base + (ghost_rows + 1) * GHOST_PITCH, :
            ]
            base = par * own_part * OWN_PITCH
            sums[base : base + 2 * OWN_PITCH, :] = sums[
                base + own_rows * OWN_PITCH : base + (own_rows + 2) * OWN_PITCH, :
            ]
        first_half = lax.broadcasted_iota(jnp.int32, (8, LANES), 1) < HALF

        def gather_halves(ref, part_rows, pitch, pad, r, terms):
            halves = []
            for par in range(2):
                total = None
                for h, row in terms:
                    for s in range(2):
                        block = par - h
                        first = ((block & 1) * part_rows + r + (block >> 1) + pad) * pitch + row + s
                        got = ref[pl.ds(first, 8, stride=pitch), :]
                        total = got if total is None else total + got
                halves.append(total)
            return jnp.where(first_half, halves[0], pltpu.roll(halves[1], HALF, 1))

        for c in range(3):
            for r in range(0, ghost_rows, 8):
                terms = [(h, h * 6 + c * 2) for h in range(2)]
                total = gather_halves(ghost_sums, ghost_part, GHOST_PITCH, 1, r, terms)
                for i in range(0, 8, side_rows):
                    sum_out[
                        sweep, (r + i) // side_rows, c * side_rows : (c + 1) * side_rows, :
                    ] = total[i : i + side_rows]
        flying = exchange(1 + 2 * sweep, lambda g: sum_out.at[sweep, g], lambda g: sum_in.at[sweep, g])
        own_total = []
        for c in range(3):
            parts = []
            for r in range(0, own_rows, 8):
                terms = [(h, h * 6 + c * 2) for h in range(4)]
                parts.append(gather_halves(sums, own_part, OWN_PITCH, 2, r, terms))
            own_total.append(jnp.concatenate(parts, axis=0))
        if sweep == SWEEPS - 1:

            def unstage(t, carry):
                cols = pl.ds(pl.multiple_of(t * LANES, LANES), LANES)
                start_ref[:, cols] = stage[pl.ds(t * STAGE + 32, 3), :]
                return carry

            lax.fori_loop(0, tiles, unstage, 0, unroll=8)
            imp_store = pltpu.make_async_copy(start_ref, out_imp, load_sem.at[0])
            imp_store.start()
        finish(flying)
        received = (
            sum_in[sweep, 0] + sum_in[sweep, 1] + sum_in[sweep, 2] + sum_in[sweep, 3]
        )
        high = received.astype(BF16).astype(F32)
        low = received - high
        mass = mass_ref[...]
        for c in range(3):
            total = own_total[c]
            for term in (high, low):
                row = jnp.concatenate(
                    [
                        bound_row[:, q * LANES : (q + 1) * LANES]
                        * jnp.broadcast_to(
                            term[c * side_rows + q : c * side_rows + q + 1], (own_rows, LANES)
                        ).astype(BF16)
                        for q in range(side_rows)
                    ],
                    axis=1,
                )
                total = total + lax.dot_general(
                    row, bound_hot[...], nt, preferred_element_type=F32
                )
            current = free_s[c * own_rows : (c + 1) * own_rows, :] + mass * total
            if sweep < SWEEPS - 1:
                spread_current(c, current)
            else:
                vel_s[pl.ds(c, own_rows, stride=3), :] = current
        if sweep < SWEEPS - 1:
            pick_bound(sweep)
            flying = exchange(
                2 + 2 * sweep, lambda g: ghost_out.at[sweep], lambda g: ghost_in.at[sweep, g]
            )
            finish(flying)
            for c in range(3):
                spread_halves(
                    ghost_s,
                    c * gpad,
                    jnp.concatenate(
                        [
                            ghost_in[sweep, g, c * side_rows : (c + 1) * side_rows, :]
                            for g in range(4)
                        ],
                        axis=0,
                    ),
                )

    def unstage_grain(t, carry):
        cols = pl.ds(pl.multiple_of(t * LANES, LANES), LANES)
        vel_ref[:, cols] = vel_s[pl.ds(t * 3, 3), :]
        return carry

    lax.fori_loop(0, own_rows, unstage_grain, 0, unroll=8)
    vel_store = pltpu.make_async_copy(vel_ref, out_vel, load_sem.at[1])
    vel_store.start()
    for copy in sent:
        copy.wait_send()
    imp_store.wait()
    vel_store.wait()


def hand_on(vel_in, imp_in, vel_out, imp_out, vel_ref, imp_ref, sem):
    pairs = ((imp_in, imp_ref, imp_out), (vel_in, vel_ref, vel_out))
    loads = [pltpu.make_async_copy(x, y, sem.at[0, k]) for k, (x, y, _) in enumerate(pairs)]
    stores = [pltpu.make_async_copy(y, z, sem.at[1, k]) for k, (_, y, z) in enumerate(pairs)]
    for load in loads:
        load.start()
    for load, store in zip(loads, stores):
        load.wait()
        store.start()
    for store in stores:
        store.wait()


def solution(mesh):
    sizes = (mesh.shape["gx"], mesh.shape["gy"])

    def local(
        velocity, inv_mass, drag, grain_cell, boundary_list, contact_pair, frames, blocks,
        impulse_start, gap, contact_mask, pressure,
    ):
        own_rows = velocity.shape[1] // LANES
        tiles = contact_pair.shape[1] // LANES
        side_rows = boundary_list.shape[0] // LANES
        cell_rows = pressure.size // LANES
        gpad = 8 * side_rows
        rounds = 2 * SWEEPS
        out_vel, out_imp = pl.pallas_call(
            lambda *refs: step_kernel(sizes, *refs),
            out_shape=(
                jax.ShapeDtypeStruct(velocity.shape, F32),
                jax.ShapeDtypeStruct(impulse_start.shape, F32),
            ),
            in_specs=[pl.BlockSpec(memory_space=pltpu.HBM)] * 12,
            out_specs=(pl.BlockSpec(memory_space=pltpu.HBM),) * 2,
            scratch_shapes=[
                pltpu.VMEM((3, velocity.shape[1]), F32),
                pltpu.VMEM((own_rows, LANES), F32),
                pltpu.VMEM((own_rows, LANES), F32),
                pltpu.VMEM((own_rows, LANES), jnp.int32),
                pltpu.VMEM((side_rows, LANES), jnp.int32),
                pltpu.VMEM((2, contact_pair.shape[1]), jnp.int32),
                pltpu.VMEM((9, contact_pair.shape[1]), F32),
                pltpu.VMEM((9, contact_pair.shape[1]), F32),
                pltpu.VMEM((3, contact_pair.shape[1]), F32),
                pltpu.VMEM((3, contact_pair.shape[1]), F32),
                pltpu.VMEM((tiles, LANES), jnp.int32),
                pltpu.VMEM(pressure.shape, F32),
                pltpu.VMEM((pressure.size // pressure.shape[2], LANES), F32),
                pltpu.VMEM((cell_rows, LANES), F32),
                pltpu.VMEM((12, cell_rows, LANES), F32),
                pltpu.VMEM((4, 5 * side_rows, LANES), F32),
                pltpu.VMEM((5 * side_rows, LANES), F32),
                pltpu.VMEM((SWEEPS - 1, 4, 3 * side_rows, LANES), F32),
                pltpu.VMEM((SWEEPS, 4, 3 * side_rows, LANES), F32),
                pltpu.VMEM((SWEEPS - 1, 3 * side_rows, LANES), F32),
                pltpu.VMEM((SWEEPS, 4, 3 * side_rows, LANES), F32),
                pltpu.VMEM((3 * cell_rows, LANES), F32),
                pltpu.VMEM((12 * cell_rows, LANES), F32),
                pltpu.VMEM((own_rows * 3, LANES), F32),
                pltpu.VMEM((3 * own_rows, LANES), F32),
                pltpu.VMEM((tiles * STAGE, LANES), F32),
                pltpu.VMEM((tiles * 3, LANES), jnp.int32),
                pltpu.VMEM((2 * tiles, LANES), jnp.int32),
                pltpu.VMEM((2 * tiles, LANES), jnp.int32),
                pltpu.VMEM((2 * tiles, LANES), F32),
                pltpu.VMEM((tiles, LANES, LANES), BF16),
                pltpu.VMEM((3 * (2 * own_rows + 8), LANES), F32),
                pltpu.VMEM((3 * gpad, LANES), F32),
                pltpu.VMEM((32 * PITCH, LANES), F32),
                pltpu.VMEM((2 * (own_rows + 2) * OWN_PITCH, LANES), F32),
                pltpu.VMEM((2 * (4 * side_rows + 1) * GHOST_PITCH, LANES), F32),
                pltpu.VMEM((LANES, side_rows * LANES), BF16),
                pltpu.VMEM((own_rows, side_rows * LANES), BF16),
                pltpu.SemaphoreType.DMA((rounds, 4)),
                pltpu.SemaphoreType.DMA((rounds, 4)),
                pltpu.SemaphoreType.DMA((12,)),
                pltpu.SemaphoreType.DMA((12,)),
                pltpu.SemaphoreType.DMA((12,)),
            ],
            compiler_params=pltpu.CompilerParams(
                collective_id=0, has_side_effects=True, vmem_limit_bytes=62 * 1024 * 1024
            ),
        )(
            velocity,
            inv_mass.reshape(own_rows, LANES),
            drag.reshape(own_rows, LANES),
            grain_cell.reshape(own_rows, LANES),
            boundary_list.reshape(side_rows, LANES),
            contact_pair,
            frames,
            blocks,
            impulse_start,
            gap,
            contact_mask.reshape(tiles, LANES),
            pressure,
        )
        return pl.pallas_call(
            hand_on,
            out_shape=(
                jax.ShapeDtypeStruct(velocity.shape, F32),
                jax.ShapeDtypeStruct(impulse_start.shape, F32),
            ),
            in_specs=[pl.BlockSpec(memory_space=pltpu.HBM)] * 2,
            out_specs=(pl.BlockSpec(memory_space=pltpu.HBM),) * 2,
            scratch_shapes=[
                pltpu.VMEM(velocity.shape, F32),
                pltpu.VMEM(impulse_start.shape, F32),
                pltpu.SemaphoreType.DMA((2, 2)),
            ],
        )(out_vel, out_imp)

    grains, lists = P(("gx", "gy")), P(None, ("gx", "gy"))
    return jax.shard_map(
        local,
        mesh=mesh,
        in_specs=(
            lists, grains, grains, grains, grains, lists, lists, lists, lists, lists, grains,
            P(None, "gx", "gy"),
        ),
        out_specs=(lists, lists),
        check_vma=False,
    )
```

```python
import jax
import jax.numpy as jnp
from jax import lax
from jax.experimental import pallas as pl
from jax.experimental.pallas import tpu as pltpu
from jax.sharding import PartitionSpec as P

SWEEPS = 2
TIME_STEP = 0.5
FRICTION = 0.5
FLOOR_VALUE = 0.1
LANES = 128
HALF = LANES // 2
ROWS = 48
PITCH = 49
STAGE = 49
OWN_PITCH = 25
GHOST_PITCH = 17
F32 = jnp.float32
BF16 = jnp.bfloat16
NEAR = ((-1, 0), (1, 0), (0, -1), (0, 1))
FAR = ((-2, 0), (2, 0), (0, -2), (0, 2), (-1, -1), (-1, 1), (1, -1), (1, 1))
AROUND = NEAR + FAR
ORDER = (0, 2, 1, 3, 0)
FIRST = {(-1, -1): 0, (1, -1): 1, (1, 1): 2, (-1, 1): 3, (-2, 0): 0, (0, -2): 1, (2, 0): 2, (0, 2): 3}


def take_lanes(values, lanes):
    return jnp.take_along_axis(values, lanes, axis=1, mode="promise_in_bounds")


def spread_row(ref, row):
    return jnp.broadcast_to(ref[pl.ds(row, 1), :], (8, LANES))


def step_kernel(
    sizes,
    vel_hbm, mass_hbm, drag_hbm, cell_hbm, bound_hbm, pair_hbm, frame_hbm, block_hbm,
    start_hbm, gap_hbm, mask_hbm, pres_hbm,
    out_vel, out_imp,
    vel_ref, mass_ref, drag_ref, cell_ref, bound_ref, pair_ref, frame_ref, block_ref,
    start_ref, gap_ref, mask_ref, pres_raw, pres_wide, pres_ref,
    pres_in, grain_in, grain_out, ghost_in, sum_in, far_in, ghost_out, sum_out,
    slope_s, slope_n, vel_s, free_s, stage, ends, codes, lanes_s, spots, table, ext, ghost_s,
    left, sums, ghost_sums, bound_hot, bound_row, part_s, same, split, joined,
    send_sem, recv_sem, pres_send, pres_recv, far_send, far_recv, load_sem,
):
    nx, ny = sizes
    tiles = mask_ref.shape[0]
    own_rows = mass_ref.shape[0]
    side_rows = bound_ref.shape[0]
    ghost_rows = 4 * side_rows
    cell_rows = pres_ref.shape[0]
    ext_rows = 2 * own_rows + 8
    gpad = 2 * ghost_rows
    own_slots = own_rows * LANES
    ghost_slots = ghost_rows * LANES
    own_part = own_rows + 2
    ghost_part = ghost_rows + 1
    row_iota = lax.broadcasted_iota(jnp.int32, (8, LANES), 0)

    mx, my = lax.axis_index("gx"), lax.axis_index("gy")
    reach = lambda dx, dy: (lax.rem(mx + dx + 2 * nx, nx), lax.rem(my + dy + 2 * ny, ny))
    sides = [reach(dx, dy) for dx, dy in NEAR]
    others = [k for k, (dx, dy) in enumerate(AROUND) if dx % nx or dy % ny]

    loads = [
        pltpu.make_async_copy(source, target, load_sem.at[k])
        for k, (source, target) in enumerate(
            (
                (vel_hbm, vel_ref), (bound_hbm, bound_ref), (drag_hbm, drag_ref),
                (mass_hbm, mass_ref), (cell_hbm, cell_ref), (pair_hbm, pair_ref),
                (mask_hbm, mask_ref), (start_hbm, start_ref), (gap_hbm, gap_ref),
                (frame_hbm, frame_ref), (block_hbm, block_ref),
            )
        )
    ]
    pres_load = pltpu.make_async_copy(pres_hbm, pres_raw, load_sem.at[11])
    pres_load.start()
    for load in loads:
        load.start()

    barrier = pltpu.get_barrier_semaphore()
    for k in others:
        pl.semaphore_signal(
            barrier, inc=1, device_id=reach(*AROUND[k]), device_id_type=pl.DeviceIdType.MESH
        )

    lane = lax.broadcasted_iota(jnp.int32, (cell_rows, LANES), 1)
    pres_load.wait()
    width = pres_raw.shape[2]
    pres_wide[:, 0:width] = pres_raw[...].reshape(-1, width)
    per_row = LANES // width
    p = pres_wide[pl.ds(0, cell_rows, stride=per_row), :]
    for k in range(1, per_row):
        piece = pltpu.roll(pres_wide[pl.ds(k, cell_rows, stride=per_row), :], k * width, 1)
        p = jnp.where(lane < k * width, p, piece)
    pres_ref[...] = p
    def exchange(step, source, target):
        copies = []
        for g in range(4):
            copies.append(
                pltpu.make_async_remote_copy(
                    src_ref=source(g),
                    dst_ref=target(g ^ 1),
                    send_sem=send_sem.at[step, g],
                    recv_sem=recv_sem.at[step, g ^ 1],
                    device_id=sides[g],
                    device_id_type=pl.DeviceIdType.MESH,
                )
            )
        for copy in copies:
            copy.start()
        return copies

    sent = []

    def finish(copies):
        for copy in copies:
            copy.wait_recv()
        sent.extend(copies)

    for load in loads[:5]:
        load.wait()
    bound_all = bound_ref[...]
    bound_lane = bound_all & (LANES - 1)
    bound_at = bound_all >> 7
    two_lane = jnp.concatenate([bound_lane, bound_lane], axis=0)
    two_at = jnp.concatenate([bound_at, bound_at], axis=0)
    half = own_rows // 2
    upper = row_iota < side_rows
    low_at = two_at < half

    def pick(row_of, kinds, unroll):
        def body(k, acc):
            acc = list(acc)
            for i in range(4):
                r = k * 4 + i
                hit = two_at == jnp.where(upper, r, r + half)
                for c in range(len(kinds)):
                    got = take_lanes(jnp.where(upper, row_of(c, r), row_of(c, r + half)), two_lane)
                    acc[c] = jnp.where(hit, got, acc[c])
            return tuple(acc)

        start = tuple(jnp.zeros((8, LANES), kind) for kind in kinds)
        acc = lax.fori_loop(0, half // 4, body, start, unroll=unroll)
        return [
            jnp.where(low_at[:side_rows], got[:side_rows], got[side_rows:]) for got in acc
        ]

    def grain_row(c, r):
        if c < 3:
            cols = pl.ds(pl.multiple_of(r * LANES, LANES), LANES)
            return jnp.broadcast_to(vel_ref[pl.ds(c, 1), cols], (8, LANES))
        return spread_row((drag_ref, mass_ref, cell_ref)[c - 3], r)

    *moving, drag_b, mass_b, cell_b = pick(grain_row, (F32,) * 5 + (jnp.int32,), 2)
    below = 1.0 + TIME_STEP * drag_b
    for c in range(3):
        grain_out[c * side_rows : (c + 1) * side_rows, :] = moving[c] / below
    grain_out[3 * side_rows : 4 * side_rows, :] = TIME_STEP * (drag_b + mass_b) / below
    grain_out[4 * side_rows : 5 * side_rows, :] = cell_b.astype(F32)
    grain_out[5 * side_rows : 6 * side_rows, :] = mass_b
    grain_out[6 * side_rows : 7 * side_rows, :] = bound_all.astype(F32)
    pl.semaphore_wait(barrier, len(others))
    spreading = {}
    for k in others:
        dx, dy = AROUND[k]
        back = AROUND.index((-dx, -dy))
        spreading[back] = pltpu.make_async_remote_copy(
            src_ref=pres_ref,
            dst_ref=pres_in.at[back],
            send_sem=pres_send.at[k],
            recv_sem=pres_recv.at[back],
            device_id=reach(dx, dy),
            device_id_type=pl.DeviceIdType.MESH,
        )
    for copy in spreading.values():
        copy.start()
    flying = exchange(0, lambda g: grain_out, lambda g: grain_in.at[g])
    for load in loads[5:]:
        load.wait()

    def stage_tile(t, carry):
        cols = pl.ds(pl.multiple_of(t * LANES, LANES), LANES)
        base = t * STAGE
        stage[pl.ds(base, 9), :] = frame_ref[:, cols]
        stage[pl.ds(base + 16, 9), :] = block_ref[:, cols]
        stage[pl.ds(base + 32, 3), :] = start_ref[:, cols]
        stage[pl.ds(base + 40, 3), :] = gap_ref[:, cols]
        ends[pl.ds(t * 3, 2), :] = pair_ref[:, cols]
        return carry

    lax.fori_loop(0, tiles, stage_tile, 0, unroll=4)

    def stage_grain(t, carry):
        cols = pl.ds(pl.multiple_of(t * LANES, LANES), LANES)
        vel_s[pl.ds(t * 3, 3), :] = vel_ref[:, cols]
        return carry

    lax.fori_loop(0, own_rows, stage_grain, 0, unroll=4)

    def place(u, carry):
        tile = u * 8 + row_iota
        for e in range(2):
            slot = ends[pl.ds(u * 24 + 1 - e, 8, stride=3), :]
            own = slot < own_slots
            near = (slot - HALF * tile) & (own_slots - 1)
            far = (slot - own_slots - HALF * (tile >> 2)) & (ghost_slots - 1)
            rel = jnp.where(own, near, far)
            at = pl.ds(pl.multiple_of(e * tiles + u * 8, 8), 8)
            codes[at, :] = jnp.where(own, 0, 4) + (rel >> 6)
            lanes_s[at, :] = rel & (LANES - 1)
            spots[at, :] = (rel & (HALF - 1)).astype(F32)
        return carry

    lax.fori_loop(0, tiles // 8, place, 0, unroll=2)

    hot_iota = lax.broadcasted_iota(jnp.int32, (LANES, LANES), 0)
    row_hot = lax.broadcasted_iota(jnp.int32, (own_rows, LANES), 0)
    for q in range(side_rows):
        cols = slice(q * LANES, (q + 1) * LANES)
        bound_hot[:, cols] = jnp.where(hot_iota == bound_lane[q : q + 1], 1.0, 0.0).astype(BF16)
        bound_row[:, cols] = jnp.where(row_hot == bound_at[q : q + 1], 1.0, 0.0).astype(BF16)

    def spread_halves(ref, first, value):
        rows = value.shape[0]
        turned = pltpu.roll(value, HALF, 1)
        after = jnp.concatenate([turned[1:], turned[:1]], axis=0)
        first_half = lax.broadcasted_iota(jnp.int32, value.shape, 1) < HALF
        ref[pl.ds(first, rows, stride=2), :] = value
        ref[pl.ds(first + 1, rows, stride=2), :] = jnp.where(first_half, turned, after)

    def spread_current(c, value):
        spread_halves(ext, c * ext_rows, value)
        ext[pl.ds(c * ext_rows + 2 * own_rows, 8), :] = ext[pl.ds(c * ext_rows, 8), :]

    iotas = [
        (lax.broadcasted_iota(jnp.int32, (16, LANES), 0) + 16 * q).astype(F32).astype(BF16)
        for q in range(HALF // 16)
    ]
    signs = [jnp.full((16, LANES), sign, BF16) for sign in (1.0, -1.0)]
    zero16 = jnp.zeros((16, LANES), BF16)

    def build(t, carry):
        for e in range(2):
            row = jnp.broadcast_to(spots[pl.ds(e * tiles + t, 1), :], (16, LANES)).astype(BF16)
            for q in range(HALF // 16):
                at = slice(e * HALF + 16 * q, e * HALF + 16 * (q + 1))
                table[t, at, :] = jnp.where(iotas[q] == row, signs[e], zero16)
        return carry

    lax.fori_loop(0, tiles, build, 0, unroll=4)
    for i in range(32):
        left[i * PITCH + 36 : i * PITCH + ROWS, :] = jnp.zeros((12, LANES), F32)

    for k in range(4):
        spreading[k].wait_recv()
    even = (lax.broadcasted_iota(jnp.int32, (cell_rows, LANES), 0) & 1) == 0
    up1 = lambda a: jnp.concatenate([a[1:], a[:1]], axis=0)
    down1 = lambda a: jnp.concatenate([a[-1:], a[:-1]], axis=0)
    turn = lambda a, n: pltpu.roll(a, n % LANES, 1)
    none = jnp.zeros((2, LANES), F32)

    def pres_at(dx, dy):
        if dx % nx == 0 and dy % ny == 0:
            return p
        return pres_in[AROUND.index((dx, dy))]

    def slopes(ref, first, dx, dy):
        mid = pres_at(dx, dy)
        prev_x, next_x = pres_at(dx - 1, dy), pres_at(dx + 1, dy)
        prev_y, next_y = pres_at(dx, dy - 1), pres_at(dx, dy + 1)
        after = turn(mid, -16)
        plus = jnp.where(lane < 112, after, jnp.where(even, up1(after), down1(turn(next_x, -16))))
        before = turn(mid, 16)
        minus = jnp.where(lane >= 16, before, jnp.where(even, up1(turn(prev_x, 16)), down1(before)))
        ref[first : first + cell_rows] = (plus - minus) * 0.5
        plus = jnp.where((lane & 15) < 15, turn(mid, -1), turn(next_y, 15))
        minus = jnp.where((lane & 15) > 0, turn(mid, 1), turn(prev_y, -15))
        ref[first + cell_rows : first + 2 * cell_rows] = (plus - minus) * 0.5
        ref[first + 2 * cell_rows : first + 3 * cell_rows] = (
            jnp.concatenate([mid[2:], none], axis=0) - jnp.concatenate([none, mid[:-2]], axis=0)
        ) * 0.5

    slopes(slope_s, 0, 0, 0)

    def free(k, carry):
        at = pl.ds(pl.multiple_of(k * 8, 8), 8)
        cells = cell_ref[at, :]
        cell_at, cell_lane = cells >> 7, cells & (LANES - 1)
        drag, mass = drag_ref[at, :], mass_ref[at, :]
        for c in range(3):
            slope = jnp.zeros((8, LANES), F32)
            for r in range(cell_rows):
                got = take_lanes(spread_row(slope_s, c * cell_rows + r), cell_lane)
                slope = jnp.where(cell_at == r, got, slope)
            v = vel_s[pl.ds(k * 24 + c, 8, stride=3), :]
            free_s[pl.ds(pl.multiple_of(c * own_rows + k * 8, 8), 8), :] = (
                v - TIME_STEP * (drag + mass) * slope
            ) / (1.0 + TIME_STEP * drag)
        return carry

    lax.fori_loop(0, own_rows // 8, free, 0, unroll=2)
    for c in range(3):
        spread_current(c, free_s[c * own_rows : (c + 1) * own_rows, :])
    for k in others[4:]:
        spreading[k].wait_recv()
    sent.extend(spreading.values())
    finish(flying)
    for g in range(4):
        slopes(slope_n, 3 * cell_rows * g, *NEAR[g])
    ghost_free = [[], [], []]
    for g in (0, 2):
        both = [
            jnp.concatenate(
                [grain_in[g + i, k * side_rows : (k + 1) * side_rows, :] for i in range(2)], axis=0
            )
            for k in range(5)
        ]
        cells = both[4].astype(jnp.int32)
        cell_at, cell_lane = cells >> 7, cells & (LANES - 1)
        for c in range(3):
            slope = jnp.zeros((8, LANES), F32)
            for r in range(cell_rows):
                first = (3 * g + c) * cell_rows + r
                row = jnp.where(
                    row_iota < side_rows,
                    spread_row(slope_n, first),
                    spread_row(slope_n, first + 3 * cell_rows),
                )
                slope = jnp.where(cell_at == r, take_lanes(row, cell_lane), slope)
            ghost_free[c].append(both[c] - both[3] * slope)
    for c in range(3):
        spread_halves(ghost_s, c * gpad, jnp.concatenate(ghost_free[c], axis=0))

    split[...] = jnp.zeros(split.shape, F32)
    nt = (((1,), (1,)), ((), ()))
    for sweep in range(SWEEPS):
        def contacts(u, odd):
            at = pl.ds(pl.multiple_of(u * 8, 8), 8)
            code, lanes = [], []
            for e in range(2):
                end_at = pl.ds(pl.multiple_of(e * tiles + u * 8, 8), 8)
                code.append(codes[end_at, :])
                lanes.append(lanes_s[end_at, :])
            relative = []
            for c in range(3):
                near = ext[pl.ds(c * ext_rows + u * 8, 8), :]
                next_ = ext[pl.ds(c * ext_rows + u * 8 + 2, 8), :]
                far = jnp.where(
                    row_iota < 4,
                    spread_row(ghost_s, c * gpad + 2 * u),
                    spread_row(ghost_s, c * gpad + 2 * u + 1),
                )
                ends_val = []
                for e in range(2):
                    val = jnp.where(
                        code[e] < 4, take_lanes(next_, lanes[e]), take_lanes(far, lanes[e])
                    )
                    ends_val.append(jnp.where(code[e] < 2, take_lanes(near, lanes[e]), val))
                relative.append(ends_val[0] - ends_val[1])
            part = lambda k: stage[pl.ds(u * (8 * STAGE) + k, 8, stride=STAGE), :]
            fr = [part(k) for k in range(9)]
            target = [
                fr[3 * m] * relative[0]
                + fr[3 * m + 1] * relative[1]
                + fr[3 * m + 2] * relative[2]
                + part(40 + m)
                for m in range(3)
            ]
            trial = []
            for k in range(3):
                before = part(32 + k)
                trial.append(
                    before
                    - (
                        part(16 + 3 * k) * target[0]
                        + part(17 + 3 * k) * target[1]
                        + part(18 + 3 * k) * target[2]
                    )
                )
            active = mask_ref[at, :].astype(F32)
            normal = jnp.maximum(trial[0], 0.0)
            tangent = jnp.sqrt(trial[1] * trial[1] + trial[2] * trial[2])
            factor = jnp.minimum(1.0, FRICTION * normal / jnp.maximum(tangent, FLOOR_VALUE))
            imp = [normal * active, factor * trial[1] * active, factor * trial[2] * active]
            for k in range(3):
                stage[pl.ds(u * (8 * STAGE) + 32 + k, 8, stride=STAGE), :] = imp[k]
            for c in range(3):
                push = fr[c] * imp[0] + fr[3 + c] * imp[1] + fr[6 + c] * imp[2]
                high = push.astype(BF16).astype(F32)
                for s, term in enumerate((high, push - high)):
                    for e in range(2):
                        for h in range(6):
                            left[
                                pl.ds((e * 8 + odd) * PITCH + (h * 3 + c) * 2 + s, 8, stride=PITCH), :
                            ] = jnp.where(code[e] == h, term, 0.0)
            ghost_sum = None
            for i in range(8):
                got = lax.dot_general(
                    jnp.concatenate(
                        [
                            left[(odd + i) * PITCH : (odd + i) * PITCH + ROWS, :].astype(BF16),
                            left[(odd + i + 8) * PITCH : (odd + i + 8) * PITCH + ROWS, :].astype(BF16),
                        ],
                        axis=1,
                    ),
                    jnp.concatenate(
                        [
                            table[u * 8 + i, e * HALF : (e + 1) * HALF, :]
                            for e in range(2)
                        ],
                        axis=1,
                    ),
                    nt,
                    preferred_element_type=F32,
                )
                at = ((i & 1) * own_part + u * 4 + (i >> 1) + 2) * OWN_PITCH
                sums[pl.ds(at, 24), 0:HALF] = got[0:24]
                ghost_sum = got[24:40] if i % 4 == 0 else ghost_sum + got[24:40]
                if i % 4 == 3:
                    at = ((i >> 2) * ghost_part + u + 1) * GHOST_PITCH
                    ghost_sums[pl.ds(at, 16), 0:HALF] = ghost_sum

        def two(k, carry):
            contacts(2 * k, 0)
            contacts(2 * k + 1, 16)
            return carry

        lax.fori_loop(0, tiles // 16, two, 0, unroll=2)
        for par in range(2):
            base = par * ghost_part * GHOST_PITCH
            ghost_sums[base : base + GHOST_PITCH, :] = ghost_sums[
                base + ghost_rows * GHOST_PITCH : base + (ghost_rows + 1) * GHOST_PITCH, :
            ]
            base = par * own_part * OWN_PITCH
            sums[base : base + 2 * OWN_PITCH, :] = sums[
                base + own_rows * OWN_PITCH : base + (own_rows + 2) * OWN_PITCH, :
            ]
        first_half = lax.broadcasted_iota(jnp.int32, (8, LANES), 1) < HALF

        def gather_halves(ref, part_rows, pitch, pad, r, terms):
            halves = []
            for par in range(2):
                total = None
                for h, row in terms:
                    for s in range(2):
                        block = par - h
                        first = ((block & 1) * part_rows + r + (block >> 1) + pad) * pitch + row + s
                        got = ref[pl.ds(first, 8, stride=pitch), :]
                        total = got if total is None else total + got
                halves.append(total)
            return jnp.where(first_half, halves[0], pltpu.roll(halves[1], HALF, 1))

        for c in range(3):
            for r in range(0, ghost_rows, 8):
                terms = [(h, h * 6 + c * 2) for h in range(2)]
                total = gather_halves(ghost_sums, ghost_part, GHOST_PITCH, 1, r, terms)
                for i in range(0, 8, side_rows):
                    for slot, group in enumerate(ORDER):
                        if group == (r + i) // side_rows:
                            sum_out[sweep, slot, c * side_rows : (c + 1) * side_rows, :] = total[
                                i : i + side_rows
                            ]
        flying = exchange(
            1 + 2 * sweep,
            lambda g: sum_out.at[sweep, ORDER.index(g)],
            lambda g: sum_in.at[sweep, g],
        )
        distant = {}
        if sweep < SWEEPS - 1:
            for k in others[4:]:
                dx, dy = AROUND[k]
                back = AROUND.index((-dx, -dy))
                count = 1 if k < 8 else 2
                distant[back] = pltpu.make_async_remote_copy(
                    src_ref=sum_out.at[sweep, pl.ds(FIRST[dx, dy], count)],
                    dst_ref=far_in.at[sweep, back - 4, pl.ds(0, count)],
                    send_sem=far_send.at[sweep, k - 4],
                    recv_sem=far_recv.at[sweep, back - 4],
                    device_id=reach(dx, dy),
                    device_id_type=pl.DeviceIdType.MESH,
                )
            for copy in distant.values():
                copy.start()
        own_total = []
        for c in range(3):
            parts = []
            for r in range(0, own_rows, 8):
                terms = [(h, h * 6 + c * 2) for h in range(4)]
                parts.append(gather_halves(sums, own_part, OWN_PITCH, 2, r, terms))
            own_total.append(jnp.concatenate(parts, axis=0))
        mass = mass_ref[...]
        for c in range(3):
            rows = slice(c * own_rows, (c + 1) * own_rows)
            part_s[rows, :] = free_s[rows, :] + mass * own_total[c]
        if sweep < SWEEPS - 1:
            got = pick(lambda c, r: spread_row(part_s, c * own_rows + r), (F32,) * 3, 4)
            for c in range(3):
                ghost_out[sweep, c * side_rows : (c + 1) * side_rows, :] = got[c]
            bases = exchange(
                2 + 2 * sweep, lambda g: ghost_out.at[sweep], lambda g: ghost_in.at[sweep, g]
            )
            if sweep == 0:
                for g in range(4):
                    list_in = grain_in[g, 6 * side_rows : 7 * side_rows, :]
                    for a in range(side_rows):
                        down = jnp.broadcast_to(list_in[a : a + 1], (LANES, LANES)).T
                        for b in range(side_rows):
                            same[g, b, a * LANES : (a + 1) * LANES, :] = jnp.where(
                                down == list_in[b : b + 1], 1.0, 0.0
                            ).astype(BF16)
        if sweep == SWEEPS - 1:

            def unstage(t, carry):
                cols = pl.ds(pl.multiple_of(t * LANES, LANES), LANES)
                start_ref[:, cols] = stage[pl.ds(t * STAGE + 32, 3), :]
                return carry

            lax.fori_loop(0, tiles, unstage, 0, unroll=8)
            imp_store = pltpu.make_async_copy(start_ref, out_imp, load_sem.at[0])
            imp_store.start()
        finish(flying)
        received = (
            sum_in[sweep, 0] + sum_in[sweep, 1] + sum_in[sweep, 2] + sum_in[sweep, 3]
        )
        high = received.astype(BF16).astype(F32)
        low = received - high
        for c in range(3):
            total = None
            for term in (high, low):
                row = jnp.concatenate(
                    [
                        bound_row[:, q * LANES : (q + 1) * LANES]
                        * jnp.broadcast_to(
                            term[c * side_rows + q : c * side_rows + q + 1], (own_rows, LANES)
                        ).astype(BF16)
                        for q in range(side_rows)
                    ],
                    axis=1,
                )
                got = lax.dot_general(row, bound_hot[...], nt, preferred_element_type=F32)
                total = got if total is None else total + got
            current = part_s[c * own_rows : (c + 1) * own_rows, :] + mass * total
            if sweep < SWEEPS - 1:
                spread_current(c, current)
            else:
                vel_s[pl.ds(c, own_rows, stride=3), :] = current
        if sweep < SWEEPS - 1:
            for copy in distant.values():
                copy.wait_recv()
            sent.extend(distant.values())

            def sum_of(dx, dy, group):
                if dx % nx == 0 and dy % ny == 0:
                    return sum_out[sweep, ORDER.index(group)]
                at = AROUND.index((dx, dy)) - 4
                return far_in[sweep, at, int(ORDER[FIRST[-dx, -dy]] != group)]

            for g in range(4):
                total = None
                for d in range(4):
                    dx, dy = NEAR[g][0] + NEAR[d][0], NEAR[g][1] + NEAR[d][1]
                    got = sum_of(dx, dy, d ^ 1)
                    total = got if total is None else total + got
                high = total.astype(BF16).astype(F32)
                split[g, 0 : 3 * side_rows, :] = high
                split[g, 3 * side_rows : 6 * side_rows, :] = total - high
                rows = jnp.concatenate(
                    [split[g, pl.ds(q, 16, stride=side_rows), :] for q in range(side_rows)], axis=1
                ).astype(BF16)
                got = jnp.dot(
                    rows,
                    jnp.concatenate([same[g, q] for q in range(side_rows)], axis=1),
                    preferred_element_type=F32,
                )
                for q in range(side_rows):
                    joined[g, q * 9 : q * 9 + 8, :] = got[0:8, q * LANES : (q + 1) * LANES]
            finish(bases)
            for c in range(3):
                ghosts = []
                for g in range(4):
                    more = (
                        joined[g, pl.ds(c, side_rows, stride=9), :]
                        + joined[g, pl.ds(3 + c, side_rows, stride=9), :]
                    )
                    ghosts.append(
                        ghost_in[sweep, g, c * side_rows : (c + 1) * side_rows, :]
                        + grain_in[g, 5 * side_rows : 6 * side_rows, :] * more
                    )
                spread_halves(ghost_s, c * gpad, jnp.concatenate(ghosts, axis=0))

    def unstage_grain(t, carry):
        cols = pl.ds(pl.multiple_of(t * LANES, LANES), LANES)
        vel_ref[:, cols] = vel_s[pl.ds(t * 3, 3), :]
        return carry

    lax.fori_loop(0, own_rows, unstage_grain, 0, unroll=8)
    vel_store = pltpu.make_async_copy(vel_ref, out_vel, load_sem.at[1])
    vel_store.start()
    for copy in sent:
        copy.wait_send()
    imp_store.wait()
    vel_store.wait()


def hand_on(vel_in, imp_in, vel_out, imp_out, vel_ref, imp_ref, sem):
    pairs = ((imp_in, imp_ref, imp_out), (vel_in, vel_ref, vel_out))
    loads = [pltpu.make_async_copy(x, y, sem.at[0, k]) for k, (x, y, _) in enumerate(pairs)]
    stores = [pltpu.make_async_copy(y, z, sem.at[1, k]) for k, (_, y, z) in enumerate(pairs)]
    for load in loads:
        load.start()
    for load, store in zip(loads, stores):
        load.wait()
        store.start()
    for store in stores:
        store.wait()


def solution(mesh):
    sizes = (mesh.shape["gx"], mesh.shape["gy"])

    def local(
        velocity, inv_mass, drag, grain_cell, boundary_list, contact_pair, frames, blocks,
        impulse_start, gap, contact_mask, pressure,
    ):
        own_rows = velocity.shape[1] // LANES
        tiles = contact_pair.shape[1] // LANES
        side_rows = boundary_list.shape[0] // LANES
        cell_rows = pressure.size // LANES
        gpad = 8 * side_rows
        rounds = 2 * SWEEPS
        out_vel, out_imp = pl.pallas_call(
            lambda *refs: step_kernel(sizes, *refs),
            out_shape=(
                jax.ShapeDtypeStruct(velocity.shape, F32),
                jax.ShapeDtypeStruct(impulse_start.shape, F32),
            ),
            in_specs=[pl.BlockSpec(memory_space=pltpu.HBM)] * 12,
            out_specs=(pl.BlockSpec(memory_space=pltpu.HBM),) * 2,
            scratch_shapes=[
                pltpu.VMEM((3, velocity.shape[1]), F32),
                pltpu.VMEM((own_rows, LANES), F32),
                pltpu.VMEM((own_rows, LANES), F32),
                pltpu.VMEM((own_rows, LANES), jnp.int32),
                pltpu.VMEM((side_rows, LANES), jnp.int32),
                pltpu.VMEM((2, contact_pair.shape[1]), jnp.int32),
                pltpu.VMEM((9, contact_pair.shape[1]), F32),
                pltpu.VMEM((9, contact_pair.shape[1]), F32),
                pltpu.VMEM((3, contact_pair.shape[1]), F32),
                pltpu.VMEM((3, contact_pair.shape[1]), F32),
                pltpu.VMEM((tiles, LANES), jnp.int32),
                pltpu.VMEM(pressure.shape, F32),
                pltpu.VMEM((pressure.size // pressure.shape[2], LANES), F32),
                pltpu.VMEM((cell_rows, LANES), F32),
                pltpu.VMEM((12, cell_rows, LANES), F32),
                pltpu.VMEM((4, 7 * side_rows, LANES), F32),
                pltpu.VMEM((7 * side_rows, LANES), F32),
                pltpu.VMEM((SWEEPS - 1, 4, 3 * side_rows, LANES), F32),
                pltpu.VMEM((SWEEPS, 4, 3 * side_rows, LANES), F32),
                pltpu.VMEM((SWEEPS - 1, 8, 2, 3 * side_rows, LANES), F32),
                pltpu.VMEM((SWEEPS - 1, 3 * side_rows, LANES), F32),
                pltpu.VMEM((SWEEPS, 5, 3 * side_rows, LANES), F32),
                pltpu.VMEM((3 * cell_rows, LANES), F32),
                pltpu.VMEM((12 * cell_rows, LANES), F32),
                pltpu.VMEM((own_rows * 3, LANES), F32),
                pltpu.VMEM((3 * own_rows, LANES), F32),
                pltpu.VMEM((tiles * STAGE, LANES), F32),
                pltpu.VMEM((tiles * 3, LANES), jnp.int32),
                pltpu.VMEM((2 * tiles, LANES), jnp.int32),
                pltpu.VMEM((2 * tiles, LANES), jnp.int32),
                pltpu.VMEM((2 * tiles, LANES), F32),
                pltpu.VMEM((tiles, LANES, LANES), BF16),
                pltpu.VMEM((3 * (2 * own_rows + 8), LANES), F32),
                pltpu.VMEM((3 * gpad, LANES), F32),
                pltpu.VMEM((32 * PITCH, LANES), F32),
                pltpu.VMEM((2 * (own_rows + 2) * OWN_PITCH, LANES), F32),
                pltpu.VMEM((2 * (4 * side_rows + 1) * GHOST_PITCH, LANES), F32),
                pltpu.VMEM((LANES, side_rows * LANES), BF16),
                pltpu.VMEM((own_rows, side_rows * LANES), BF16),
                pltpu.VMEM((3 * own_rows, LANES), F32),
                pltpu.VMEM((4, side_rows, side_rows * LANES, LANES), BF16),
                pltpu.VMEM((4, 16 * side_rows, LANES), F32),
                pltpu.VMEM((4, 9 * side_rows, LANES), F32),
                pltpu.SemaphoreType.DMA((rounds, 4)),
                pltpu.SemaphoreType.DMA((rounds, 4)),
                pltpu.SemaphoreType.DMA((12,)),
                pltpu.SemaphoreType.DMA((12,)),
                pltpu.SemaphoreType.DMA((SWEEPS - 1, 8)),
                pltpu.SemaphoreType.DMA((SWEEPS - 1, 8)),
                pltpu.SemaphoreType.DMA((12,)),
            ],
            compiler_params=pltpu.CompilerParams(
                collective_id=0, has_side_effects=True, vmem_limit_bytes=62 * 1024 * 1024
            ),
        )(
            velocity,
            inv_mass.reshape(own_rows, LANES),
            drag.reshape(own_rows, LANES),
            grain_cell.reshape(own_rows, LANES),
            boundary_list.reshape(side_rows, LANES),
            contact_pair,
            frames,
            blocks,
            impulse_start,
            gap,
            contact_mask.reshape(tiles, LANES),
            pressure,
        )
        return pl.pallas_call(
            hand_on,
            out_shape=(
                jax.ShapeDtypeStruct(velocity.shape, F32),
                jax.ShapeDtypeStruct(impulse_start.shape, F32),
            ),
            in_specs=[pl.BlockSpec(memory_space=pltpu.HBM)] * 2,
            out_specs=(pl.BlockSpec(memory_space=pltpu.HBM),) * 2,
            scratch_shapes=[
                pltpu.VMEM(velocity.shape, F32),
                pltpu.VMEM(impulse_start.shape, F32),
                pltpu.SemaphoreType.DMA((2, 2)),
            ],
        )(out_vel, out_imp)

    grains, lists = P(("gx", "gy")), P(None, ("gx", "gy"))
    return jax.shard_map(
        local,
        mesh=mesh,
        in_specs=(
            lists, grains, grains, grains, grains, lists, lists, lists, lists, lists, grains,
            P(None, "gx", "gy"),
        ),
        out_specs=(lists, lists),
        check_vma=False,
    )
```

```python
import jax
import jax.numpy as jnp
from jax import lax
from jax.experimental import pallas as pl
from jax.experimental.pallas import tpu as pltpu
from jax.sharding import PartitionSpec as P

SWEEPS = 2
TIME_STEP = 0.5
FRICTION = 0.5
FLOOR_VALUE = 0.1
LANES = 128
HALF = LANES // 2
ROWS = 48
PITCH = 49
STAGE = 49
OWN_PITCH = 25
GHOST_PITCH = 17
F32 = jnp.float32
BF16 = jnp.bfloat16
NEAR = ((-1, 0), (1, 0), (0, -1), (0, 1))
FAR = ((-2, 0), (2, 0), (0, -2), (0, 2), (-1, -1), (-1, 1), (1, -1), (1, 1))
AROUND = NEAR + FAR
ORDER = (0, 2, 1, 3, 0)
FIRST = {(-1, -1): 0, (1, -1): 1, (1, 1): 2, (-1, 1): 3, (-2, 0): 0, (0, -2): 1, (2, 0): 2, (0, 2): 3}


def take_lanes(values, lanes):
    return jnp.take_along_axis(values, lanes, axis=1, mode="promise_in_bounds")


def spread_row(ref, row):
    return jnp.broadcast_to(ref[pl.ds(row, 1), :], (8, LANES))


def step_kernel(
    sizes,
    vel_hbm, mass_hbm, drag_hbm, cell_hbm, bound_hbm, pair_hbm, frame_hbm, block_hbm,
    start_hbm, gap_hbm, mask_hbm, pres_hbm,
    out_vel, out_imp,
    vel_ref, mass_ref, drag_ref, cell_ref, bound_ref, pair_ref, frame_ref, block_ref,
    start_ref, gap_ref, mask_ref, pres_raw, pres_wide, pres_ref,
    pres_in, grain_in, grain_out, ghost_in, sum_in, far_in, ghost_out, sum_out,
    slope_s, slope_n, vel_s, free_s, stage, ends, codes, lanes_s, spots, table, ext, ghost_s,
    left, sums, ghost_sums, bound_hot, bound_row, part_s, same, split, joined,
    send_sem, recv_sem, pres_send, pres_recv, far_send, far_recv, load_sem,
):
    nx, ny = sizes
    tiles = mask_ref.shape[0]
    own_rows = mass_ref.shape[0]
    side_rows = bound_ref.shape[0]
    ghost_rows = 4 * side_rows
    cell_rows = pres_ref.shape[0]
    ext_rows = 2 * own_rows + 8
    gpad = 2 * ghost_rows
    own_slots = own_rows * LANES
    ghost_slots = ghost_rows * LANES
    own_part = own_rows + 2
    ghost_part = ghost_rows + 1
    row_iota = lax.broadcasted_iota(jnp.int32, (8, LANES), 0)

    mx, my = lax.axis_index("gx"), lax.axis_index("gy")
    reach = lambda dx, dy: (lax.rem(mx + dx + 2 * nx, nx), lax.rem(my + dy + 2 * ny, ny))
    sides = [reach(dx, dy) for dx, dy in NEAR]
    others = [k for k, (dx, dy) in enumerate(AROUND) if dx % nx or dy % ny]

    loads = [
        pltpu.make_async_copy(source, target, load_sem.at[k])
        for k, (source, target) in enumerate(
            (
                (vel_hbm, vel_ref), (bound_hbm, bound_ref), (drag_hbm, drag_ref),
                (mass_hbm, mass_ref), (cell_hbm, cell_ref), (pair_hbm, pair_ref),
                (mask_hbm, mask_ref), (start_hbm, start_ref), (gap_hbm, gap_ref),
                (frame_hbm, frame_ref), (block_hbm, block_ref),
            )
        )
    ]
    pres_load = pltpu.make_async_copy(pres_hbm, pres_raw, load_sem.at[11])
    pres_load.start()
    for load in loads:
        load.start()

    barrier = pltpu.get_barrier_semaphore()
    for k in others:
        pl.semaphore_signal(
            barrier, inc=1, device_id=reach(*AROUND[k]), device_id_type=pl.DeviceIdType.MESH
        )

    lane = lax.broadcasted_iota(jnp.int32, (cell_rows, LANES), 1)
    pres_load.wait()
    width = pres_raw.shape[2]
    pres_wide[:, 0:width] = pres_raw[...].reshape(-1, width)
    per_row = LANES // width
    p = pres_wide[pl.ds(0, cell_rows, stride=per_row), :]
    for k in range(1, per_row):
        piece = pltpu.roll(pres_wide[pl.ds(k, cell_rows, stride=per_row), :], k * width, 1)
        p = jnp.where(lane < k * width, p, piece)
    pres_ref[...] = p
    def exchange(step, source, target):
        copies = []
        for g in range(4):
            copies.append(
                pltpu.make_async_remote_copy(
                    src_ref=source(g),
                    dst_ref=target(g ^ 1),
                    send_sem=send_sem.at[step, g],
                    recv_sem=recv_sem.at[step, g ^ 1],
                    device_id=sides[g],
                    device_id_type=pl.DeviceIdType.MESH,
                )
            )
        for copy in copies:
            copy.start()
        return copies

    sent = []

    def finish(copies):
        for copy in copies:
            copy.wait_recv()
        sent.extend(copies)

    for load in loads[:5]:
        load.wait()
    bound_all = bound_ref[...]
    bound_lane = bound_all & (LANES - 1)
    bound_at = bound_all >> 7
    two_lane = jnp.concatenate([bound_lane, bound_lane], axis=0)
    two_at = jnp.concatenate([bound_at, bound_at], axis=0)
    half = own_rows // 2
    upper = row_iota < side_rows
    low_at = two_at < half

    def pick(row_of, kinds, unroll):
        def body(k, acc):
            acc = list(acc)
            for i in range(4):
                r = k * 4 + i
                hit = two_at == jnp.where(upper, r, r + half)
                for c in range(len(kinds)):
                    got = take_lanes(jnp.where(upper, row_of(c, r), row_of(c, r + half)), two_lane)
                    acc[c] = jnp.where(hit, got, acc[c])
            return tuple(acc)

        start = tuple(jnp.zeros((8, LANES), kind) for kind in kinds)
        acc = lax.fori_loop(0, half // 4, body, start, unroll=unroll)
        return [
            jnp.where(low_at[:side_rows], got[:side_rows], got[side_rows:]) for got in acc
        ]

    def grain_row(c, r):
        if c < 3:
            cols = pl.ds(pl.multiple_of(r * LANES, LANES), LANES)
            return jnp.broadcast_to(vel_ref[pl.ds(c, 1), cols], (8, LANES))
        return spread_row((drag_ref, mass_ref, cell_ref)[c - 3], r)

    *moving, drag_b, mass_b, cell_b = pick(grain_row, (F32,) * 5 + (jnp.int32,), 2)
    below = 1.0 + TIME_STEP * drag_b
    for c in range(3):
        grain_out[c * side_rows : (c + 1) * side_rows, :] = moving[c] / below
    grain_out[3 * side_rows : 4 * side_rows, :] = TIME_STEP * (drag_b + mass_b) / below
    grain_out[4 * side_rows : 5 * side_rows, :] = cell_b.astype(F32)
    grain_out[5 * side_rows : 6 * side_rows, :] = mass_b
    grain_out[6 * side_rows : 7 * side_rows, :] = bound_all.astype(F32)
    pl.semaphore_wait(barrier, len(others))
    spreading = {}
    for k in others:
        dx, dy = AROUND[k]
        back = AROUND.index((-dx, -dy))
        spreading[back] = pltpu.make_async_remote_copy(
            src_ref=pres_ref,
            dst_ref=pres_in.at[back],
            send_sem=pres_send.at[k],
            recv_sem=pres_recv.at[back],
            device_id=reach(dx, dy),
            device_id_type=pl.DeviceIdType.MESH,
        )
    for copy in spreading.values():
        copy.start()
    flying = exchange(0, lambda g: grain_out, lambda g: grain_in.at[g])
    for load in loads[5:]:
        load.wait()

    def stage_tile(t, carry):
        cols = pl.ds(pl.multiple_of(t * LANES, LANES), LANES)
        base = t * STAGE
        stage[pl.ds(base, 9), :] = frame_ref[:, cols]
        stage[pl.ds(base + 16, 9), :] = block_ref[:, cols]
        stage[pl.ds(base + 32, 3), :] = start_ref[:, cols]
        stage[pl.ds(base + 40, 3), :] = gap_ref[:, cols]
        ends[pl.ds(t * 3, 2), :] = pair_ref[:, cols]
        return carry

    lax.fori_loop(0, tiles, stage_tile, 0, unroll=4)

    def stage_grain(t, carry):
        cols = pl.ds(pl.multiple_of(t * LANES, LANES), LANES)
        vel_s[pl.ds(t * 3, 3), :] = vel_ref[:, cols]
        return carry

    lax.fori_loop(0, own_rows, stage_grain, 0, unroll=4)

    def place(u, carry):
        tile = u * 8 + row_iota
        for e in range(2):
            slot = ends[pl.ds(u * 24 + 1 - e, 8, stride=3), :]
            own = slot < own_slots
            near = (slot - HALF * tile) & (own_slots - 1)
            far = (slot - own_slots - HALF * (tile >> 2)) & (ghost_slots - 1)
            rel = jnp.where(own, near, far)
            at = pl.ds(pl.multiple_of(e * tiles + u * 8, 8), 8)
            codes[at, :] = jnp.where(own, 0, 4) + (rel >> 6)
            lanes_s[at, :] = rel & (LANES - 1)
            spots[at, :] = (rel & (HALF - 1)).astype(F32)
        return carry

    lax.fori_loop(0, tiles // 8, place, 0, unroll=2)

    hot_iota = lax.broadcasted_iota(jnp.int32, (LANES, LANES), 0)
    row_hot = lax.broadcasted_iota(jnp.int32, (own_rows, LANES), 0)
    for q in range(side_rows):
        cols = slice(q * LANES, (q + 1) * LANES)
        bound_hot[:, cols] = jnp.where(hot_iota == bound_lane[q : q + 1], 1.0, 0.0).astype(BF16)
        bound_row[:, cols] = jnp.where(row_hot == bound_at[q : q + 1], 1.0, 0.0).astype(BF16)

    def spread_halves(ref, first, value):
        rows = value.shape[0]
        turned = pltpu.roll(value, HALF, 1)
        after = jnp.concatenate([turned[1:], turned[:1]], axis=0)
        first_half = lax.broadcasted_iota(jnp.int32, value.shape, 1) < HALF
        ref[pl.ds(first, rows, stride=2), :] = value
        ref[pl.ds(first + 1, rows, stride=2), :] = jnp.where(first_half, turned, after)

    def spread_current(c, value):
        spread_halves(ext, c * ext_rows, value)
        ext[pl.ds(c * ext_rows + 2 * own_rows, 8), :] = ext[pl.ds(c * ext_rows, 8), :]

    iotas = [
        (lax.broadcasted_iota(jnp.int32, (16, LANES), 0) + 16 * q).astype(F32).astype(BF16)
        for q in range(HALF // 16)
    ]
    signs = [jnp.full((16, LANES), sign, BF16) for sign in (1.0, -1.0)]
    zero16 = jnp.zeros((16, LANES), BF16)

    def build(t, carry):
        for e in range(2):
            row = jnp.broadcast_to(spots[pl.ds(e * tiles + t, 1), :], (16, LANES)).astype(BF16)
            for q in range(HALF // 16):
                at = slice(e * HALF + 16 * q, e * HALF + 16 * (q + 1))
                table[t, at, :] = jnp.where(iotas[q] == row, signs[e], zero16)
        return carry

    lax.fori_loop(0, tiles, build, 0, unroll=4)
    for i in range(32):
        left[i * PITCH + 36 : i * PITCH + ROWS, :] = jnp.zeros((12, LANES), F32)

    for k in range(4):
        spreading[k].wait_recv()
    even = (lax.broadcasted_iota(jnp.int32, (cell_rows, LANES), 0) & 1) == 0
    up1 = lambda a: jnp.concatenate([a[1:], a[:1]], axis=0)
    down1 = lambda a: jnp.concatenate([a[-1:], a[:-1]], axis=0)
    turn = lambda a, n: pltpu.roll(a, n % LANES, 1)
    none = jnp.zeros((2, LANES), F32)

    def pres_at(dx, dy):
        if dx % nx == 0 and dy % ny == 0:
            return p
        return pres_in[AROUND.index((dx, dy))]

    def slopes(ref, first, dx, dy):
        mid = pres_at(dx, dy)
        prev_x, next_x = pres_at(dx - 1, dy), pres_at(dx + 1, dy)
        prev_y, next_y = pres_at(dx, dy - 1), pres_at(dx, dy + 1)
        after = turn(mid, -16)
        plus = jnp.where(lane < 112, after, jnp.where(even, up1(after), down1(turn(next_x, -16))))
        before = turn(mid, 16)
        minus = jnp.where(lane >= 16, before, jnp.where(even, up1(turn(prev_x, 16)), down1(before)))
        ref[first : first + cell_rows] = (plus - minus) * 0.5
        plus = jnp.where((lane & 15) < 15, turn(mid, -1), turn(next_y, 15))
        minus = jnp.where((lane & 15) > 0, turn(mid, 1), turn(prev_y, -15))
        ref[first + cell_rows : first + 2 * cell_rows] = (plus - minus) * 0.5
        ref[first + 2 * cell_rows : first + 3 * cell_rows] = (
            jnp.concatenate([mid[2:], none], axis=0) - jnp.concatenate([none, mid[:-2]], axis=0)
        ) * 0.5

    slopes(slope_s, 0, 0, 0)

    def free(k, carry):
        at = pl.ds(pl.multiple_of(k * 8, 8), 8)
        cells = cell_ref[at, :]
        cell_at, cell_lane = cells >> 7, cells & (LANES - 1)
        drag, mass = drag_ref[at, :], mass_ref[at, :]
        for c in range(3):
            slope = jnp.zeros((8, LANES), F32)
            for r in range(cell_rows):
                got = take_lanes(spread_row(slope_s, c * cell_rows + r), cell_lane)
                slope = jnp.where(cell_at == r, got, slope)
            v = vel_s[pl.ds(k * 24 + c, 8, stride=3), :]
            free_s[pl.ds(pl.multiple_of(c * own_rows + k * 8, 8), 8), :] = (
                v - TIME_STEP * (drag + mass) * slope
            ) / (1.0 + TIME_STEP * drag)
        return carry

    lax.fori_loop(0, own_rows // 8, free, 0, unroll=2)
    for c in range(3):
        spread_current(c, free_s[c * own_rows : (c + 1) * own_rows, :])
    for k in others[4:]:
        spreading[k].wait_recv()
    sent.extend(spreading.values())
    finish(flying)
    for g in range(4):
        slopes(slope_n, 3 * cell_rows * g, *NEAR[g])
    ghost_free = [[], [], []]
    for g in (0, 2):
        both = [
            jnp.concatenate(
                [grain_in[g + i, k * side_rows : (k + 1) * side_rows, :] for i in range(2)], axis=0
            )
            for k in range(5)
        ]
        cells = both[4].astype(jnp.int32)
        cell_at, cell_lane = cells >> 7, cells & (LANES - 1)
        for c in range(3):
            slope = jnp.zeros((8, LANES), F32)
            for r in range(cell_rows):
                first = (3 * g + c) * cell_rows + r
                row = jnp.where(
                    row_iota < side_rows,
                    spread_row(slope_n, first),
                    spread_row(slope_n, first + 3 * cell_rows),
                )
                slope = jnp.where(cell_at == r, take_lanes(row, cell_lane), slope)
            ghost_free[c].append(both[c] - both[3] * slope)
    for c in range(3):
        spread_halves(ghost_s, c * gpad, jnp.concatenate(ghost_free[c], axis=0))

    split[...] = jnp.zeros(split.shape, F32)
    nt = (((1,), (1,)), ((), ()))
    for sweep in range(SWEEPS):
        def contacts(u, odd):
            at = pl.ds(pl.multiple_of(u * 8, 8), 8)
            code, lanes = [], []
            for e in range(2):
                end_at = pl.ds(pl.multiple_of(e * tiles + u * 8, 8), 8)
                code.append(codes[end_at, :])
                lanes.append(lanes_s[end_at, :])
            relative = []
            for c in range(3):
                near = ext[pl.ds(c * ext_rows + u * 8, 8), :]
                next_ = ext[pl.ds(c * ext_rows + u * 8 + 2, 8), :]
                far = jnp.where(
                    row_iota < 4,
                    spread_row(ghost_s, c * gpad + 2 * u),
                    spread_row(ghost_s, c * gpad + 2 * u + 1),
                )
                ends_val = []
                for e in range(2):
                    val = jnp.where(
                        code[e] < 4, take_lanes(next_, lanes[e]), take_lanes(far, lanes[e])
                    )
                    ends_val.append(jnp.where(code[e] < 2, take_lanes(near, lanes[e]), val))
                relative.append(ends_val[0] - ends_val[1])
            part = lambda k: stage[pl.ds(u * (8 * STAGE) + k, 8, stride=STAGE), :]
            fr = [part(k) for k in range(9)]
            target = [
                fr[3 * m] * relative[0]
                + fr[3 * m + 1] * relative[1]
                + fr[3 * m + 2] * relative[2]
                + part(40 + m)
                for m in range(3)
            ]
            trial = []
            for k in range(3):
                before = part(32 + k)
                trial.append(
                    before
                    - (
                        part(16 + 3 * k) * target[0]
                        + part(17 + 3 * k) * target[1]
                        + part(18 + 3 * k) * target[2]
                    )
                )
            active = mask_ref[at, :].astype(F32)
            normal = jnp.maximum(trial[0], 0.0)
            tangent = jnp.sqrt(trial[1] * trial[1] + trial[2] * trial[2])
            factor = jnp.minimum(1.0, FRICTION * normal / jnp.maximum(tangent, FLOOR_VALUE))
            imp = [normal * active, factor * trial[1] * active, factor * trial[2] * active]
            for k in range(3):
                stage[pl.ds(u * (8 * STAGE) + 32 + k, 8, stride=STAGE), :] = imp[k]
            for c in range(3):
                push = fr[c] * imp[0] + fr[3 + c] * imp[1] + fr[6 + c] * imp[2]
                high = push.astype(BF16).astype(F32)
                for s, term in enumerate((high, push - high)):
                    for e in range(2):
                        for h in range(6):
                            left[
                                pl.ds((e * 8 + odd) * PITCH + (h * 3 + c) * 2 + s, 8, stride=PITCH), :
                            ] = jnp.where(code[e] == h, term, 0.0)
            ghost_sum = None
            for i in range(8):
                got = lax.dot_general(
                    jnp.concatenate(
                        [
                            left[(odd + i) * PITCH : (odd + i) * PITCH + ROWS, :].astype(BF16),
                            left[(odd + i + 8) * PITCH : (odd + i + 8) * PITCH + ROWS, :].astype(BF16),
                        ],
                        axis=1,
                    ),
                    jnp.concatenate(
                        [
                            table[u * 8 + i, e * HALF : (e + 1) * HALF, :]
                            for e in range(2)
                        ],
                        axis=1,
                    ),
                    nt,
                    preferred_element_type=F32,
                )
                at = ((i & 1) * own_part + u * 4 + (i >> 1) + 2) * OWN_PITCH
                sums[pl.ds(at, 24), 0:HALF] = got[0:24]
                ghost_sum = got[24:40] if i % 4 == 0 else ghost_sum + got[24:40]
                if i % 4 == 3:
                    at = ((i >> 2) * ghost_part + u + 1) * GHOST_PITCH
                    ghost_sums[pl.ds(at, 16), 0:HALF] = ghost_sum

        def two(k, carry):
            contacts(2 * k, 0)
            contacts(2 * k + 1, 16)
            return carry

        lax.fori_loop(0, tiles // 16, two, 0, unroll=2)
        for par in range(2):
            base = par * ghost_part * GHOST_PITCH
            ghost_sums[base : base + GHOST_PITCH, :] = ghost_sums[
                base + ghost_rows * GHOST_PITCH : base + (ghost_rows + 1) * GHOST_PITCH, :
            ]
            base = par * own_part * OWN_PITCH
            sums[base : base + 2 * OWN_PITCH, :] = sums[
                base + own_rows * OWN_PITCH : base + (own_rows + 2) * OWN_PITCH, :
            ]
        first_half = lax.broadcasted_iota(jnp.int32, (8, LANES), 1) < HALF

        def gather_halves(ref, part_rows, pitch, pad, r, terms):
            halves = []
            for par in range(2):
                total = None
                for h, row in terms:
                    for s in range(2):
                        block = par - h
                        first = ((block & 1) * part_rows + r + (block >> 1) + pad) * pitch + row + s
                        got = ref[pl.ds(first, 8, stride=pitch), :]
                        total = got if total is None else total + got
                halves.append(total)
            return jnp.where(first_half, halves[0], pltpu.roll(halves[1], HALF, 1))

        for c in range(3):
            for r in range(0, ghost_rows, 8):
                terms = [(h, h * 6 + c * 2) for h in range(2)]
                total = gather_halves(ghost_sums, ghost_part, GHOST_PITCH, 1, r, terms)
                for i in range(0, 8, side_rows):
                    for slot, group in enumerate(ORDER):
                        if group == (r + i) // side_rows:
                            sum_out[sweep, slot, c * side_rows : (c + 1) * side_rows, :] = total[
                                i : i + side_rows
                            ]
        flying = exchange(
            1 + 2 * sweep,
            lambda g: sum_out.at[sweep, ORDER.index(g)],
            lambda g: sum_in.at[sweep, g],
        )
        distant = {}
        if sweep < SWEEPS - 1:
            for k in others[4:]:
                dx, dy = AROUND[k]
                back = AROUND.index((-dx, -dy))
                count = 1 if k < 8 else 2
                distant[back] = pltpu.make_async_remote_copy(
                    src_ref=sum_out.at[sweep, pl.ds(FIRST[dx, dy], count)],
                    dst_ref=far_in.at[sweep, back - 4, pl.ds(0, count)],
                    send_sem=far_send.at[sweep, k - 4],
                    recv_sem=far_recv.at[sweep, back - 4],
                    device_id=reach(dx, dy),
                    device_id_type=pl.DeviceIdType.MESH,
                )
            for copy in distant.values():
                copy.start()
        own_total = []
        for c in range(3):
            parts = []
            for r in range(0, own_rows, 8):
                terms = [(h, h * 6 + c * 2) for h in range(4)]
                parts.append(gather_halves(sums, own_part, OWN_PITCH, 2, r, terms))
            own_total.append(jnp.concatenate(parts, axis=0))
        mass = mass_ref[...]
        for c in range(3):
            rows = slice(c * own_rows, (c + 1) * own_rows)
            part_s[rows, :] = free_s[rows, :] + mass * own_total[c]
        if sweep < SWEEPS - 1:
            got = pick(lambda c, r: spread_row(part_s, c * own_rows + r), (F32,) * 3, 4)
            for c in range(3):
                ghost_out[sweep, c * side_rows : (c + 1) * side_rows, :] = got[c]
            bases = exchange(
                2 + 2 * sweep, lambda g: ghost_out.at[sweep], lambda g: ghost_in.at[sweep, g]
            )
            if sweep == 0:
                for g in range(4):
                    list_in = grain_in[g, 6 * side_rows : 7 * side_rows, :]
                    for a in range(side_rows):
                        down = jnp.broadcast_to(list_in[a : a + 1], (LANES, LANES)).T
                        for b in range(side_rows):
                            same[g, b, a * LANES : (a + 1) * LANES, :] = jnp.where(
                                down == list_in[b : b + 1], 1.0, 0.0
                            ).astype(BF16)
        if sweep == SWEEPS - 1:

            def unstage(t, carry):
                cols = pl.ds(pl.multiple_of(t * LANES, LANES), LANES)
                out_imp[:, cols] = stage[pl.ds(t * STAGE + 32, 3), :]
                return carry

            lax.fori_loop(0, tiles, unstage, 0, unroll=8)
        finish(flying)
        received = (
            sum_in[sweep, 0] + sum_in[sweep, 1] + sum_in[sweep, 2] + sum_in[sweep, 3]
        )
        high = received.astype(BF16).astype(F32)
        low = received - high
        for c in range(3):
            total = None
            for term in (high, low):
                row = jnp.concatenate(
                    [
                        bound_row[:, q * LANES : (q + 1) * LANES]
                        * jnp.broadcast_to(
                            term[c * side_rows + q : c * side_rows + q + 1], (own_rows, LANES)
                        ).astype(BF16)
                        for q in range(side_rows)
                    ],
                    axis=1,
                )
                got = lax.dot_general(row, bound_hot[...], nt, preferred_element_type=F32)
                total = got if total is None else total + got
            current = part_s[c * own_rows : (c + 1) * own_rows, :] + mass * total
            if sweep < SWEEPS - 1:
                spread_current(c, current)
            else:
                vel_s[pl.ds(c, own_rows, stride=3), :] = current
        if sweep < SWEEPS - 1:
            for copy in distant.values():
                copy.wait_recv()
            sent.extend(distant.values())

            def sum_of(dx, dy, group):
                if dx % nx == 0 and dy % ny == 0:
                    return sum_out[sweep, ORDER.index(group)]
                at = AROUND.index((dx, dy)) - 4
                return far_in[sweep, at, int(ORDER[FIRST[-dx, -dy]] != group)]

            for g in range(4):
                total = None
                for d in range(4):
                    dx, dy = NEAR[g][0] + NEAR[d][0], NEAR[g][1] + NEAR[d][1]
                    got = sum_of(dx, dy, d ^ 1)
                    total = got if total is None else total + got
                high = total.astype(BF16).astype(F32)
                split[g, 0 : 3 * side_rows, :] = high
                split[g, 3 * side_rows : 6 * side_rows, :] = total - high
                rows = jnp.concatenate(
                    [split[g, pl.ds(q, 16, stride=side_rows), :] for q in range(side_rows)], axis=1
                ).astype(BF16)
                got = jnp.dot(
                    rows,
                    jnp.concatenate([same[g, q] for q in range(side_rows)], axis=1),
                    preferred_element_type=F32,
                )
                for q in range(side_rows):
                    joined[g, q * 9 : q * 9 + 8, :] = got[0:8, q * LANES : (q + 1) * LANES]
            finish(bases)
            for c in range(3):
                ghosts = []
                for g in range(4):
                    more = (
                        joined[g, pl.ds(c, side_rows, stride=9), :]
                        + joined[g, pl.ds(3 + c, side_rows, stride=9), :]
                    )
                    ghosts.append(
                        ghost_in[sweep, g, c * side_rows : (c + 1) * side_rows, :]
                        + grain_in[g, 5 * side_rows : 6 * side_rows, :] * more
                    )
                spread_halves(ghost_s, c * gpad, jnp.concatenate(ghosts, axis=0))

    def unstage_grain(t, carry):
        cols = pl.ds(pl.multiple_of(t * LANES, LANES), LANES)
        out_vel[:, cols] = vel_s[pl.ds(t * 3, 3), :]
        return carry

    lax.fori_loop(0, own_rows, unstage_grain, 0, unroll=8)
    for copy in sent:
        copy.wait_send()


def hand_on(vel_in, imp_in, vel_out, imp_out, sem):
    copies = [
        pltpu.make_async_copy(imp_in, imp_out, sem.at[0]),
        pltpu.make_async_copy(vel_in, vel_out, sem.at[1]),
    ]
    for copy in copies:
        copy.start()
    for copy in copies:
        copy.wait()


def solution(mesh):
    sizes = (mesh.shape["gx"], mesh.shape["gy"])

    def local(
        velocity, inv_mass, drag, grain_cell, boundary_list, contact_pair, frames, blocks,
        impulse_start, gap, contact_mask, pressure,
    ):
        own_rows = velocity.shape[1] // LANES
        tiles = contact_pair.shape[1] // LANES
        side_rows = boundary_list.shape[0] // LANES
        cell_rows = pressure.size // LANES
        gpad = 8 * side_rows
        rounds = 2 * SWEEPS
        out_vel, out_imp = pl.pallas_call(
            lambda *refs: step_kernel(sizes, *refs),
            out_shape=(pltpu.VMEM(velocity.shape, F32), pltpu.VMEM(impulse_start.shape, F32)),
            in_specs=[pl.BlockSpec(memory_space=pltpu.HBM)] * 12,
            out_specs=(pl.BlockSpec(memory_space=pltpu.VMEM),) * 2,
            scratch_shapes=[
                pltpu.VMEM((3, velocity.shape[1]), F32),
                pltpu.VMEM((own_rows, LANES), F32),
                pltpu.VMEM((own_rows, LANES), F32),
                pltpu.VMEM((own_rows, LANES), jnp.int32),
                pltpu.VMEM((side_rows, LANES), jnp.int32),
                pltpu.VMEM((2, contact_pair.shape[1]), jnp.int32),
                pltpu.VMEM((9, contact_pair.shape[1]), F32),
                pltpu.VMEM((9, contact_pair.shape[1]), F32),
                pltpu.VMEM((3, contact_pair.shape[1]), F32),
                pltpu.VMEM((3, contact_pair.shape[1]), F32),
                pltpu.VMEM((tiles, LANES), jnp.int32),
                pltpu.VMEM(pressure.shape, F32),
                pltpu.VMEM((pressure.size // pressure.shape[2], LANES), F32),
                pltpu.VMEM((cell_rows, LANES), F32),
                pltpu.VMEM((12, cell_rows, LANES), F32),
                pltpu.VMEM((4, 7 * side_rows, LANES), F32),
                pltpu.VMEM((7 * side_rows, LANES), F32),
                pltpu.VMEM((SWEEPS - 1, 4, 3 * side_rows, LANES), F32),
                pltpu.VMEM((SWEEPS, 4, 3 * side_rows, LANES), F32),
                pltpu.VMEM((SWEEPS - 1, 8, 2, 3 * side_rows, LANES), F32),
                pltpu.VMEM((SWEEPS - 1, 3 * side_rows, LANES), F32),
                pltpu.VMEM((SWEEPS, 5, 3 * side_rows, LANES), F32),
                pltpu.VMEM((3 * cell_rows, LANES), F32),
                pltpu.VMEM((12 * cell_rows, LANES), F32),
                pltpu.VMEM((own_rows * 3, LANES), F32),
                pltpu.VMEM((3 * own_rows, LANES), F32),
                pltpu.VMEM((tiles * STAGE, LANES), F32),
                pltpu.VMEM((tiles * 3, LANES), jnp.int32),
                pltpu.VMEM((2 * tiles, LANES), jnp.int32),
                pltpu.VMEM((2 * tiles, LANES), jnp.int32),
                pltpu.VMEM((2 * tiles, LANES), F32),
                pltpu.VMEM((tiles, LANES, LANES), BF16),
                pltpu.VMEM((3 * (2 * own_rows + 8), LANES), F32),
                pltpu.VMEM((3 * gpad, LANES), F32),
                pltpu.VMEM((32 * PITCH, LANES), F32),
                pltpu.VMEM((2 * (own_rows + 2) * OWN_PITCH, LANES), F32),
                pltpu.VMEM((2 * (4 * side_rows + 1) * GHOST_PITCH, LANES), F32),
                pltpu.VMEM((LANES, side_rows * LANES), BF16),
                pltpu.VMEM((own_rows, side_rows * LANES), BF16),
                pltpu.VMEM((3 * own_rows, LANES), F32),
                pltpu.VMEM((4, side_rows, side_rows * LANES, LANES), BF16),
                pltpu.VMEM((4, 16 * side_rows, LANES), F32),
                pltpu.VMEM((4, 9 * side_rows, LANES), F32),
                pltpu.SemaphoreType.DMA((rounds, 4)),
                pltpu.SemaphoreType.DMA((rounds, 4)),
                pltpu.SemaphoreType.DMA((12,)),
                pltpu.SemaphoreType.DMA((12,)),
                pltpu.SemaphoreType.DMA((SWEEPS - 1, 8)),
                pltpu.SemaphoreType.DMA((SWEEPS - 1, 8)),
                pltpu.SemaphoreType.DMA((12,)),
            ],
            compiler_params=pltpu.CompilerParams(
                collective_id=0, has_side_effects=True, vmem_limit_bytes=60 * 1024 * 1024
            ),
        )(
            velocity,
            inv_mass.reshape(own_rows, LANES),
            drag.reshape(own_rows, LANES),
            grain_cell.reshape(own_rows, LANES),
            boundary_list.reshape(side_rows, LANES),
            contact_pair,
            frames,
            blocks,
            impulse_start,
            gap,
            contact_mask.reshape(tiles, LANES),
            pressure,
        )
        return pl.pallas_call(
            hand_on,
            out_shape=(
                jax.ShapeDtypeStruct(velocity.shape, F32),
                jax.ShapeDtypeStruct(impulse_start.shape, F32),
            ),
            in_specs=[pl.BlockSpec(memory_space=pl.ANY)] * 2,
            out_specs=(pl.BlockSpec(memory_space=pltpu.HBM),) * 2,
            scratch_shapes=[pltpu.SemaphoreType.DMA((2,))],
        )(
            pltpu.with_memory_space_constraint(out_vel, pltpu.VMEM),
            pltpu.with_memory_space_constraint(out_imp, pltpu.VMEM),
        )

    grains, lists = P(("gx", "gy")), P(None, ("gx", "gy"))
    return jax.shard_map(
        local,
        mesh=mesh,
        in_specs=(
            lists, grains, grains, grains, grains, lists, lists, lists, lists, lists, grains,
            P(None, "gx", "gy"),
        ),
        out_specs=(lists, lists),
        check_vma=False,
    )
```

```python
import jax
import jax.numpy as jnp
from jax import lax
from jax.experimental import pallas as pl
from jax.experimental.pallas import tpu as pltpu
from jax.sharding import PartitionSpec as P

SWEEPS = 2
TIME_STEP = 0.5
FRICTION = 0.5
FLOOR_VALUE = 0.1
LANES = 128
HALF = LANES // 2
ROWS = 48
PITCH = 49
STAGE = 49
OWN_PITCH = 25
GHOST_PITCH = 17
F32 = jnp.float32
BF16 = jnp.bfloat16
NEAR = ((-1, 0), (1, 0), (0, -1), (0, 1))
FAR = ((-2, 0), (2, 0), (0, -2), (0, 2), (-1, -1), (-1, 1), (1, -1), (1, 1))
AROUND = NEAR + FAR
ORDER = (0, 2, 1, 3, 0)
FIRST = {(-1, -1): 0, (1, -1): 1, (1, 1): 2, (-1, 1): 3, (-2, 0): 0, (0, -2): 1, (2, 0): 2, (0, 2): 3}


def take_lanes(values, lanes):
    return jnp.take_along_axis(values, lanes, axis=1, mode="promise_in_bounds")


def spread_row(ref, row):
    return jnp.broadcast_to(ref[pl.ds(row, 1), :], (8, LANES))


def step_kernel(
    sizes,
    vel_hbm, mass_hbm, drag_hbm, cell_hbm, bound_hbm, pair_hbm, frame_hbm, block_hbm,
    start_hbm, gap_hbm, mask_hbm, pres_hbm,
    out_vel, out_imp,
    vel_ref, mass_ref, drag_ref, cell_ref, bound_ref, pair_ref, frame_ref, block_ref,
    start_ref, gap_ref, mask_ref, pres_raw, pres_wide, pres_ref,
    pres_in, grain_in, grain_out, ghost_in, sum_in, far_in, ghost_out, sum_out,
    slope_s, slope_n, vel_s, free_s, stage, ends, codes, lanes_s, spots, table, ext, ghost_s,
    left, sums, ghost_sums, bound_hot, bound_row, part_s, push_s, same, split, joined,
    send_sem, recv_sem, pres_send, pres_recv, far_send, far_recv, load_sem,
):
    nx, ny = sizes
    tiles = mask_ref.shape[0]
    own_rows = mass_ref.shape[0]
    side_rows = bound_ref.shape[0]
    ghost_rows = 4 * side_rows
    cell_rows = pres_ref.shape[0]
    ext_rows = 2 * own_rows + 8
    gpad = 2 * ghost_rows
    own_slots = own_rows * LANES
    ghost_slots = ghost_rows * LANES
    own_part = own_rows + 2
    ghost_part = ghost_rows + 1
    row_iota = lax.broadcasted_iota(jnp.int32, (8, LANES), 0)

    mx, my = lax.axis_index("gx"), lax.axis_index("gy")
    reach = lambda dx, dy: (lax.rem(mx + dx + 2 * nx, nx), lax.rem(my + dy + 2 * ny, ny))
    sides = [reach(dx, dy) for dx, dy in NEAR]
    others = [k for k, (dx, dy) in enumerate(AROUND) if dx % nx or dy % ny]

    loads = [
        pltpu.make_async_copy(source, target, load_sem.at[k])
        for k, (source, target) in enumerate(
            (
                (vel_hbm, vel_ref), (bound_hbm, bound_ref), (drag_hbm, drag_ref),
                (mass_hbm, mass_ref), (cell_hbm, cell_ref), (pair_hbm, pair_ref),
                (mask_hbm, mask_ref), (start_hbm, start_ref), (gap_hbm, gap_ref),
                (frame_hbm, frame_ref), (block_hbm, block_ref),
            )
        )
    ]
    pres_load = pltpu.make_async_copy(pres_hbm, pres_raw, load_sem.at[11])
    pres_load.start()
    for load in loads:
        load.start()

    barrier = pltpu.get_barrier_semaphore()
    for k in others:
        pl.semaphore_signal(
            barrier, inc=1, device_id=reach(*AROUND[k]), device_id_type=pl.DeviceIdType.MESH
        )

    lane = lax.broadcasted_iota(jnp.int32, (cell_rows, LANES), 1)
    pres_load.wait()
    width = pres_raw.shape[2]
    pres_wide[:, 0:width] = pres_raw[...].reshape(-1, width)
    per_row = LANES // width
    p = pres_wide[pl.ds(0, cell_rows, stride=per_row), :]
    for k in range(1, per_row):
        piece = pltpu.roll(pres_wide[pl.ds(k, cell_rows, stride=per_row), :], k * width, 1)
        p = jnp.where(lane < k * width, p, piece)
    pres_ref[...] = p
    def exchange(step, source, target):
        copies = []
        for g in range(4):
            copies.append(
                pltpu.make_async_remote_copy(
                    src_ref=source(g),
                    dst_ref=target(g ^ 1),
                    send_sem=send_sem.at[step, g],
                    recv_sem=recv_sem.at[step, g ^ 1],
                    device_id=sides[g],
                    device_id_type=pl.DeviceIdType.MESH,
                )
            )
        for copy in copies:
            copy.start()
        return copies

    sent = []

    def finish(copies):
        for copy in copies:
            copy.wait_recv()
        sent.extend(copies)

    for load in loads[:5]:
        load.wait()
    bound_all = bound_ref[...]
    bound_lane = bound_all & (LANES - 1)
    bound_at = bound_all >> 7
    two_lane = jnp.concatenate([bound_lane, bound_lane], axis=0)
    two_at = jnp.concatenate([bound_at, bound_at], axis=0)
    half = own_rows // 2
    upper = row_iota < side_rows
    low_at = two_at < half

    def pick(row_of, kinds, unroll):
        def body(k, acc):
            acc = list(acc)
            for i in range(4):
                r = k * 4 + i
                hit = two_at == jnp.where(upper, r, r + half)
                for c in range(len(kinds)):
                    got = take_lanes(jnp.where(upper, row_of(c, r), row_of(c, r + half)), two_lane)
                    acc[c] = jnp.where(hit, got, acc[c])
            return tuple(acc)

        start = tuple(jnp.zeros((8, LANES), kind) for kind in kinds)
        acc = lax.fori_loop(0, half // 4, body, start, unroll=unroll)
        return [
            jnp.where(low_at[:side_rows], got[:side_rows], got[side_rows:]) for got in acc
        ]

    def grain_row(c, r):
        if c < 3:
            cols = pl.ds(pl.multiple_of(r * LANES, LANES), LANES)
            return jnp.broadcast_to(vel_ref[pl.ds(c, 1), cols], (8, LANES))
        return spread_row((drag_ref, mass_ref, cell_ref)[c - 3], r)

    *moving, drag_b, mass_b, cell_b = pick(grain_row, (F32,) * 5 + (jnp.int32,), 2)
    below = 1.0 + TIME_STEP * drag_b
    for c in range(3):
        grain_out[c * side_rows : (c + 1) * side_rows, :] = moving[c] / below
    grain_out[3 * side_rows : 4 * side_rows, :] = TIME_STEP * (drag_b + mass_b) / below
    grain_out[4 * side_rows : 5 * side_rows, :] = cell_b.astype(F32)
    grain_out[5 * side_rows : 6 * side_rows, :] = mass_b
    grain_out[6 * side_rows : 7 * side_rows, :] = bound_all.astype(F32)
    pl.semaphore_wait(barrier, len(others))
    spreading = {}
    for k in others:
        dx, dy = AROUND[k]
        back = AROUND.index((-dx, -dy))
        spreading[back] = pltpu.make_async_remote_copy(
            src_ref=pres_ref,
            dst_ref=pres_in.at[back],
            send_sem=pres_send.at[k],
            recv_sem=pres_recv.at[back],
            device_id=reach(dx, dy),
            device_id_type=pl.DeviceIdType.MESH,
        )
    for copy in spreading.values():
        copy.start()
    flying = exchange(0, lambda g: grain_out, lambda g: grain_in.at[g])
    for load in loads[5:]:
        load.wait()

    def stage_tile(t, carry):
        cols = pl.ds(pl.multiple_of(t * LANES, LANES), LANES)
        base = t * STAGE
        stage[pl.ds(base, 9), :] = frame_ref[:, cols]
        stage[pl.ds(base + 16, 9), :] = block_ref[:, cols]
        stage[pl.ds(base + 32, 3), :] = start_ref[:, cols]
        stage[pl.ds(base + 40, 3), :] = gap_ref[:, cols]
        ends[pl.ds(t * 3, 2), :] = pair_ref[:, cols]
        return carry

    lax.fori_loop(0, tiles, stage_tile, 0, unroll=4)

    def stage_grain(t, carry):
        cols = pl.ds(pl.multiple_of(t * LANES, LANES), LANES)
        vel_s[pl.ds(t * 3, 3), :] = vel_ref[:, cols]
        return carry

    lax.fori_loop(0, own_rows, stage_grain, 0, unroll=4)

    def place(u, carry):
        tile = u * 8 + row_iota
        for e in range(2):
            slot = ends[pl.ds(u * 24 + 1 - e, 8, stride=3), :]
            own = slot < own_slots
            near = (slot - HALF * tile) & (own_slots - 1)
            far = (slot - own_slots - HALF * (tile >> 2)) & (ghost_slots - 1)
            rel = jnp.where(own, near, far)
            at = pl.ds(pl.multiple_of(e * tiles + u * 8, 8), 8)
            codes[at, :] = jnp.where(own, 0, 4) + (rel >> 6)
            lanes_s[at, :] = rel & (LANES - 1)
            spots[at, :] = (rel & (HALF - 1)).astype(F32)
        return carry

    lax.fori_loop(0, tiles // 8, place, 0, unroll=2)

    hot_iota = lax.broadcasted_iota(jnp.int32, (LANES, LANES), 0)
    row_hot = lax.broadcasted_iota(jnp.int32, (own_rows, LANES), 0)
    for q in range(side_rows):
        cols = slice(q * LANES, (q + 1) * LANES)
        bound_hot[:, cols] = jnp.where(hot_iota == bound_lane[q : q + 1], 1.0, 0.0).astype(BF16)
        bound_row[:, cols] = jnp.where(row_hot == bound_at[q : q + 1], 1.0, 0.0).astype(BF16)

    def spread_halves(ref, first, value):
        rows = value.shape[0]
        turned = pltpu.roll(value, HALF, 1)
        after = jnp.concatenate([turned[1:], turned[:1]], axis=0)
        first_half = lax.broadcasted_iota(jnp.int32, value.shape, 1) < HALF
        ref[pl.ds(first, rows, stride=2), :] = value
        ref[pl.ds(first + 1, rows, stride=2), :] = jnp.where(first_half, turned, after)

    def spread_current(c, value):
        spread_halves(ext, c * ext_rows, value)
        ext[pl.ds(c * ext_rows + 2 * own_rows, 8), :] = ext[pl.ds(c * ext_rows, 8), :]

    iotas = [
        (lax.broadcasted_iota(jnp.int32, (16, LANES), 0) + 16 * q).astype(F32).astype(BF16)
        for q in range(HALF // 16)
    ]
    signs = [jnp.full((16, LANES), sign, BF16) for sign in (1.0, -1.0)]
    zero16 = jnp.zeros((16, LANES), BF16)

    def build(t, carry):
        for e in range(2):
            row = jnp.broadcast_to(spots[pl.ds(e * tiles + t, 1), :], (16, LANES)).astype(BF16)
            for q in range(HALF // 16):
                at = slice(e * HALF + 16 * q, e * HALF + 16 * (q + 1))
                table[t, at, :] = jnp.where(iotas[q] == row, signs[e], zero16)
        return carry

    lax.fori_loop(0, tiles, build, 0, unroll=4)
    for i in range(64):
        left[i * PITCH + 36 : i * PITCH + ROWS, :] = jnp.zeros((12, LANES), F32)

    for k in range(4):
        spreading[k].wait_recv()
    even = (lax.broadcasted_iota(jnp.int32, (cell_rows, LANES), 0) & 1) == 0
    up1 = lambda a: jnp.concatenate([a[1:], a[:1]], axis=0)
    down1 = lambda a: jnp.concatenate([a[-1:], a[:-1]], axis=0)
    turn = lambda a, n: pltpu.roll(a, n % LANES, 1)
    none = jnp.zeros((2, LANES), F32)

    def pres_at(dx, dy):
        if dx % nx == 0 and dy % ny == 0:
            return p
        return pres_in[AROUND.index((dx, dy))]

    def slopes(ref, first, dx, dy):
        mid = pres_at(dx, dy)
        prev_x, next_x = pres_at(dx - 1, dy), pres_at(dx + 1, dy)
        prev_y, next_y = pres_at(dx, dy - 1), pres_at(dx, dy + 1)
        after = turn(mid, -16)
        plus = jnp.where(lane < 112, after, jnp.where(even, up1(after), down1(turn(next_x, -16))))
        before = turn(mid, 16)
        minus = jnp.where(lane >= 16, before, jnp.where(even, up1(turn(prev_x, 16)), down1(before)))
        ref[first : first + cell_rows] = (plus - minus) * 0.5
        plus = jnp.where((lane & 15) < 15, turn(mid, -1), turn(next_y, 15))
        minus = jnp.where((lane & 15) > 0, turn(mid, 1), turn(prev_y, -15))
        ref[first + cell_rows : first + 2 * cell_rows] = (plus - minus) * 0.5
        ref[first + 2 * cell_rows : first + 3 * cell_rows] = (
            jnp.concatenate([mid[2:], none], axis=0) - jnp.concatenate([none, mid[:-2]], axis=0)
        ) * 0.5

    slopes(slope_s, 0, 0, 0)

    def free(k, carry):
        at = pl.ds(pl.multiple_of(k * 8, 8), 8)
        cells = cell_ref[at, :]
        cell_at, cell_lane = cells >> 7, cells & (LANES - 1)
        drag, mass = drag_ref[at, :], mass_ref[at, :]
        for c in range(3):
            slope = jnp.zeros((8, LANES), F32)
            for r in range(cell_rows):
                got = take_lanes(spread_row(slope_s, c * cell_rows + r), cell_lane)
                slope = jnp.where(cell_at == r, got, slope)
            v = vel_s[pl.ds(k * 24 + c, 8, stride=3), :]
            free_s[pl.ds(pl.multiple_of(c * own_rows + k * 8, 8), 8), :] = (
                v - TIME_STEP * (drag + mass) * slope
            ) / (1.0 + TIME_STEP * drag)
        return carry

    lax.fori_loop(0, own_rows // 8, free, 0, unroll=2)
    for c in range(3):
        spread_current(c, free_s[c * own_rows : (c + 1) * own_rows, :])
    for k in others[4:]:
        spreading[k].wait_recv()
    sent.extend(spreading.values())
    finish(flying)
    for g in range(4):
        slopes(slope_n, 3 * cell_rows * g, *NEAR[g])
    ghost_free = [[], [], []]
    for g in (0, 2):
        both = [
            jnp.concatenate(
                [grain_in[g + i, k * side_rows : (k + 1) * side_rows, :] for i in range(2)], axis=0
            )
            for k in range(5)
        ]
        cells = both[4].astype(jnp.int32)
        cell_at, cell_lane = cells >> 7, cells & (LANES - 1)
        for c in range(3):
            slope = jnp.zeros((8, LANES), F32)
            for r in range(cell_rows):
                first = (3 * g + c) * cell_rows + r
                row = jnp.where(
                    row_iota < side_rows,
                    spread_row(slope_n, first),
                    spread_row(slope_n, first + 3 * cell_rows),
                )
                slope = jnp.where(cell_at == r, take_lanes(row, cell_lane), slope)
            ghost_free[c].append(both[c] - both[3] * slope)
    for c in range(3):
        spread_halves(ghost_s, c * gpad, jnp.concatenate(ghost_free[c], axis=0))

    split[...] = jnp.zeros(split.shape, F32)
    nt = (((1,), (1,)), ((), ()))
    for sweep in range(SWEEPS):
        def contacts(u, odd):
            at = pl.ds(pl.multiple_of(u * 8, 8), 8)
            code, lanes = [], []
            for e in range(2):
                end_at = pl.ds(pl.multiple_of(e * tiles + u * 8, 8), 8)
                code.append(codes[end_at, :])
                lanes.append(lanes_s[end_at, :])
            relative = []
            for c in range(3):
                near = ext[pl.ds(c * ext_rows + u * 8, 8), :]
                next_ = ext[pl.ds(c * ext_rows + u * 8 + 2, 8), :]
                far = jnp.where(
                    row_iota < 4,
                    spread_row(ghost_s, c * gpad + 2 * u),
                    spread_row(ghost_s, c * gpad + 2 * u + 1),
                )
                ends_val = []
                for e in range(2):
                    val = jnp.where(
                        code[e] < 4, take_lanes(next_, lanes[e]), take_lanes(far, lanes[e])
                    )
                    ends_val.append(jnp.where(code[e] < 2, take_lanes(near, lanes[e]), val))
                relative.append(ends_val[0] - ends_val[1])
            part = lambda k: stage[pl.ds(u * (8 * STAGE) + k, 8, stride=STAGE), :]
            fr = [part(k) for k in range(9)]
            target = [
                fr[3 * m] * relative[0]
                + fr[3 * m + 1] * relative[1]
                + fr[3 * m + 2] * relative[2]
                + part(40 + m)
                for m in range(3)
            ]
            trial = []
            for k in range(3):
                before = part(32 + k)
                trial.append(
                    before
                    - (
                        part(16 + 3 * k) * target[0]
                        + part(17 + 3 * k) * target[1]
                        + part(18 + 3 * k) * target[2]
                    )
                )
            active = mask_ref[at, :].astype(F32)
            normal = jnp.maximum(trial[0], 0.0)
            tangent = jnp.sqrt(trial[1] * trial[1] + trial[2] * trial[2])
            factor = jnp.minimum(1.0, FRICTION * normal / jnp.maximum(tangent, FLOOR_VALUE))
            imp = [normal * active, factor * trial[1] * active, factor * trial[2] * active]
            for k in range(3):
                stage[pl.ds(u * (8 * STAGE) + 32 + k, 8, stride=STAGE), :] = imp[k]
            pushes = [fr[c] * imp[0] + fr[3 + c] * imp[1] + fr[6 + c] * imp[2] for c in range(3)]
            if sweep < SWEEPS - 1:
                scatter(u, odd, code, pushes, range(6))
                return
            for c in range(3):
                push_s[c, at, :] = pushes[c]
            scatter(u, odd, code, pushes, (4, 5))

        def scatter(u, odd, code, pushes, blocks):
            rows = -(-len(blocks) * 6 // 16) * 16
            for c in range(3):
                high = pushes[c].astype(BF16).astype(F32)
                for s, term in enumerate((high, pushes[c] - high)):
                    for e in range(2):
                        for n, h in enumerate(blocks):
                            left[
                                pl.ds((e * 8 + odd) * PITCH + (n * 3 + c) * 2 + s, 8, stride=PITCH), :
                            ] = jnp.where(code[e] == h, term, 0.0)
            ghost_sum = None
            for i in range(8):
                got = lax.dot_general(
                    jnp.concatenate(
                        [
                            left[first : first + rows, :].astype(BF16)
                            for first in ((odd + i) * PITCH, (odd + i + 8) * PITCH)
                        ],
                        axis=1,
                    ),
                    jnp.concatenate(
                        [
                            table[u * 8 + i, e * HALF : (e + 1) * HALF, :]
                            for e in range(2)
                        ],
                        axis=1,
                    ),
                    nt,
                    preferred_element_type=F32,
                )
                if 0 in blocks:
                    at = ((i & 1) * own_part + u * 4 + (i >> 1) + 2) * OWN_PITCH
                    sums[pl.ds(at, 24), 0:HALF] = got[0:24]
                if 5 in blocks:
                    far = 6 * (len(blocks) - 2)
                    got = got[far : far + 16]
                    ghost_sum = got if i % 4 == 0 else ghost_sum + got
                    if i % 4 == 3:
                        at = ((i >> 2) * ghost_part + u + 1) * GHOST_PITCH
                        ghost_sums[pl.ds(at, 16), 0:HALF] = ghost_sum

        def own_scatter(u, odd):
            at = pl.ds(pl.multiple_of(u * 8, 8), 8)
            code = [codes[pl.ds(pl.multiple_of(e * tiles + u * 8, 8), 8), :] for e in range(2)]
            scatter(u, odd, code, [push_s[c, at, :] for c in range(3)], range(4))

        def own_two(k, carry):
            for i in range(4):
                own_scatter(4 * k + i, 16 * i)
            return carry

        def two(k, carry):
            for i in range(4):
                contacts(4 * k + i, 16 * i)
            return carry

        lax.fori_loop(0, tiles // 32, two, 0, unroll=4)
        for par in range(2):
            base = par * ghost_part * GHOST_PITCH
            ghost_sums[base : base + GHOST_PITCH, :] = ghost_sums[
                base + ghost_rows * GHOST_PITCH : base + (ghost_rows + 1) * GHOST_PITCH, :
            ]
        first_half = lax.broadcasted_iota(jnp.int32, (8, LANES), 1) < HALF

        def gather_halves(ref, part_rows, pitch, pad, r, terms):
            halves = []
            for par in range(2):
                total = None
                for h, row in terms:
                    for s in range(2):
                        block = par - h
                        first = ((block & 1) * part_rows + r + (block >> 1) + pad) * pitch + row + s
                        got = ref[pl.ds(first, 8, stride=pitch), :]
                        total = got if total is None else total + got
                halves.append(total)
            return jnp.where(first_half, halves[0], pltpu.roll(halves[1], HALF, 1))

        for c in range(3):
            for r in range(0, ghost_rows, 8):
                terms = [(h, h * 6 + c * 2) for h in range(2)]
                total = gather_halves(ghost_sums, ghost_part, GHOST_PITCH, 1, r, terms)
                for i in range(0, 8, side_rows):
                    for slot, group in enumerate(ORDER):
                        if group == (r + i) // side_rows:
                            sum_out[sweep, slot, c * side_rows : (c + 1) * side_rows, :] = total[
                                i : i + side_rows
                            ]
        flying = exchange(
            1 + 2 * sweep,
            lambda g: sum_out.at[sweep, ORDER.index(g)],
            lambda g: sum_in.at[sweep, g],
        )
        distant = {}
        if sweep < SWEEPS - 1:
            for k in others[4:]:
                dx, dy = AROUND[k]
                back = AROUND.index((-dx, -dy))
                count = 1 if k < 8 else 2
                distant[back] = pltpu.make_async_remote_copy(
                    src_ref=sum_out.at[sweep, pl.ds(FIRST[dx, dy], count)],
                    dst_ref=far_in.at[sweep, back - 4, pl.ds(0, count)],
                    send_sem=far_send.at[sweep, k - 4],
                    recv_sem=far_recv.at[sweep, back - 4],
                    device_id=reach(dx, dy),
                    device_id_type=pl.DeviceIdType.MESH,
                )
            for copy in distant.values():
                copy.start()
        if sweep == SWEEPS - 1:
            lax.fori_loop(0, tiles // 32, own_two, 0, unroll=2)
        for par in range(2):
            base = par * own_part * OWN_PITCH
            sums[base : base + 2 * OWN_PITCH, :] = sums[
                base + own_rows * OWN_PITCH : base + (own_rows + 2) * OWN_PITCH, :
            ]
        own_total = []
        for c in range(3):
            parts = []
            for r in range(0, own_rows, 8):
                terms = [(h, h * 6 + c * 2) for h in range(4)]
                parts.append(gather_halves(sums, own_part, OWN_PITCH, 2, r, terms))
            own_total.append(jnp.concatenate(parts, axis=0))
        mass = mass_ref[...]
        for c in range(3):
            rows = slice(c * own_rows, (c + 1) * own_rows)
            part_s[rows, :] = free_s[rows, :] + mass * own_total[c]
        if sweep < SWEEPS - 1:
            got = pick(lambda c, r: spread_row(part_s, c * own_rows + r), (F32,) * 3, 4)
            for c in range(3):
                ghost_out[sweep, c * side_rows : (c + 1) * side_rows, :] = got[c]
            bases = exchange(
                2 + 2 * sweep, lambda g: ghost_out.at[sweep], lambda g: ghost_in.at[sweep, g]
            )
            if sweep == 0:
                for g in range(4):
                    list_in = grain_in[g, 6 * side_rows : 7 * side_rows, :]
                    for a in range(side_rows):
                        down = jnp.broadcast_to(list_in[a : a + 1], (LANES, LANES)).T
                        for b in range(side_rows):
                            same[g, b, a * LANES : (a + 1) * LANES, :] = jnp.where(
                                down == list_in[b : b + 1], 1.0, 0.0
                            ).astype(BF16)
        if sweep == SWEEPS - 1:

            def unstage(t, carry):
                cols = pl.ds(pl.multiple_of(t * LANES, LANES), LANES)
                out_imp[:, cols] = stage[pl.ds(t * STAGE + 32, 3), :]
                return carry

            lax.fori_loop(0, tiles, unstage, 0, unroll=8)
        finish(flying)
        received = (
            sum_in[sweep, 0] + sum_in[sweep, 1] + sum_in[sweep, 2] + sum_in[sweep, 3]
        )
        high = received.astype(BF16).astype(F32)
        low = received - high
        for c in range(3):
            total = None
            for term in (high, low):
                row = jnp.concatenate(
                    [
                        bound_row[:, q * LANES : (q + 1) * LANES]
                        * jnp.broadcast_to(
                            term[c * side_rows + q : c * side_rows + q + 1], (own_rows, LANES)
                        ).astype(BF16)
                        for q in range(side_rows)
                    ],
                    axis=1,
                )
                got = lax.dot_general(row, bound_hot[...], nt, preferred_element_type=F32)
                total = got if total is None else total + got
            current = part_s[c * own_rows : (c + 1) * own_rows, :] + mass * total
            if sweep < SWEEPS - 1:
                spread_current(c, current)
            else:
                vel_s[pl.ds(c, own_rows, stride=3), :] = current
        if sweep < SWEEPS - 1:
            for copy in distant.values():
                copy.wait_recv()
            sent.extend(distant.values())

            def sum_of(dx, dy, group):
                if dx % nx == 0 and dy % ny == 0:
                    return sum_out[sweep, ORDER.index(group)]
                at = AROUND.index((dx, dy)) - 4
                return far_in[sweep, at, int(ORDER[FIRST[-dx, -dy]] != group)]

            for g in range(4):
                total = None
                for d in range(4):
                    dx, dy = NEAR[g][0] + NEAR[d][0], NEAR[g][1] + NEAR[d][1]
                    got = sum_of(dx, dy, d ^ 1)
                    total = got if total is None else total + got
                high = total.astype(BF16).astype(F32)
                split[g, 0 : 3 * side_rows, :] = high
                split[g, 3 * side_rows : 6 * side_rows, :] = total - high
                rows = jnp.concatenate(
                    [split[g, pl.ds(q, 16, stride=side_rows), :] for q in range(side_rows)], axis=1
                ).astype(BF16)
                got = jnp.dot(
                    rows,
                    jnp.concatenate([same[g, q] for q in range(side_rows)], axis=1),
                    preferred_element_type=F32,
                )
                for q in range(side_rows):
                    joined[g, q * 9 : q * 9 + 8, :] = got[0:8, q * LANES : (q + 1) * LANES]
            finish(bases)
            for c in range(3):
                ghosts = []
                for g in range(4):
                    more = (
                        joined[g, pl.ds(c, side_rows, stride=9), :]
                        + joined[g, pl.ds(3 + c, side_rows, stride=9), :]
                    )
                    ghosts.append(
                        ghost_in[sweep, g, c * side_rows : (c + 1) * side_rows, :]
                        + grain_in[g, 5 * side_rows : 6 * side_rows, :] * more
                    )
                spread_halves(ghost_s, c * gpad, jnp.concatenate(ghosts, axis=0))

    def unstage_grain(t, carry):
        cols = pl.ds(pl.multiple_of(t * LANES, LANES), LANES)
        out_vel[:, cols] = vel_s[pl.ds(t * 3, 3), :]
        return carry

    lax.fori_loop(0, own_rows, unstage_grain, 0, unroll=8)
    for copy in sent:
        copy.wait_send()


def hand_on(vel_in, imp_in, vel_out, imp_out, sem):
    copies = [
        pltpu.make_async_copy(imp_in, imp_out, sem.at[0]),
        pltpu.make_async_copy(vel_in, vel_out, sem.at[1]),
    ]
    for copy in copies:
        copy.start()
    for copy in copies:
        copy.wait()


def solution(mesh):
    sizes = (mesh.shape["gx"], mesh.shape["gy"])

    def local(
        velocity, inv_mass, drag, grain_cell, boundary_list, contact_pair, frames, blocks,
        impulse_start, gap, contact_mask, pressure,
    ):
        own_rows = velocity.shape[1] // LANES
        tiles = contact_pair.shape[1] // LANES
        side_rows = boundary_list.shape[0] // LANES
        cell_rows = pressure.size // LANES
        gpad = 8 * side_rows
        rounds = 2 * SWEEPS
        out_vel, out_imp = pl.pallas_call(
            lambda *refs: step_kernel(sizes, *refs),
            out_shape=(pltpu.VMEM(velocity.shape, F32), pltpu.VMEM(impulse_start.shape, F32)),
            in_specs=[pl.BlockSpec(memory_space=pltpu.HBM)] * 12,
            out_specs=(pl.BlockSpec(memory_space=pltpu.VMEM),) * 2,
            scratch_shapes=[
                pltpu.VMEM((3, velocity.shape[1]), F32),
                pltpu.VMEM((own_rows, LANES), F32),
                pltpu.VMEM((own_rows, LANES), F32),
                pltpu.VMEM((own_rows, LANES), jnp.int32),
                pltpu.VMEM((side_rows, LANES), jnp.int32),
                pltpu.VMEM((2, contact_pair.shape[1]), jnp.int32),
                pltpu.VMEM((9, contact_pair.shape[1]), F32),
                pltpu.VMEM((9, contact_pair.shape[1]), F32),
                pltpu.VMEM((3, contact_pair.shape[1]), F32),
                pltpu.VMEM((3, contact_pair.shape[1]), F32),
                pltpu.VMEM((tiles, LANES), jnp.int32),
                pltpu.VMEM(pressure.shape, F32),
                pltpu.VMEM((pressure.size // pressure.shape[2], LANES), F32),
                pltpu.VMEM((cell_rows, LANES), F32),
                pltpu.VMEM((12, cell_rows, LANES), F32),
                pltpu.VMEM((4, 7 * side_rows, LANES), F32),
                pltpu.VMEM((7 * side_rows, LANES), F32),
                pltpu.VMEM((SWEEPS - 1, 4, 3 * side_rows, LANES), F32),
                pltpu.VMEM((SWEEPS, 4, 3 * side_rows, LANES), F32),
                pltpu.VMEM((SWEEPS - 1, 8, 2, 3 * side_rows, LANES), F32),
                pltpu.VMEM((SWEEPS - 1, 3 * side_rows, LANES), F32),
                pltpu.VMEM((SWEEPS, 5, 3 * side_rows, LANES), F32),
                pltpu.VMEM((3 * cell_rows, LANES), F32),
                pltpu.VMEM((12 * cell_rows, LANES), F32),
                pltpu.VMEM((own_rows * 3, LANES), F32),
                pltpu.VMEM((3 * own_rows, LANES), F32),
                pltpu.VMEM((tiles * STAGE, LANES), F32),
                pltpu.VMEM((tiles * 3, LANES), jnp.int32),
                pltpu.VMEM((2 * tiles, LANES), jnp.int32),
                pltpu.VMEM((2 * tiles, LANES), jnp.int32),
                pltpu.VMEM((2 * tiles, LANES), F32),
                pltpu.VMEM((tiles, LANES, LANES), BF16),
                pltpu.VMEM((3 * (2 * own_rows + 8), LANES), F32),
                pltpu.VMEM((3 * gpad, LANES), F32),
                pltpu.VMEM((64 * PITCH, LANES), F32),
                pltpu.VMEM((2 * (own_rows + 2) * OWN_PITCH, LANES), F32),
                pltpu.VMEM((2 * (4 * side_rows + 1) * GHOST_PITCH, LANES), F32),
                pltpu.VMEM((LANES, side_rows * LANES), BF16),
                pltpu.VMEM((own_rows, side_rows * LANES), BF16),
                pltpu.VMEM((3 * own_rows, LANES), F32),
                pltpu.VMEM((3, tiles, LANES), F32),
                pltpu.VMEM((4, side_rows, side_rows * LANES, LANES), BF16),
                pltpu.VMEM((4, 16 * side_rows, LANES), F32),
                pltpu.VMEM((4, 9 * side_rows, LANES), F32),
                pltpu.SemaphoreType.DMA((rounds, 4)),
                pltpu.SemaphoreType.DMA((rounds, 4)),
                pltpu.SemaphoreType.DMA((12,)),
                pltpu.SemaphoreType.DMA((12,)),
                pltpu.SemaphoreType.DMA((SWEEPS - 1, 8)),
                pltpu.SemaphoreType.DMA((SWEEPS - 1, 8)),
                pltpu.SemaphoreType.DMA((12,)),
            ],
            compiler_params=pltpu.CompilerParams(
                collective_id=0, has_side_effects=True, vmem_limit_bytes=60 * 1024 * 1024
            ),
        )(
            velocity,
            inv_mass.reshape(own_rows, LANES),
            drag.reshape(own_rows, LANES),
            grain_cell.reshape(own_rows, LANES),
            boundary_list.reshape(side_rows, LANES),
            contact_pair,
            frames,
            blocks,
            impulse_start,
            gap,
            contact_mask.reshape(tiles, LANES),
            pressure,
        )
        return pl.pallas_call(
            hand_on,
            out_shape=(
                jax.ShapeDtypeStruct(velocity.shape, F32),
                jax.ShapeDtypeStruct(impulse_start.shape, F32),
            ),
            in_specs=[pl.BlockSpec(memory_space=pl.ANY)] * 2,
            out_specs=(pl.BlockSpec(memory_space=pltpu.HBM),) * 2,
            scratch_shapes=[pltpu.SemaphoreType.DMA((2,))],
        )(
            pltpu.with_memory_space_constraint(out_vel, pltpu.VMEM),
            pltpu.with_memory_space_constraint(out_imp, pltpu.VMEM),
        )

    grains, lists = P(("gx", "gy")), P(None, ("gx", "gy"))
    return jax.shard_map(
        local,
        mesh=mesh,
        in_specs=(
            lists, grains, grains, grains, grains, lists, lists, lists, lists, lists, grains,
            P(None, "gx", "gy"),
        ),
        out_specs=(lists, lists),
        check_vma=False,
    )
```

```python
import jax
import jax.numpy as jnp
from jax import lax
from jax.experimental import pallas as pl
from jax.experimental.pallas import tpu as pltpu
from jax.sharding import PartitionSpec as P

SWEEPS = 2
TIME_STEP = 0.5
FRICTION = 0.5
FLOOR_VALUE = 0.1
LANES = 128
HALF = LANES // 2
ROWS = 48
PITCH = 49
STAGE = 49
OWN_PITCH = 25
GHOST_PITCH = 17
F32 = jnp.float32
BF16 = jnp.bfloat16
NEAR = ((-1, 0), (1, 0), (0, -1), (0, 1))
FAR = ((-2, 0), (2, 0), (0, -2), (0, 2), (-1, -1), (-1, 1), (1, -1), (1, 1))
AROUND = NEAR + FAR
ORDER = (0, 2, 1, 3, 0)
FIRST = {(-1, -1): 0, (1, -1): 1, (1, 1): 2, (-1, 1): 3, (-2, 0): 0, (0, -2): 1, (2, 0): 2, (0, 2): 3}


def take_lanes(values, lanes):
    return jnp.take_along_axis(values, lanes, axis=1, mode="promise_in_bounds")


def spread_row(ref, row):
    return jnp.broadcast_to(ref[pl.ds(row, 1), :], (8, LANES))


def step_kernel(
    sizes,
    vel_hbm, mass_hbm, drag_hbm, cell_hbm, bound_hbm, pair_hbm, frame_hbm, block_hbm,
    start_hbm, gap_hbm, mask_hbm, pres_hbm,
    out_vel, out_imp,
    vel_ref, mass_ref, drag_ref, cell_ref, bound_ref, pair_ref, frame_ref, block_ref,
    start_ref, gap_ref, mask_ref, pres_raw, pres_wide, pres_ref,
    pres_in, grain_in, grain_out, ghost_in, sum_in, far_in, ghost_out, sum_out,
    slope_s, slope_n, vel_s, free_s, stage, ends, codes, lanes_s, spots, table, ext, ghost_s,
    left, sums, ghost_sums, bound_hot, bound_row, part_s, push_s, same, split, joined,
    send_sem, recv_sem, pres_send, pres_recv, far_send, far_recv, load_sem,
):
    nx, ny = sizes
    tiles = mask_ref.shape[0]
    own_rows = mass_ref.shape[0]
    side_rows = bound_ref.shape[0]
    ghost_rows = 4 * side_rows
    cell_rows = pres_ref.shape[0]
    ext_rows = 2 * own_rows + 8
    gpad = 2 * ghost_rows
    own_slots = own_rows * LANES
    ghost_slots = ghost_rows * LANES
    own_part = own_rows + 2
    ghost_part = ghost_rows + 1
    row_iota = lax.broadcasted_iota(jnp.int32, (8, LANES), 0)

    mx, my = lax.axis_index("gx"), lax.axis_index("gy")
    reach = lambda dx, dy: (lax.rem(mx + dx + 2 * nx, nx), lax.rem(my + dy + 2 * ny, ny))
    sides = [reach(dx, dy) for dx, dy in NEAR]
    others = [k for k, (dx, dy) in enumerate(AROUND) if dx % nx or dy % ny]

    loads = [
        pltpu.make_async_copy(source, target, load_sem.at[k])
        for k, (source, target) in enumerate(
            (
                (vel_hbm, vel_ref), (bound_hbm, bound_ref), (drag_hbm, drag_ref),
                (mass_hbm, mass_ref), (cell_hbm, cell_ref), (pair_hbm, pair_ref),
                (mask_hbm, mask_ref), (start_hbm, start_ref), (gap_hbm, gap_ref),
                (frame_hbm, frame_ref), (block_hbm, block_ref),
            )
        )
    ]
    pres_load = pltpu.make_async_copy(pres_hbm, pres_raw, load_sem.at[11])
    pres_load.start()
    for load in loads:
        load.start()

    barrier = pltpu.get_barrier_semaphore()
    for k in others:
        pl.semaphore_signal(
            barrier, inc=1, device_id=reach(*AROUND[k]), device_id_type=pl.DeviceIdType.MESH
        )

    lane = lax.broadcasted_iota(jnp.int32, (cell_rows, LANES), 1)
    pres_load.wait()
    width = pres_raw.shape[2]
    pres_wide[:, 0:width] = pres_raw[...].reshape(-1, width)
    per_row = LANES // width
    p = pres_wide[pl.ds(0, cell_rows, stride=per_row), :]
    for k in range(1, per_row):
        piece = pltpu.roll(pres_wide[pl.ds(k, cell_rows, stride=per_row), :], k * width, 1)
        p = jnp.where(lane < k * width, p, piece)
    pres_ref[...] = p
    def exchange(step, source, target):
        copies = []
        for g in range(4):
            copies.append(
                pltpu.make_async_remote_copy(
                    src_ref=source(g),
                    dst_ref=target(g ^ 1),
                    send_sem=send_sem.at[step, g],
                    recv_sem=recv_sem.at[step, g ^ 1],
                    device_id=sides[g],
                    device_id_type=pl.DeviceIdType.MESH,
                )
            )
        for copy in copies:
            copy.start()
        return copies

    sent = []

    def finish(copies):
        for copy in copies:
            copy.wait_recv()
        sent.extend(copies)

    for load in loads[:5]:
        load.wait()
    bound_all = bound_ref[...]
    bound_lane = bound_all & (LANES - 1)
    bound_at = bound_all >> 7
    two_lane = jnp.concatenate([bound_lane, bound_lane], axis=0)
    two_at = jnp.concatenate([bound_at, bound_at], axis=0)
    half = own_rows // 2
    upper = row_iota < side_rows
    low_at = two_at < half

    def pick(row_of, kinds, unroll):
        def body(k, acc):
            acc = list(acc)
            for i in range(4):
                r = k * 4 + i
                hit = two_at == jnp.where(upper, r, r + half)
                for c in range(len(kinds)):
                    got = take_lanes(jnp.where(upper, row_of(c, r), row_of(c, r + half)), two_lane)
                    acc[c] = jnp.where(hit, got, acc[c])
            return tuple(acc)

        start = tuple(jnp.zeros((8, LANES), kind) for kind in kinds)
        acc = lax.fori_loop(0, half // 4, body, start, unroll=unroll)
        return [
            jnp.where(low_at[:side_rows], got[:side_rows], got[side_rows:]) for got in acc
        ]

    def grain_row(c, r):
        if c < 3:
            cols = pl.ds(pl.multiple_of(r * LANES, LANES), LANES)
            return jnp.broadcast_to(vel_ref[pl.ds(c, 1), cols], (8, LANES))
        return spread_row((drag_ref, mass_ref, cell_ref)[c - 3], r)

    *moving, drag_b, mass_b, cell_b = pick(grain_row, (F32,) * 5 + (jnp.int32,), 8)
    below = 1.0 + TIME_STEP * drag_b
    for c in range(3):
        grain_out[c * side_rows : (c + 1) * side_rows, :] = moving[c] / below
    grain_out[3 * side_rows : 4 * side_rows, :] = TIME_STEP * (drag_b + mass_b) / below
    grain_out[4 * side_rows : 5 * side_rows, :] = cell_b.astype(F32)
    grain_out[5 * side_rows : 6 * side_rows, :] = mass_b
    grain_out[6 * side_rows : 7 * side_rows, :] = bound_all.astype(F32)
    pl.semaphore_wait(barrier, len(others))
    spreading = {}
    for k in others:
        dx, dy = AROUND[k]
        back = AROUND.index((-dx, -dy))
        spreading[back] = pltpu.make_async_remote_copy(
            src_ref=pres_ref,
            dst_ref=pres_in.at[back],
            send_sem=pres_send.at[k],
            recv_sem=pres_recv.at[back],
            device_id=reach(dx, dy),
            device_id_type=pl.DeviceIdType.MESH,
        )
    for copy in spreading.values():
        copy.start()
    flying = exchange(0, lambda g: grain_out, lambda g: grain_in.at[g])
    for load in loads[5:]:
        load.wait()

    def stage_tile(t, carry):
        cols = pl.ds(pl.multiple_of(t * LANES, LANES), LANES)
        base = t * STAGE
        stage[pl.ds(base, 9), :] = frame_ref[:, cols]
        stage[pl.ds(base + 16, 9), :] = block_ref[:, cols]
        stage[pl.ds(base + 32, 3), :] = start_ref[:, cols]
        stage[pl.ds(base + 40, 3), :] = gap_ref[:, cols]
        ends[pl.ds(t * 3, 2), :] = pair_ref[:, cols]
        return carry

    lax.fori_loop(0, tiles, stage_tile, 0, unroll=4)

    def stage_grain(t, carry):
        cols = pl.ds(pl.multiple_of(t * LANES, LANES), LANES)
        vel_s[pl.ds(t * 3, 3), :] = vel_ref[:, cols]
        return carry

    lax.fori_loop(0, own_rows, stage_grain, 0, unroll=4)

    def place(u, carry):
        tile = u * 8 + row_iota
        for e in range(2):
            slot = ends[pl.ds(u * 24 + 1 - e, 8, stride=3), :]
            own = slot < own_slots
            near = (slot - HALF * tile) & (own_slots - 1)
            far = (slot - own_slots - HALF * (tile >> 2)) & (ghost_slots - 1)
            rel = jnp.where(own, near, far)
            at = pl.ds(pl.multiple_of(e * tiles + u * 8, 8), 8)
            codes[at, :] = jnp.where(own, 0, 4) + (rel >> 6)
            lanes_s[at, :] = rel & (LANES - 1)
            spots[at, :] = (rel & (HALF - 1)).astype(F32)
        return carry

    lax.fori_loop(0, tiles // 8, place, 0, unroll=2)

    hot_iota = lax.broadcasted_iota(jnp.int32, (LANES, LANES), 0)
    row_hot = lax.broadcasted_iota(jnp.int32, (own_rows, LANES), 0)
    for q in range(side_rows):
        cols = slice(q * LANES, (q + 1) * LANES)
        bound_hot[:, cols] = jnp.where(hot_iota == bound_lane[q : q + 1], 1.0, 0.0).astype(BF16)
        bound_row[:, cols] = jnp.where(row_hot == bound_at[q : q + 1], 1.0, 0.0).astype(BF16)

    def spread_halves(ref, first, value):
        rows = value.shape[0]
        turned = pltpu.roll(value, HALF, 1)
        after = jnp.concatenate([turned[1:], turned[:1]], axis=0)
        first_half = lax.broadcasted_iota(jnp.int32, value.shape, 1) < HALF
        ref[pl.ds(first, rows, stride=2), :] = value
        ref[pl.ds(first + 1, rows, stride=2), :] = jnp.where(first_half, turned, after)

    def spread_current(c, value):
        spread_halves(ext, c * ext_rows, value)
        ext[pl.ds(c * ext_rows + 2 * own_rows, 8), :] = ext[pl.ds(c * ext_rows, 8), :]

    iotas = [
        (lax.broadcasted_iota(jnp.int32, (16, LANES), 0) + 16 * q).astype(F32).astype(BF16)
        for q in range(HALF // 16)
    ]
    signs = [jnp.full((16, LANES), sign, BF16) for sign in (1.0, -1.0)]
    zero16 = jnp.zeros((16, LANES), BF16)

    def build(t, carry):
        for e in range(2):
            row = jnp.broadcast_to(spots[pl.ds(e * tiles + t, 1), :], (16, LANES)).astype(BF16)
            for q in range(HALF // 16):
                at = slice(e * HALF + 16 * q, e * HALF + 16 * (q + 1))
                table[t, at, :] = jnp.where(iotas[q] == row, signs[e], zero16)
        return carry

    lax.fori_loop(0, tiles, build, 0, unroll=4)
    for i in range(64):
        left[i * PITCH + 36 : i * PITCH + ROWS, :] = jnp.zeros((12, LANES), F32)

    for k in range(4):
        spreading[k].wait_recv()
    even = (lax.broadcasted_iota(jnp.int32, (cell_rows, LANES), 0) & 1) == 0
    up1 = lambda a: jnp.concatenate([a[1:], a[:1]], axis=0)
    down1 = lambda a: jnp.concatenate([a[-1:], a[:-1]], axis=0)
    turn = lambda a, n: pltpu.roll(a, n % LANES, 1)
    none = jnp.zeros((2, LANES), F32)

    def pres_at(dx, dy):
        if dx % nx == 0 and dy % ny == 0:
            return p
        return pres_in[AROUND.index((dx, dy))]

    def slopes(ref, first, dx, dy):
        mid = pres_at(dx, dy)
        prev_x, next_x = pres_at(dx - 1, dy), pres_at(dx + 1, dy)
        prev_y, next_y = pres_at(dx, dy - 1), pres_at(dx, dy + 1)
        after = turn(mid, -16)
        plus = jnp.where(lane < 112, after, jnp.where(even, up1(after), down1(turn(next_x, -16))))
        before = turn(mid, 16)
        minus = jnp.where(lane >= 16, before, jnp.where(even, up1(turn(prev_x, 16)), down1(before)))
        ref[first : first + cell_rows] = (plus - minus) * 0.5
        plus = jnp.where((lane & 15) < 15, turn(mid, -1), turn(next_y, 15))
        minus = jnp.where((lane & 15) > 0, turn(mid, 1), turn(prev_y, -15))
        ref[first + cell_rows : first + 2 * cell_rows] = (plus - minus) * 0.5
        ref[first + 2 * cell_rows : first + 3 * cell_rows] = (
            jnp.concatenate([mid[2:], none], axis=0) - jnp.concatenate([none, mid[:-2]], axis=0)
        ) * 0.5

    slopes(slope_s, 0, 0, 0)

    def free(k, carry):
        at = pl.ds(pl.multiple_of(k * 8, 8), 8)
        cells = cell_ref[at, :]
        cell_at, cell_lane = cells >> 7, cells & (LANES - 1)
        drag, mass = drag_ref[at, :], mass_ref[at, :]
        for c in range(3):
            slope = jnp.zeros((8, LANES), F32)
            for r in range(cell_rows):
                got = take_lanes(spread_row(slope_s, c * cell_rows + r), cell_lane)
                slope = jnp.where(cell_at == r, got, slope)
            v = vel_s[pl.ds(k * 24 + c, 8, stride=3), :]
            free_s[pl.ds(pl.multiple_of(c * own_rows + k * 8, 8), 8), :] = (
                v - TIME_STEP * (drag + mass) * slope
            ) / (1.0 + TIME_STEP * drag)
        return carry

    lax.fori_loop(0, own_rows // 8, free, 0, unroll=8)
    for c in range(3):
        spread_current(c, free_s[c * own_rows : (c + 1) * own_rows, :])
    for k in others[4:]:
        spreading[k].wait_recv()
    sent.extend(spreading.values())
    finish(flying)
    for g in range(4):
        slopes(slope_n, 3 * cell_rows * g, *NEAR[g])
    ghost_free = [[], [], []]
    for g in (0, 2):
        both = [
            jnp.concatenate(
                [grain_in[g + i, k * side_rows : (k + 1) * side_rows, :] for i in range(2)], axis=0
            )
            for k in range(5)
        ]
        cells = both[4].astype(jnp.int32)
        cell_at, cell_lane = cells >> 7, cells & (LANES - 1)
        for c in range(3):
            slope = jnp.zeros((8, LANES), F32)
            for r in range(cell_rows):
                first = (3 * g + c) * cell_rows + r
                row = jnp.where(
                    row_iota < side_rows,
                    spread_row(slope_n, first),
                    spread_row(slope_n, first + 3 * cell_rows),
                )
                slope = jnp.where(cell_at == r, take_lanes(row, cell_lane), slope)
            ghost_free[c].append(both[c] - both[3] * slope)
    for c in range(3):
        spread_halves(ghost_s, c * gpad, jnp.concatenate(ghost_free[c], axis=0))

    split[...] = jnp.zeros(split.shape, F32)
    nt = (((1,), (1,)), ((), ()))
    for sweep in range(SWEEPS):
        def contacts(u, odd):
            at = pl.ds(pl.multiple_of(u * 8, 8), 8)
            code, lanes = [], []
            for e in range(2):
                end_at = pl.ds(pl.multiple_of(e * tiles + u * 8, 8), 8)
                code.append(codes[end_at, :])
                lanes.append(lanes_s[end_at, :])
            relative = []
            for c in range(3):
                near = ext[pl.ds(c * ext_rows + u * 8, 8), :]
                next_ = ext[pl.ds(c * ext_rows + u * 8 + 2, 8), :]
                far = jnp.where(
                    row_iota < 4,
                    spread_row(ghost_s, c * gpad + 2 * u),
                    spread_row(ghost_s, c * gpad + 2 * u + 1),
                )
                ends_val = []
                for e in range(2):
                    val = jnp.where(
                        code[e] < 4, take_lanes(next_, lanes[e]), take_lanes(far, lanes[e])
                    )
                    ends_val.append(jnp.where(code[e] < 2, take_lanes(near, lanes[e]), val))
                relative.append(ends_val[0] - ends_val[1])
            part = lambda k: stage[pl.ds(u * (8 * STAGE) + k, 8, stride=STAGE), :]
            fr = [part(k) for k in range(9)]
            target = [
                fr[3 * m] * relative[0]
                + fr[3 * m + 1] * relative[1]
                + fr[3 * m + 2] * relative[2]
                + part(40 + m)
                for m in range(3)
            ]
            trial = []
            for k in range(3):
                before = part(32 + k)
                trial.append(
                    before
                    - (
                        part(16 + 3 * k) * target[0]
                        + part(17 + 3 * k) * target[1]
                        + part(18 + 3 * k) * target[2]
                    )
                )
            active = mask_ref[at, :].astype(F32)
            normal = jnp.maximum(trial[0], 0.0)
            tangent = jnp.sqrt(trial[1] * trial[1] + trial[2] * trial[2])
            factor = jnp.minimum(1.0, FRICTION * normal / jnp.maximum(tangent, FLOOR_VALUE))
            imp = [normal * active, factor * trial[1] * active, factor * trial[2] * active]
            for k in range(3):
                stage[pl.ds(u * (8 * STAGE) + 32 + k, 8, stride=STAGE), :] = imp[k]
            pushes = [fr[c] * imp[0] + fr[3 + c] * imp[1] + fr[6 + c] * imp[2] for c in range(3)]
            if sweep < SWEEPS - 1:
                scatter(u, odd, code, pushes, range(6))
                return
            for c in range(3):
                push_s[c, at, :] = pushes[c]
            scatter(u, odd, code, pushes, (4, 5))

        def scatter(u, odd, code, pushes, blocks):
            rows = -(-len(blocks) * 6 // 16) * 16
            for c in range(3):
                high = pushes[c].astype(BF16).astype(F32)
                for s, term in enumerate((high, pushes[c] - high)):
                    for e in range(2):
                        for n, h in enumerate(blocks):
                            left[
                                pl.ds((e * 8 + odd) * PITCH + (n * 3 + c) * 2 + s, 8, stride=PITCH), :
                            ] = jnp.where(code[e] == h, term, 0.0)
            ghost_sum = None
            for i in range(8):
                got = lax.dot_general(
                    jnp.concatenate(
                        [
                            left[first : first + rows, :].astype(BF16)
                            for first in ((odd + i) * PITCH, (odd + i + 8) * PITCH)
                        ],
                        axis=1,
                    ),
                    jnp.concatenate(
                        [
                            table[u * 8 + i, e * HALF : (e + 1) * HALF, :]
                            for e in range(2)
                        ],
                        axis=1,
                    ),
                    nt,
                    preferred_element_type=F32,
                )
                if 0 in blocks:
                    at = ((i & 1) * own_part + u * 4 + (i >> 1) + 2) * OWN_PITCH
                    sums[pl.ds(at, 24), 0:HALF] = got[0:24]
                if 5 in blocks:
                    far = 6 * (len(blocks) - 2)
                    got = got[far : far + 16]
                    ghost_sum = got if i % 4 == 0 else ghost_sum + got
                    if i % 4 == 3:
                        at = ((i >> 2) * ghost_part + u + 1) * GHOST_PITCH
                        ghost_sums[pl.ds(at, 16), 0:HALF] = ghost_sum

        def own_scatter(u, odd):
            at = pl.ds(pl.multiple_of(u * 8, 8), 8)
            code = [codes[pl.ds(pl.multiple_of(e * tiles + u * 8, 8), 8), :] for e in range(2)]
            scatter(u, odd, code, [push_s[c, at, :] for c in range(3)], range(4))

        def own_two(k, carry):
            for i in range(4):
                own_scatter(4 * k + i, 16 * i)
            return carry

        def two(k, carry):
            for i in range(4):
                contacts(4 * k + i, 16 * i)
            return carry

        lax.fori_loop(0, tiles // 32, two, 0, unroll=4)
        for par in range(2):
            base = par * ghost_part * GHOST_PITCH
            ghost_sums[base : base + GHOST_PITCH, :] = ghost_sums[
                base + ghost_rows * GHOST_PITCH : base + (ghost_rows + 1) * GHOST_PITCH, :
            ]
        first_half = lax.broadcasted_iota(jnp.int32, (8, LANES), 1) < HALF

        def gather_halves(ref, part_rows, pitch, pad, r, terms):
            halves = []
            for par in range(2):
                total = None
                for h, row in terms:
                    for s in range(2):
                        block = par - h
                        first = ((block & 1) * part_rows + r + (block >> 1) + pad) * pitch + row + s
                        got = ref[pl.ds(first, 8, stride=pitch), :]
                        total = got if total is None else total + got
                halves.append(total)
            return jnp.where(first_half, halves[0], pltpu.roll(halves[1], HALF, 1))

        for c in range(3):
            for r in range(0, ghost_rows, 8):
                terms = [(h, h * 6 + c * 2) for h in range(2)]
                total = gather_halves(ghost_sums, ghost_part, GHOST_PITCH, 1, r, terms)
                for i in range(0, 8, side_rows):
                    for slot, group in enumerate(ORDER):
                        if group == (r + i) // side_rows:
                            sum_out[sweep, slot, c * side_rows : (c + 1) * side_rows, :] = total[
                                i : i + side_rows
                            ]
        flying = exchange(
            1 + 2 * sweep,
            lambda g: sum_out.at[sweep, ORDER.index(g)],
            lambda g: sum_in.at[sweep, g],
        )
        distant = {}
        if sweep < SWEEPS - 1:
            for k in others[4:]:
                dx, dy = AROUND[k]
                back = AROUND.index((-dx, -dy))
                count = 1 if k < 8 else 2
                distant[back] = pltpu.make_async_remote_copy(
                    src_ref=sum_out.at[sweep, pl.ds(FIRST[dx, dy], count)],
                    dst_ref=far_in.at[sweep, back - 4, pl.ds(0, count)],
                    send_sem=far_send.at[sweep, k - 4],
                    recv_sem=far_recv.at[sweep, back - 4],
                    device_id=reach(dx, dy),
                    device_id_type=pl.DeviceIdType.MESH,
                )
            for copy in distant.values():
                copy.start()
        if sweep == SWEEPS - 1:
            lax.fori_loop(0, tiles // 32, own_two, 0, unroll=2)
        for par in range(2):
            base = par * own_part * OWN_PITCH
            sums[base : base + 2 * OWN_PITCH, :] = sums[
                base + own_rows * OWN_PITCH : base + (own_rows + 2) * OWN_PITCH, :
            ]
        own_total = []
        for c in range(3):
            parts = []
            for r in range(0, own_rows, 8):
                terms = [(h, h * 6 + c * 2) for h in range(4)]
                parts.append(gather_halves(sums, own_part, OWN_PITCH, 2, r, terms))
            own_total.append(jnp.concatenate(parts, axis=0))
        mass = mass_ref[...]
        for c in range(3):
            rows = slice(c * own_rows, (c + 1) * own_rows)
            part_s[rows, :] = free_s[rows, :] + mass * own_total[c]
        if sweep < SWEEPS - 1:
            got = pick(lambda c, r: spread_row(part_s, c * own_rows + r), (F32,) * 3, 8)
            for c in range(3):
                ghost_out[sweep, c * side_rows : (c + 1) * side_rows, :] = got[c]
            bases = exchange(
                2 + 2 * sweep, lambda g: ghost_out.at[sweep], lambda g: ghost_in.at[sweep, g]
            )
            if sweep == 0:
                for g in range(4):
                    list_in = grain_in[g, 6 * side_rows : 7 * side_rows, :]
                    for a in range(side_rows):
                        down = jnp.broadcast_to(list_in[a : a + 1], (LANES, LANES)).T
                        for b in range(side_rows):
                            same[g, b, a * LANES : (a + 1) * LANES, :] = jnp.where(
                                down == list_in[b : b + 1], 1.0, 0.0
                            ).astype(BF16)
        if sweep == SWEEPS - 1:

            def unstage(t, carry):
                cols = pl.ds(pl.multiple_of(t * LANES, LANES), LANES)
                out_imp[:, cols] = stage[pl.ds(t * STAGE + 32, 3), :]
                return carry

            lax.fori_loop(0, tiles, unstage, 0, unroll=8)
        finish(flying)
        received = (
            sum_in[sweep, 0] + sum_in[sweep, 1] + sum_in[sweep, 2] + sum_in[sweep, 3]
        )
        high = received.astype(BF16).astype(F32)
        low = received - high
        rows = [
            jnp.concatenate(
                [
                    bound_row[:, q * LANES : (q + 1) * LANES]
                    * jnp.broadcast_to(
                        term[c * side_rows + q : c * side_rows + q + 1], (own_rows, LANES)
                    ).astype(BF16)
                    for q in range(side_rows)
                ],
                axis=1,
            )
            for c in range(3)
            for term in (high, low)
        ]
        got = lax.dot_general(
            jnp.concatenate(rows, axis=0), bound_hot[...], nt, preferred_element_type=F32
        )
        for c in range(3):
            first = 2 * c * own_rows
            total = got[first : first + own_rows] + got[first + own_rows : first + 2 * own_rows]
            current = part_s[c * own_rows : (c + 1) * own_rows, :] + mass * total
            if sweep < SWEEPS - 1:
                spread_current(c, current)
            else:
                vel_s[pl.ds(c, own_rows, stride=3), :] = current
        if sweep < SWEEPS - 1:
            for copy in distant.values():
                copy.wait_recv()
            sent.extend(distant.values())

            def sum_of(dx, dy, group):
                if dx % nx == 0 and dy % ny == 0:
                    return sum_out[sweep, ORDER.index(group)]
                at = AROUND.index((dx, dy)) - 4
                return far_in[sweep, at, int(ORDER[FIRST[-dx, -dy]] != group)]

            for g in range(4):
                total = None
                for d in range(4):
                    dx, dy = NEAR[g][0] + NEAR[d][0], NEAR[g][1] + NEAR[d][1]
                    got = sum_of(dx, dy, d ^ 1)
                    total = got if total is None else total + got
                high = total.astype(BF16).astype(F32)
                split[g, 0 : 3 * side_rows, :] = high
                split[g, 3 * side_rows : 6 * side_rows, :] = total - high
                rows = jnp.concatenate(
                    [split[g, pl.ds(q, 16, stride=side_rows), :] for q in range(side_rows)], axis=1
                ).astype(BF16)
                got = jnp.dot(
                    rows,
                    jnp.concatenate([same[g, q] for q in range(side_rows)], axis=1),
                    preferred_element_type=F32,
                )
                for q in range(side_rows):
                    joined[g, q * 9 : q * 9 + 8, :] = got[0:8, q * LANES : (q + 1) * LANES]
            finish(bases)
            for c in range(3):
                ghosts = []
                for g in range(4):
                    more = (
                        joined[g, pl.ds(c, side_rows, stride=9), :]
                        + joined[g, pl.ds(3 + c, side_rows, stride=9), :]
                    )
                    ghosts.append(
                        ghost_in[sweep, g, c * side_rows : (c + 1) * side_rows, :]
                        + grain_in[g, 5 * side_rows : 6 * side_rows, :] * more
                    )
                spread_halves(ghost_s, c * gpad, jnp.concatenate(ghosts, axis=0))

    def unstage_grain(t, carry):
        cols = pl.ds(pl.multiple_of(t * LANES, LANES), LANES)
        out_vel[:, cols] = vel_s[pl.ds(t * 3, 3), :]
        return carry

    lax.fori_loop(0, own_rows, unstage_grain, 0, unroll=8)
    for copy in sent:
        copy.wait_send()


def hand_on(vel_in, imp_in, vel_out, imp_out, sem):
    copies = [
        pltpu.make_async_copy(imp_in, imp_out, sem.at[0]),
        pltpu.make_async_copy(vel_in, vel_out, sem.at[1]),
    ]
    for copy in copies:
        copy.start()
    for copy in copies:
        copy.wait()


def solution(mesh):
    sizes = (mesh.shape["gx"], mesh.shape["gy"])

    def local(
        velocity, inv_mass, drag, grain_cell, boundary_list, contact_pair, frames, blocks,
        impulse_start, gap, contact_mask, pressure,
    ):
        own_rows = velocity.shape[1] // LANES
        tiles = contact_pair.shape[1] // LANES
        side_rows = boundary_list.shape[0] // LANES
        cell_rows = pressure.size // LANES
        gpad = 8 * side_rows
        rounds = 2 * SWEEPS
        out_vel, out_imp = pl.pallas_call(
            lambda *refs: step_kernel(sizes, *refs),
            out_shape=(pltpu.VMEM(velocity.shape, F32), pltpu.VMEM(impulse_start.shape, F32)),
            in_specs=[pl.BlockSpec(memory_space=pltpu.HBM)] * 12,
            out_specs=(pl.BlockSpec(memory_space=pltpu.VMEM),) * 2,
            scratch_shapes=[
                pltpu.VMEM((3, velocity.shape[1]), F32),
                pltpu.VMEM((own_rows, LANES), F32),
                pltpu.VMEM((own_rows, LANES), F32),
                pltpu.VMEM((own_rows, LANES), jnp.int32),
                pltpu.VMEM((side_rows, LANES), jnp.int32),
                pltpu.VMEM((2, contact_pair.shape[1]), jnp.int32),
                pltpu.VMEM((9, contact_pair.shape[1]), F32),
                pltpu.VMEM((9, contact_pair.shape[1]), F32),
                pltpu.VMEM((3, contact_pair.shape[1]), F32),
                pltpu.VMEM((3, contact_pair.shape[1]), F32),
                pltpu.VMEM((tiles, LANES), jnp.int32),
                pltpu.VMEM(pressure.shape, F32),
                pltpu.VMEM((pressure.size // pressure.shape[2], LANES), F32),
                pltpu.VMEM((cell_rows, LANES), F32),
                pltpu.VMEM((12, cell_rows, LANES), F32),
                pltpu.VMEM((4, 7 * side_rows, LANES), F32),
                pltpu.VMEM((7 * side_rows, LANES), F32),
                pltpu.VMEM((SWEEPS - 1, 4, 3 * side_rows, LANES), F32),
                pltpu.VMEM((SWEEPS, 4, 3 * side_rows, LANES), F32),
                pltpu.VMEM((SWEEPS - 1, 8, 2, 3 * side_rows, LANES), F32),
                pltpu.VMEM((SWEEPS - 1, 3 * side_rows, LANES), F32),
                pltpu.VMEM((SWEEPS, 5, 3 * side_rows, LANES), F32),
                pltpu.VMEM((3 * cell_rows, LANES), F32),
                pltpu.VMEM((12 * cell_rows, LANES), F32),
                pltpu.VMEM((own_rows * 3, LANES), F32),
                pltpu.VMEM((3 * own_rows, LANES), F32),
                pltpu.VMEM((tiles * STAGE, LANES), F32),
                pltpu.VMEM((tiles * 3, LANES), jnp.int32),
                pltpu.VMEM((2 * tiles, LANES), jnp.int32),
                pltpu.VMEM((2 * tiles, LANES), jnp.int32),
                pltpu.VMEM((2 * tiles, LANES), F32),
                pltpu.VMEM((tiles, LANES, LANES), BF16),
                pltpu.VMEM((3 * (2 * own_rows + 8), LANES), F32),
                pltpu.VMEM((3 * gpad, LANES), F32),
                pltpu.VMEM((64 * PITCH, LANES), F32),
                pltpu.VMEM((2 * (own_rows + 2) * OWN_PITCH, LANES), F32),
                pltpu.VMEM((2 * (4 * side_rows + 1) * GHOST_PITCH, LANES), F32),
                pltpu.VMEM((LANES, side_rows * LANES), BF16),
                pltpu.VMEM((own_rows, side_rows * LANES), BF16),
                pltpu.VMEM((3 * own_rows, LANES), F32),
                pltpu.VMEM((3, tiles, LANES), F32),
                pltpu.VMEM((4, side_rows, side_rows * LANES, LANES), BF16),
                pltpu.VMEM((4, 16 * side_rows, LANES), F32),
                pltpu.VMEM((4, 9 * side_rows, LANES), F32),
                pltpu.SemaphoreType.DMA((rounds, 4)),
                pltpu.SemaphoreType.DMA((rounds, 4)),
                pltpu.SemaphoreType.DMA((12,)),
                pltpu.SemaphoreType.DMA((12,)),
                pltpu.SemaphoreType.DMA((SWEEPS - 1, 8)),
                pltpu.SemaphoreType.DMA((SWEEPS - 1, 8)),
                pltpu.SemaphoreType.DMA((12,)),
            ],
            compiler_params=pltpu.CompilerParams(
                collective_id=0, has_side_effects=True, vmem_limit_bytes=60 * 1024 * 1024
            ),
        )(
            velocity,
            inv_mass.reshape(own_rows, LANES),
            drag.reshape(own_rows, LANES),
            grain_cell.reshape(own_rows, LANES),
            boundary_list.reshape(side_rows, LANES),
            contact_pair,
            frames,
            blocks,
            impulse_start,
            gap,
            contact_mask.reshape(tiles, LANES),
            pressure,
        )
        return pl.pallas_call(
            hand_on,
            out_shape=(
                jax.ShapeDtypeStruct(velocity.shape, F32),
                jax.ShapeDtypeStruct(impulse_start.shape, F32),
            ),
            in_specs=[pl.BlockSpec(memory_space=pl.ANY)] * 2,
            out_specs=(pl.BlockSpec(memory_space=pltpu.HBM),) * 2,
            scratch_shapes=[pltpu.SemaphoreType.DMA((2,))],
        )(
            pltpu.with_memory_space_constraint(out_vel, pltpu.VMEM),
            pltpu.with_memory_space_constraint(out_imp, pltpu.VMEM),
        )

    grains, lists = P(("gx", "gy")), P(None, ("gx", "gy"))
    return jax.shard_map(
        local,
        mesh=mesh,
        in_specs=(
            lists, grains, grains, grains, grains, lists, lists, lists, lists, lists, grains,
            P(None, "gx", "gy"),
        ),
        out_specs=(lists, lists),
        check_vma=False,
    )
```

```python
import jax
import jax.numpy as jnp
from jax import lax
from jax.experimental import pallas as pl
from jax.experimental.pallas import tpu as pltpu
from jax.sharding import PartitionSpec as P

SWEEPS = 2
TIME_STEP = 0.5
FRICTION = 0.5
FLOOR_VALUE = 0.1
LANES = 128
HALF = LANES // 2
ROWS = 48
PITCH = 49
STAGE = 49
OWN_PITCH = 25
GHOST_PITCH = 17
F32 = jnp.float32
BF16 = jnp.bfloat16
NEAR = ((-1, 0), (1, 0), (0, -1), (0, 1))
FAR = ((-2, 0), (2, 0), (0, -2), (0, 2), (-1, -1), (-1, 1), (1, -1), (1, 1))
AROUND = NEAR + FAR
ORDER = (0, 2, 1, 3, 0)
FIRST = {(-1, -1): 0, (1, -1): 1, (1, 1): 2, (-1, 1): 3, (-2, 0): 0, (0, -2): 1, (2, 0): 2, (0, 2): 3}


def take_lanes(values, lanes):
    return jnp.take_along_axis(values, lanes, axis=1, mode="promise_in_bounds")


def spread_row(ref, row):
    return jnp.broadcast_to(ref[pl.ds(row, 1), :], (8, LANES))


def step_kernel(
    sizes,
    vel_hbm, mass_hbm, drag_hbm, cell_hbm, bound_hbm, pair_hbm, frame_hbm, block_hbm,
    start_hbm, gap_hbm, mask_hbm, pres_hbm,
    out_vel, out_imp,
    vel_ref, mass_ref, drag_ref, cell_ref, bound_ref, pair_ref, frame_ref, block_ref,
    start_ref, gap_ref, mask_ref, pres_raw, pres_wide, pres_ref,
    pres_in, grain_in, grain_out, ghost_in, sum_in, far_in, ghost_out, sum_out,
    slope_s, slope_n, vel_s, free_s, stage, ends, codes, lanes_s, spots, table, ext, ghost_s,
    left, sums, ghost_sums, bound_hot, bound_row, part_s, push_s, same, split, joined,
    send_sem, recv_sem, pres_send, pres_recv, far_send, far_recv, load_sem,
):
    nx, ny = sizes
    tiles = mask_ref.shape[0]
    own_rows = mass_ref.shape[0]
    side_rows = bound_ref.shape[0]
    ghost_rows = 4 * side_rows
    cell_rows = pres_ref.shape[0]
    ext_rows = 2 * own_rows + 8
    gpad = 2 * ghost_rows
    own_slots = own_rows * LANES
    ghost_slots = ghost_rows * LANES
    own_part = own_rows + 2
    ghost_part = ghost_rows + 1
    row_iota = lax.broadcasted_iota(jnp.int32, (8, LANES), 0)

    mx, my = lax.axis_index("gx"), lax.axis_index("gy")
    reach = lambda dx, dy: (lax.rem(mx + dx + 2 * nx, nx), lax.rem(my + dy + 2 * ny, ny))
    sides = [reach(dx, dy) for dx, dy in NEAR]
    others = [k for k, (dx, dy) in enumerate(AROUND) if dx % nx or dy % ny]

    loads = [
        pltpu.make_async_copy(source, target, load_sem.at[k])
        for k, (source, target) in enumerate(
            (
                (vel_hbm, vel_ref), (bound_hbm, bound_ref), (drag_hbm, drag_ref),
                (mass_hbm, mass_ref), (cell_hbm, cell_ref), (pair_hbm, pair_ref),
                (mask_hbm, mask_ref), (start_hbm, start_ref), (gap_hbm, gap_ref),
                (frame_hbm, frame_ref), (block_hbm, block_ref),
            )
        )
    ]
    pres_load = pltpu.make_async_copy(pres_hbm, pres_raw, load_sem.at[11])
    pres_load.start()
    for load in loads:
        load.start()

    barrier = pltpu.get_barrier_semaphore()
    for k in others:
        pl.semaphore_signal(
            barrier, inc=1, device_id=reach(*AROUND[k]), device_id_type=pl.DeviceIdType.MESH
        )

    lane = lax.broadcasted_iota(jnp.int32, (cell_rows, LANES), 1)
    pres_load.wait()
    width = pres_raw.shape[2]
    pres_wide[:, 0:width] = pres_raw[...].reshape(-1, width)
    per_row = LANES // width
    p = pres_wide[pl.ds(0, cell_rows, stride=per_row), :]
    for k in range(1, per_row):
        piece = pltpu.roll(pres_wide[pl.ds(k, cell_rows, stride=per_row), :], k * width, 1)
        p = jnp.where(lane < k * width, p, piece)
    pres_ref[...] = p
    def exchange(step, source, target):
        copies = []
        for g in range(4):
            copies.append(
                pltpu.make_async_remote_copy(
                    src_ref=source(g),
                    dst_ref=target(g ^ 1),
                    send_sem=send_sem.at[step, g],
                    recv_sem=recv_sem.at[step, g ^ 1],
                    device_id=sides[g],
                    device_id_type=pl.DeviceIdType.MESH,
                )
            )
        for copy in copies:
            copy.start()
        return copies

    sent = []

    def finish(copies):
        for copy in copies:
            copy.wait_recv()
        sent.extend(copies)

    for load in loads[:5]:
        load.wait()
    bound_all = bound_ref[...]
    bound_lane = bound_all & (LANES - 1)
    bound_at = bound_all >> 7
    two_lane = jnp.concatenate([bound_lane, bound_lane], axis=0)
    two_at = jnp.concatenate([bound_at, bound_at], axis=0)
    half = own_rows // 2
    upper = row_iota < side_rows
    low_at = two_at < half

    def pick(row_of, kinds, unroll):
        def body(k, acc):
            acc = list(acc)
            for i in range(4):
                r = k * 4 + i
                hit = two_at == jnp.where(upper, r, r + half)
                for c in range(len(kinds)):
                    got = take_lanes(jnp.where(upper, row_of(c, r), row_of(c, r + half)), two_lane)
                    acc[c] = jnp.where(hit, got, acc[c])
            return tuple(acc)

        start = tuple(jnp.zeros((8, LANES), kind) for kind in kinds)
        acc = lax.fori_loop(0, half // 4, body, start, unroll=unroll)
        return [
            jnp.where(low_at[:side_rows], got[:side_rows], got[side_rows:]) for got in acc
        ]

    def grain_row(c, r):
        if c < 3:
            cols = pl.ds(pl.multiple_of(r * LANES, LANES), LANES)
            return jnp.broadcast_to(vel_ref[pl.ds(c, 1), cols], (8, LANES))
        return spread_row((drag_ref, mass_ref, cell_ref)[c - 3], r)

    *moving, drag_b, mass_b, cell_b = pick(grain_row, (F32,) * 5 + (jnp.int32,), 8)
    below = 1.0 + TIME_STEP * drag_b
    for c in range(3):
        grain_out[c * side_rows : (c + 1) * side_rows, :] = moving[c] / below
    grain_out[3 * side_rows : 4 * side_rows, :] = TIME_STEP * (drag_b + mass_b) / below
    grain_out[4 * side_rows : 5 * side_rows, :] = cell_b.astype(F32)
    grain_out[5 * side_rows : 6 * side_rows, :] = mass_b
    grain_out[6 * side_rows : 7 * side_rows, :] = bound_all.astype(F32)
    pl.semaphore_wait(barrier, len(others))
    spreading = {}
    for k in others:
        dx, dy = AROUND[k]
        back = AROUND.index((-dx, -dy))
        spreading[back] = pltpu.make_async_remote_copy(
            src_ref=pres_ref,
            dst_ref=pres_in.at[back],
            send_sem=pres_send.at[k],
            recv_sem=pres_recv.at[back],
            device_id=reach(dx, dy),
            device_id_type=pl.DeviceIdType.MESH,
        )
    for copy in spreading.values():
        copy.start()
    flying = exchange(0, lambda g: grain_out, lambda g: grain_in.at[g])
    for load in loads[5:]:
        load.wait()

    def stage_tile(t, carry):
        cols = pl.ds(pl.multiple_of(t * LANES, LANES), LANES)
        base = t * STAGE
        stage[pl.ds(base, 9), :] = frame_ref[:, cols]
        stage[pl.ds(base + 16, 9), :] = block_ref[:, cols]
        stage[pl.ds(base + 32, 3), :] = start_ref[:, cols]
        stage[pl.ds(base + 40, 3), :] = gap_ref[:, cols]
        ends[pl.ds(t * 3, 2), :] = pair_ref[:, cols]
        return carry

    lax.fori_loop(0, tiles, stage_tile, 0, unroll=4)

    def stage_grain(t, carry):
        cols = pl.ds(pl.multiple_of(t * LANES, LANES), LANES)
        vel_s[pl.ds(t * 3, 3), :] = vel_ref[:, cols]
        return carry

    lax.fori_loop(0, own_rows, stage_grain, 0, unroll=4)

    def place(u, carry):
        tile = u * 8 + row_iota
        for e in range(2):
            slot = ends[pl.ds(u * 24 + 1 - e, 8, stride=3), :]
            own = slot < own_slots
            near = (slot - HALF * tile) & (own_slots - 1)
            far = (slot - own_slots - HALF * (tile >> 2)) & (ghost_slots - 1)
            rel = jnp.where(own, near, far)
            at = pl.ds(pl.multiple_of(e * tiles + u * 8, 8), 8)
            codes[at, :] = jnp.where(own, 0, 4) + (rel >> 6)
            lanes_s[at, :] = rel & (LANES - 1)
            spots[at, :] = (rel & (HALF - 1)).astype(F32)
        return carry

    lax.fori_loop(0, tiles // 8, place, 0, unroll=2)

    hot_iota = lax.broadcasted_iota(jnp.int32, (LANES, LANES), 0)
    row_hot = lax.broadcasted_iota(jnp.int32, (own_rows, LANES), 0)
    for q in range(side_rows):
        cols = slice(q * LANES, (q + 1) * LANES)
        bound_hot[:, cols] = jnp.where(hot_iota == bound_lane[q : q + 1], 1.0, 0.0).astype(BF16)
        bound_row[:, cols] = jnp.where(row_hot == bound_at[q : q + 1], 1.0, 0.0).astype(BF16)

    def spread_halves(ref, first, value):
        rows = value.shape[0]
        turned = pltpu.roll(value, HALF, 1)
        after = jnp.concatenate([turned[1:], turned[:1]], axis=0)
        first_half = lax.broadcasted_iota(jnp.int32, value.shape, 1) < HALF
        ref[pl.ds(first, rows, stride=2), :] = value
        ref[pl.ds(first + 1, rows, stride=2), :] = jnp.where(first_half, turned, after)

    def spread_current(c, value):
        spread_halves(ext, c * ext_rows, value)
        ext[pl.ds(c * ext_rows + 2 * own_rows, 8), :] = ext[pl.ds(c * ext_rows, 8), :]

    iotas = [
        (lax.broadcasted_iota(jnp.int32, (16, LANES), 0) + 16 * q).astype(F32).astype(BF16)
        for q in range(HALF // 16)
    ]
    signs = [jnp.full((16, LANES), sign, BF16) for sign in (1.0, -1.0)]
    zero16 = jnp.zeros((16, LANES), BF16)

    def build(t, carry):
        for e in range(2):
            row = jnp.broadcast_to(spots[pl.ds(e * tiles + t, 1), :], (16, LANES)).astype(BF16)
            for q in range(HALF // 16):
                at = slice(e * HALF + 16 * q, e * HALF + 16 * (q + 1))
                table[t, at, :] = jnp.where(iotas[q] == row, signs[e], zero16)
        return carry

    lax.fori_loop(0, tiles, build, 0, unroll=4)
    for i in range(64):
        left[i * PITCH + 36 : i * PITCH + ROWS, :] = jnp.zeros((12, LANES), F32)

    even = (lax.broadcasted_iota(jnp.int32, (cell_rows, LANES), 0) & 1) == 0
    up1 = lambda a: jnp.concatenate([a[1:], a[:1]], axis=0)
    down1 = lambda a: jnp.concatenate([a[-1:], a[:-1]], axis=0)
    turn = lambda a, n: pltpu.roll(a, n % LANES, 1)
    none = jnp.zeros((2, LANES), F32)

    def pres_at(dx, dy):
        if dx % nx == 0 and dy % ny == 0:
            return p
        return pres_in[AROUND.index((dx, dy))]

    def slope(c, dx, dy):
        mid = pres_at(dx, dy)
        if c == 0:
            prev_x, next_x = pres_at(dx - 1, dy), pres_at(dx + 1, dy)
            after, before = turn(mid, -16), turn(mid, 16)
            plus = jnp.where(
                lane < 112, after, jnp.where(even, up1(after), down1(turn(next_x, -16)))
            )
            minus = jnp.where(
                lane >= 16, before, jnp.where(even, up1(turn(prev_x, 16)), down1(before))
            )
        elif c == 1:
            prev_y, next_y = pres_at(dx, dy - 1), pres_at(dx, dy + 1)
            plus = jnp.where((lane & 15) < 15, turn(mid, -1), turn(next_y, 15))
            minus = jnp.where((lane & 15) > 0, turn(mid, 1), turn(prev_y, -15))
        else:
            plus = jnp.concatenate([mid[2:], none], axis=0)
            minus = jnp.concatenate([none, mid[:-2]], axis=0)
        return (plus - minus) * 0.5

    for c, needs in ((2, ()), (1, (2, 3)), (0, (0, 1))):
        for k in needs:
            spreading[k].wait_recv()
        slope_s[...] = slope(c, 0, 0)

        def free(k, carry):
            at = pl.ds(pl.multiple_of(k * 8, 8), 8)
            cells = cell_ref[at, :]
            cell_at, cell_lane = cells >> 7, cells & (LANES - 1)
            drag, mass = drag_ref[at, :], mass_ref[at, :]
            got = jnp.zeros((8, LANES), F32)
            for r in range(cell_rows):
                row = take_lanes(spread_row(slope_s, r), cell_lane)
                got = jnp.where(cell_at == r, row, got)
            v = vel_s[pl.ds(k * 24 + c, 8, stride=3), :]
            free_s[pl.ds(pl.multiple_of(c * own_rows + k * 8, 8), 8), :] = (
                v - TIME_STEP * (drag + mass) * got
            ) / (1.0 + TIME_STEP * drag)
            return carry

        lax.fori_loop(0, own_rows // 8, free, 0, unroll=8)
        spread_current(c, free_s[c * own_rows : (c + 1) * own_rows, :])
    for k in others[4:]:
        spreading[k].wait_recv()
    sent.extend(spreading.values())
    finish(flying)
    for g in range(4):
        for c in range(3):
            first = (3 * g + c) * cell_rows
            slope_n[first : first + cell_rows, :] = slope(c, *NEAR[g])
    ghost_free = [[], [], []]
    for g in (0, 2):
        both = [
            jnp.concatenate(
                [grain_in[g + i, k * side_rows : (k + 1) * side_rows, :] for i in range(2)], axis=0
            )
            for k in range(5)
        ]
        cells = both[4].astype(jnp.int32)
        cell_at, cell_lane = cells >> 7, cells & (LANES - 1)
        for c in range(3):
            here = jnp.zeros((8, LANES), F32)
            for r in range(cell_rows):
                first = (3 * g + c) * cell_rows + r
                row = jnp.where(
                    row_iota < side_rows,
                    spread_row(slope_n, first),
                    spread_row(slope_n, first + 3 * cell_rows),
                )
                here = jnp.where(cell_at == r, take_lanes(row, cell_lane), here)
            ghost_free[c].append(both[c] - both[3] * here)
    for c in range(3):
        spread_halves(ghost_s, c * gpad, jnp.concatenate(ghost_free[c], axis=0))

    split[...] = jnp.zeros(split.shape, F32)
    nt = (((1,), (1,)), ((), ()))
    for sweep in range(SWEEPS):
        def contacts(u, odd):
            at = pl.ds(pl.multiple_of(u * 8, 8), 8)
            code, lanes = [], []
            for e in range(2):
                end_at = pl.ds(pl.multiple_of(e * tiles + u * 8, 8), 8)
                code.append(codes[end_at, :])
                lanes.append(lanes_s[end_at, :])
            relative = []
            for c in range(3):
                near = ext[pl.ds(c * ext_rows + u * 8, 8), :]
                next_ = ext[pl.ds(c * ext_rows + u * 8 + 2, 8), :]
                far = jnp.where(
                    row_iota < 4,
                    spread_row(ghost_s, c * gpad + 2 * u),
                    spread_row(ghost_s, c * gpad + 2 * u + 1),
                )
                ends_val = []
                for e in range(2):
                    val = jnp.where(
                        code[e] < 4, take_lanes(next_, lanes[e]), take_lanes(far, lanes[e])
                    )
                    ends_val.append(jnp.where(code[e] < 2, take_lanes(near, lanes[e]), val))
                relative.append(ends_val[0] - ends_val[1])
            part = lambda k: stage[pl.ds(u * (8 * STAGE) + k, 8, stride=STAGE), :]
            fr = [part(k) for k in range(9)]
            target = [
                fr[3 * m] * relative[0]
                + fr[3 * m + 1] * relative[1]
                + fr[3 * m + 2] * relative[2]
                + part(40 + m)
                for m in range(3)
            ]
            trial = []
            for k in range(3):
                before = part(32 + k)
                trial.append(
                    before
                    - (
                        part(16 + 3 * k) * target[0]
                        + part(17 + 3 * k) * target[1]
                        + part(18 + 3 * k) * target[2]
                    )
                )
            active = mask_ref[at, :].astype(F32)
            normal = jnp.maximum(trial[0], 0.0)
            tangent = jnp.sqrt(trial[1] * trial[1] + trial[2] * trial[2])
            factor = jnp.minimum(1.0, FRICTION * normal / jnp.maximum(tangent, FLOOR_VALUE))
            imp = [normal * active, factor * trial[1] * active, factor * trial[2] * active]
            for k in range(3):
                stage[pl.ds(u * (8 * STAGE) + 32 + k, 8, stride=STAGE), :] = imp[k]
            pushes = [fr[c] * imp[0] + fr[3 + c] * imp[1] + fr[6 + c] * imp[2] for c in range(3)]
            if sweep < SWEEPS - 1:
                scatter(u, odd, code, pushes, range(6))
                return
            for c in range(3):
                push_s[c, at, :] = pushes[c]
            scatter(u, odd, code, pushes, (4, 5))

        def scatter(u, odd, code, pushes, blocks):
            rows = -(-len(blocks) * 6 // 16) * 16
            for c in range(3):
                high = pushes[c].astype(BF16).astype(F32)
                for s, term in enumerate((high, pushes[c] - high)):
                    for e in range(2):
                        for n, h in enumerate(blocks):
                            left[
                                pl.ds((e * 8 + odd) * PITCH + (n * 3 + c) * 2 + s, 8, stride=PITCH), :
                            ] = jnp.where(code[e] == h, term, 0.0)
            ghost_sum = None
            for i in range(8):
                got = lax.dot_general(
                    jnp.concatenate(
                        [
                            left[first : first + rows, :].astype(BF16)
                            for first in ((odd + i) * PITCH, (odd + i + 8) * PITCH)
                        ],
                        axis=1,
                    ),
                    jnp.concatenate(
                        [
                            table[u * 8 + i, e * HALF : (e + 1) * HALF, :]
                            for e in range(2)
                        ],
                        axis=1,
                    ),
                    nt,
                    preferred_element_type=F32,
                )
                if 0 in blocks:
                    at = ((i & 1) * own_part + u * 4 + (i >> 1) + 2) * OWN_PITCH
                    sums[pl.ds(at, 24), 0:HALF] = got[0:24]
                if 5 in blocks:
                    far = 6 * (len(blocks) - 2)
                    got = got[far : far + 16]
                    ghost_sum = got if i % 4 == 0 else ghost_sum + got
                    if i % 4 == 3:
                        at = ((i >> 2) * ghost_part + u + 1) * GHOST_PITCH
                        ghost_sums[pl.ds(at, 16), 0:HALF] = ghost_sum

        def own_scatter(u, odd):
            at = pl.ds(pl.multiple_of(u * 8, 8), 8)
            code = [codes[pl.ds(pl.multiple_of(e * tiles + u * 8, 8), 8), :] for e in range(2)]
            scatter(u, odd, code, [push_s[c, at, :] for c in range(3)], range(4))

        def own_two(k, carry):
            for i in range(4):
                own_scatter(4 * k + i, 16 * i)
            return carry

        def two(k, carry):
            for i in range(4):
                contacts(4 * k + i, 16 * i)
            return carry

        lax.fori_loop(0, tiles // 32, two, 0, unroll=4)
        for par in range(2):
            base = par * ghost_part * GHOST_PITCH
            ghost_sums[base : base + GHOST_PITCH, :] = ghost_sums[
                base + ghost_rows * GHOST_PITCH : base + (ghost_rows + 1) * GHOST_PITCH, :
            ]
        first_half = lax.broadcasted_iota(jnp.int32, (8, LANES), 1) < HALF

        def gather_halves(ref, part_rows, pitch, pad, r, terms):
            halves = []
            for par in range(2):
                total = None
                for h, row in terms:
                    for s in range(2):
                        block = par - h
                        first = ((block & 1) * part_rows + r + (block >> 1) + pad) * pitch + row + s
                        got = ref[pl.ds(first, 8, stride=pitch), :]
                        total = got if total is None else total + got
                halves.append(total)
            return jnp.where(first_half, halves[0], pltpu.roll(halves[1], HALF, 1))

        for c in range(3):
            for r in range(0, ghost_rows, 8):
                terms = [(h, h * 6 + c * 2) for h in range(2)]
                total = gather_halves(ghost_sums, ghost_part, GHOST_PITCH, 1, r, terms)
                for i in range(0, 8, side_rows):
                    for slot, group in enumerate(ORDER):
                        if group == (r + i) // side_rows:
                            sum_out[sweep, slot, c * side_rows : (c + 1) * side_rows, :] = total[
                                i : i + side_rows
                            ]
        flying = exchange(
            1 + 2 * sweep,
            lambda g: sum_out.at[sweep, ORDER.index(g)],
            lambda g: sum_in.at[sweep, g],
        )
        distant = {}
        if sweep < SWEEPS - 1:
            for k in others[4:]:
                dx, dy = AROUND[k]
                back = AROUND.index((-dx, -dy))
                count = 1 if k < 8 else 2
                distant[back] = pltpu.make_async_remote_copy(
                    src_ref=sum_out.at[sweep, pl.ds(FIRST[dx, dy], count)],
                    dst_ref=far_in.at[sweep, back - 4, pl.ds(0, count)],
                    send_sem=far_send.at[sweep, k - 4],
                    recv_sem=far_recv.at[sweep, back - 4],
                    device_id=reach(dx, dy),
                    device_id_type=pl.DeviceIdType.MESH,
                )
            for copy in distant.values():
                copy.start()
        if sweep == SWEEPS - 1:
            lax.fori_loop(0, tiles // 32, own_two, 0, unroll=2)
        for par in range(2):
            base = par * own_part * OWN_PITCH
            sums[base : base + 2 * OWN_PITCH, :] = sums[
                base + own_rows * OWN_PITCH : base + (own_rows + 2) * OWN_PITCH, :
            ]
        own_total = []
        for c in range(3):
            parts = []
            for r in range(0, own_rows, 8):
                terms = [(h, h * 6 + c * 2) for h in range(4)]
                parts.append(gather_halves(sums, own_part, OWN_PITCH, 2, r, terms))
            own_total.append(jnp.concatenate(parts, axis=0))
        mass = mass_ref[...]
        for c in range(3):
            rows = slice(c * own_rows, (c + 1) * own_rows)
            part_s[rows, :] = free_s[rows, :] + mass * own_total[c]
        if sweep < SWEEPS - 1:
            got = pick(lambda c, r: spread_row(part_s, c * own_rows + r), (F32,) * 3, 8)
            for c in range(3):
                ghost_out[sweep, c * side_rows : (c + 1) * side_rows, :] = got[c]
            bases = exchange(
                2 + 2 * sweep, lambda g: ghost_out.at[sweep], lambda g: ghost_in.at[sweep, g]
            )
            if sweep == 0:
                for g in range(4):
                    list_in = grain_in[g, 6 * side_rows : 7 * side_rows, :]
                    for a in range(side_rows):
                        down = jnp.broadcast_to(list_in[a : a + 1], (LANES, LANES)).T
                        for b in range(side_rows):
                            same[g, b, a * LANES : (a + 1) * LANES, :] = jnp.where(
                                down == list_in[b : b + 1], 1.0, 0.0
                            ).astype(BF16)
        if sweep == SWEEPS - 1:

            def unstage(t, carry):
                cols = pl.ds(pl.multiple_of(t * LANES, LANES), LANES)
                out_imp[:, cols] = stage[pl.ds(t * STAGE + 32, 3), :]
                return carry

            lax.fori_loop(0, tiles, unstage, 0, unroll=8)
        finish(flying)
        received = (
            sum_in[sweep, 0] + sum_in[sweep, 1] + sum_in[sweep, 2] + sum_in[sweep, 3]
        )
        high = received.astype(BF16).astype(F32)
        low = received - high
        rows = [
            jnp.concatenate(
                [
                    bound_row[:, q * LANES : (q + 1) * LANES]
                    * jnp.broadcast_to(
                        term[c * side_rows + q : c * side_rows + q + 1], (own_rows, LANES)
                    ).astype(BF16)
                    for q in range(side_rows)
                ],
                axis=1,
            )
            for c in range(3)
            for term in (high, low)
        ]
        got = lax.dot_general(
            jnp.concatenate(rows, axis=0), bound_hot[...], nt, preferred_element_type=F32
        )
        for c in range(3):
            first = 2 * c * own_rows
            total = got[first : first + own_rows] + got[first + own_rows : first + 2 * own_rows]
            current = part_s[c * own_rows : (c + 1) * own_rows, :] + mass * total
            if sweep < SWEEPS - 1:
                spread_current(c, current)
            else:
                vel_s[pl.ds(c, own_rows, stride=3), :] = current
        if sweep < SWEEPS - 1:
            for copy in distant.values():
                copy.wait_recv()
            sent.extend(distant.values())

            def sum_of(dx, dy, group):
                if dx % nx == 0 and dy % ny == 0:
                    return sum_out[sweep, ORDER.index(group)]
                at = AROUND.index((dx, dy)) - 4
                return far_in[sweep, at, int(ORDER[FIRST[-dx, -dy]] != group)]

            for g in range(4):
                total = None
                for d in range(4):
                    dx, dy = NEAR[g][0] + NEAR[d][0], NEAR[g][1] + NEAR[d][1]
                    got = sum_of(dx, dy, d ^ 1)
                    total = got if total is None else total + got
                high = total.astype(BF16).astype(F32)
                split[g, 0 : 3 * side_rows, :] = high
                split[g, 3 * side_rows : 6 * side_rows, :] = total - high
                rows = jnp.concatenate(
                    [split[g, pl.ds(q, 16, stride=side_rows), :] for q in range(side_rows)], axis=1
                ).astype(BF16)
                got = jnp.dot(
                    rows,
                    jnp.concatenate([same[g, q] for q in range(side_rows)], axis=1),
                    preferred_element_type=F32,
                )
                for q in range(side_rows):
                    joined[g, q * 9 : q * 9 + 8, :] = got[0:8, q * LANES : (q + 1) * LANES]
            finish(bases)
            for c in range(3):
                ghosts = []
                for g in range(4):
                    more = (
                        joined[g, pl.ds(c, side_rows, stride=9), :]
                        + joined[g, pl.ds(3 + c, side_rows, stride=9), :]
                    )
                    ghosts.append(
                        ghost_in[sweep, g, c * side_rows : (c + 1) * side_rows, :]
                        + grain_in[g, 5 * side_rows : 6 * side_rows, :] * more
                    )
                spread_halves(ghost_s, c * gpad, jnp.concatenate(ghosts, axis=0))

    def unstage_grain(t, carry):
        cols = pl.ds(pl.multiple_of(t * LANES, LANES), LANES)
        out_vel[:, cols] = vel_s[pl.ds(t * 3, 3), :]
        return carry

    lax.fori_loop(0, own_rows, unstage_grain, 0, unroll=8)
    for copy in sent:
        copy.wait_send()


def hand_on(vel_in, imp_in, vel_out, imp_out, sem):
    copies = [
        pltpu.make_async_copy(imp_in, imp_out, sem.at[0]),
        pltpu.make_async_copy(vel_in, vel_out, sem.at[1]),
    ]
    for copy in copies:
        copy.start()
    for copy in copies:
        copy.wait()


def solution(mesh):
    sizes = (mesh.shape["gx"], mesh.shape["gy"])

    def local(
        velocity, inv_mass, drag, grain_cell, boundary_list, contact_pair, frames, blocks,
        impulse_start, gap, contact_mask, pressure,
    ):
        own_rows = velocity.shape[1] // LANES
        tiles = contact_pair.shape[1] // LANES
        side_rows = boundary_list.shape[0] // LANES
        cell_rows = pressure.size // LANES
        gpad = 8 * side_rows
        rounds = 2 * SWEEPS
        out_vel, out_imp = pl.pallas_call(
            lambda *refs: step_kernel(sizes, *refs),
            out_shape=(pltpu.VMEM(velocity.shape, F32), pltpu.VMEM(impulse_start.shape, F32)),
            in_specs=[pl.BlockSpec(memory_space=pltpu.HBM)] * 12,
            out_specs=(pl.BlockSpec(memory_space=pltpu.VMEM),) * 2,
            scratch_shapes=[
                pltpu.VMEM((3, velocity.shape[1]), F32),
                pltpu.VMEM((own_rows, LANES), F32),
                pltpu.VMEM((own_rows, LANES), F32),
                pltpu.VMEM((own_rows, LANES), jnp.int32),
                pltpu.VMEM((side_rows, LANES), jnp.int32),
                pltpu.VMEM((2, contact_pair.shape[1]), jnp.int32),
                pltpu.VMEM((9, contact_pair.shape[1]), F32),
                pltpu.VMEM((9, contact_pair.shape[1]), F32),
                pltpu.VMEM((3, contact_pair.shape[1]), F32),
                pltpu.VMEM((3, contact_pair.shape[1]), F32),
                pltpu.VMEM((tiles, LANES), jnp.int32),
                pltpu.VMEM(pressure.shape, F32),
                pltpu.VMEM((pressure.size // pressure.shape[2], LANES), F32),
                pltpu.VMEM((cell_rows, LANES), F32),
                pltpu.VMEM((12, cell_rows, LANES), F32),
                pltpu.VMEM((4, 7 * side_rows, LANES), F32),
                pltpu.VMEM((7 * side_rows, LANES), F32),
                pltpu.VMEM((SWEEPS - 1, 4, 3 * side_rows, LANES), F32),
                pltpu.VMEM((SWEEPS, 4, 3 * side_rows, LANES), F32),
                pltpu.VMEM((SWEEPS - 1, 8, 2, 3 * side_rows, LANES), F32),
                pltpu.VMEM((SWEEPS - 1, 3 * side_rows, LANES), F32),
                pltpu.VMEM((SWEEPS, 5, 3 * side_rows, LANES), F32),
                pltpu.VMEM((cell_rows, LANES), F32),
                pltpu.VMEM((12 * cell_rows, LANES), F32),
                pltpu.VMEM((own_rows * 3, LANES), F32),
                pltpu.VMEM((3 * own_rows, LANES), F32),
                pltpu.VMEM((tiles * STAGE, LANES), F32),
                pltpu.VMEM((tiles * 3, LANES), jnp.int32),
                pltpu.VMEM((2 * tiles, LANES), jnp.int32),
                pltpu.VMEM((2 * tiles, LANES), jnp.int32),
                pltpu.VMEM((2 * tiles, LANES), F32),
                pltpu.VMEM((tiles, LANES, LANES), BF16),
                pltpu.VMEM((3 * (2 * own_rows + 8), LANES), F32),
                pltpu.VMEM((3 * gpad, LANES), F32),
                pltpu.VMEM((64 * PITCH, LANES), F32),
                pltpu.VMEM((2 * (own_rows + 2) * OWN_PITCH, LANES), F32),
                pltpu.VMEM((2 * (4 * side_rows + 1) * GHOST_PITCH, LANES), F32),
                pltpu.VMEM((LANES, side_rows * LANES), BF16),
                pltpu.VMEM((own_rows, side_rows * LANES), BF16),
                pltpu.VMEM((3 * own_rows, LANES), F32),
                pltpu.VMEM((3, tiles, LANES), F32),
                pltpu.VMEM((4, side_rows, side_rows * LANES, LANES), BF16),
                pltpu.VMEM((4, 16 * side_rows, LANES), F32),
                pltpu.VMEM((4, 9 * side_rows, LANES), F32),
                pltpu.SemaphoreType.DMA((rounds, 4)),
                pltpu.SemaphoreType.DMA((rounds, 4)),
                pltpu.SemaphoreType.DMA((12,)),
                pltpu.SemaphoreType.DMA((12,)),
                pltpu.SemaphoreType.DMA((SWEEPS - 1, 8)),
                pltpu.SemaphoreType.DMA((SWEEPS - 1, 8)),
                pltpu.SemaphoreType.DMA((12,)),
            ],
            compiler_params=pltpu.CompilerParams(
                collective_id=0, has_side_effects=True, vmem_limit_bytes=60 * 1024 * 1024
            ),
        )(
            velocity,
            inv_mass.reshape(own_rows, LANES),
            drag.reshape(own_rows, LANES),
            grain_cell.reshape(own_rows, LANES),
            boundary_list.reshape(side_rows, LANES),
            contact_pair,
            frames,
            blocks,
            impulse_start,
            gap,
            contact_mask.reshape(tiles, LANES),
            pressure,
        )
        return pl.pallas_call(
            hand_on,
            out_shape=(
                jax.ShapeDtypeStruct(velocity.shape, F32),
                jax.ShapeDtypeStruct(impulse_start.shape, F32),
            ),
            in_specs=[pl.BlockSpec(memory_space=pl.ANY)] * 2,
            out_specs=(pl.BlockSpec(memory_space=pltpu.HBM),) * 2,
            scratch_shapes=[pltpu.SemaphoreType.DMA((2,))],
        )(
            pltpu.with_memory_space_constraint(out_vel, pltpu.VMEM),
            pltpu.with_memory_space_constraint(out_imp, pltpu.VMEM),
        )

    grains, lists = P(("gx", "gy")), P(None, ("gx", "gy"))
    return jax.shard_map(
        local,
        mesh=mesh,
        in_specs=(
            lists, grains, grains, grains, grains, lists, lists, lists, lists, lists, grains,
            P(None, "gx", "gy"),
        ),
        out_specs=(lists, lists),
        check_vma=False,
    )
```
